32 devices in a mesh: dp: 16 (over z, x, core), ctx: 2 (over y).
Axes of the slice: x: 2, y: 2, z: 4, core: 2. Of those that a mesh axis runs over, the one named last changes fastest.
Arguments:
- x_tokens: bfloat16 [32, 1568, 768], P('dp', 'ctx'), may hold values from -6 to 6
- out_grad: bfloat16 [32, 1568, 768], P('dp', 'ctx'), may hold values from -6 to 6
- w_qkv: float32 [768, 2304], P('ctx'), may hold values from -0.3125 to 0.3125
- w_out: float32 [768, 768], P('ctx'), may hold values from -0.75 to 0.75
- w_up: float32 [768, 3072], P('ctx'), may hold values from -0.21875 to 0.21875
- w_down: float32 [3072, 768], P('ctx'), may hold values from -0.109375 to 0.109375
- vectors: float32 [12, 768], P(None, 'ctx'), may hold values from -0.5 to 1.5
- qkv_mean: float32 [768, 2304], P('ctx'), may hold values from -896 to 896
- qkv_square: float32 [768, 2304], P('ctx'), may hold values from 12293.12 to 196689.92
- out_mean: float32 [768, 768], P('ctx'), may hold values from -384 to 384
- out_square: float32 [768, 768], P('ctx'), may hold values from 2257.92 to 36126.72
- up_mean: float32 [768, 3072], P('ctx'), may hold values from -448 to 448
- up_square: float32 [768, 3072], P('ctx'), may hold values from 3073.28 to 49172.48
- down_mean: float32 [3072, 768], P('ctx'), may hold values from -768 to 768
- down_square: float32 [3072, 768], P('ctx'), may hold values from 9031.68 to 144506.88
- vectors_mean: float32 [12, 768], P(None, 'ctx'), may hold values from -640 to 640
- vectors_square: float32 [12, 768], P(None, 'ctx'), may hold values from 1568 to 100352
Outputs:
- y_tokens: bfloat16 [32, 1568, 768], P('dp', 'ctx')
- x_grad: bfloat16 [32, 1568, 768], P('dp', 'ctx')
- qkv_moment: float32 [768, 2304], P('ctx')
- qkv_second: float32 [768, 2304], P('ctx')
- qkv_master: float32 [768, 2304], P('ctx')
- out_moment: float32 [768, 768], P('ctx')
- out_second: float32 [768, 768], P('ctx')
- out_master: float32 [768, 768], P('ctx')
- up_moment: float32 [768, 3072], P('ctx')
- up_second: float32 [768, 3072], P('ctx')
- up_master: float32 [768, 3072], P('ctx')
- down_moment: float32 [3072, 768], P('ctx')
- down_second: float32 [3072, 768], P('ctx')
- down_master: float32 [3072, 768], P('ctx')
- vectors_moment: float32 [12, 768], P(None, 'ctx')
- vectors_second: float32 [12, 768], P(None, 'ctx')
- vectors_master: float32 [12, 768], P(None, 'ctx')
The draws below stay inside these ranges and needn't reach their ends.
All inputs are finite; a program needn't handle non-finite values.
Results may differ from the reference program's by a relative error of at most 0.02.
Values may be sent and summed in bfloat16 or wider, within the bound.
A program may use at most 640 MiB of HBM per device.

```python
import math
import jax
import jax.numpy as jnp
from jax import lax

D = 768
FF = 3072
HD = 64
SEQ = 1568
STEP = 10
CLIPS = 32
VEC_ROWS = 12


def draw_vectors(key, part):
    key = jax.random.fold_in(key, 7)
    row_total = 8 + FF // D
    gain_key = jax.random.fold_in(key, 1)
    shifts = jnp.clip(0.1 * jax.random.normal(key, (row_total, D), jnp.float32), -0.5, 0.5)
    gains = 1.0 + jax.random.uniform(gain_key, (row_total, D), jnp.float32, -0.3, 0.3)
    row_index = jnp.arange(row_total)[:, None]
    is_gain = (row_index == 0) | (row_index == 5)
    return jnp.where(is_gain, gains, shifts)


def block_scale(stream_key, extent, split, smallest, largest):
    factor_of = 1.0
    for position, parts in split:
        steps = jax.random.uniform(jax.random.fold_in(jax.random.fold_in(stream_key, 6), position), (parts,), jnp.float32, smallest / len(split), largest / len(split))
        factor_of = factor_of * jnp.repeat(jnp.exp(steps), extent[position] // parts).reshape((-1,) + (1,) * (len(extent) - 1 - position))
    return factor_of


def normal_values(key, dims, spread, most, shards=(), held_as=jnp.bfloat16):
    entries = jax.random.normal(key, dims, jnp.float32) * spread
    if len(shards) > 0:
        entries = block_scale(key, dims, shards, -0.22, 0.18) * entries
    return jnp.clip(entries, min=-most, max=most).astype(held_as)


def setup_inputs(seed: int = 0) -> dict:
    arg_keys = jax.random.split(jax.random.key(seed), 18)
    x_tokens = normal_values(arg_keys[0], (CLIPS, SEQ, D), 1.0, 6.0, ((0, 16), (1, 2)))
    out_grad = normal_values(arg_keys[1], (CLIPS, SEQ, D), 1.0, 6.0, ((0, 16), (1, 2)))
    w_qkv = normal_values(arg_keys[2], (D, 3 * D), (D // 2) ** -0.5, 0.3125, ((0, 2),), jnp.float32)
    w_out = normal_values(arg_keys[3], (D, D), HD ** -0.5, 0.75, ((0, 2),), jnp.float32)
    w_up = normal_values(arg_keys[4], (D, FF), D ** -0.5, 0.21875, ((0, 2),), jnp.float32)
    w_down = normal_values(arg_keys[5], (FF, D), FF ** -0.5, 0.109375, ((0, 2),), jnp.float32)
    vectors = draw_vectors(jax.random.fold_in(arg_keys[17], 71), 0)
    qkv_mean = normal_values(arg_keys[7], (D, 3 * D), (0.7 * (CLIPS * SEQ) ** 0.5), 896.0, ((0, 2),), jnp.float32)
    qkv_square = jnp.clip(jnp.exp(math.log(196689.92) - 2.7725887 * jax.random.uniform(arg_keys[8], (D, 3 * D), jnp.float32) ** block_scale(arg_keys[8], (D, 3 * D), ((0, 2),), -0.2, 0.2)), 12293.12, 196689.92)
    out_mean = normal_values(arg_keys[9], (D, D), (0.3 * (CLIPS * SEQ) ** 0.5), 384.0, ((0, 2),), jnp.float32)
    out_square = jnp.clip(jnp.exp(math.log(36126.72) - 2.7725887 * jax.random.uniform(arg_keys[10], (D, D), jnp.float32) ** block_scale(arg_keys[10], (D, D), ((0, 2),), -0.2, 0.2)), 2257.92, 36126.72)
    up_mean = normal_values(arg_keys[11], (D, FF), (0.35 * (CLIPS * SEQ) ** 0.5), 448.0, ((0, 2),), jnp.float32)
    up_square = jnp.clip(jnp.exp(math.log(49172.48) - 2.7725887 * jax.random.uniform(arg_keys[12], (D, FF), jnp.float32) ** block_scale(arg_keys[12], (D, FF), ((0, 2),), -0.2, 0.2)), 3073.28, 49172.48)
    down_mean = normal_values(arg_keys[13], (FF, D), (0.6 * (CLIPS * SEQ) ** 0.5), 768.0, ((0, 2),), jnp.float32)
    down_square = jnp.clip(jnp.exp(math.log(144506.88) - 2.7725887 * jax.random.uniform(arg_keys[14], (FF, D), jnp.float32) ** block_scale(arg_keys[14], (FF, D), ((0, 2),), -0.2, 0.2)), 9031.68, 144506.88)
    vectors_mean = normal_values(arg_keys[15], (VEC_ROWS, D), (0.5 * (CLIPS * SEQ) ** 0.5), 640.0, ((1, 2),), jnp.float32)
    vectors_square = jnp.clip(jnp.exp(math.log(100352.0) - 4.158883 * jax.random.uniform(arg_keys[16], (VEC_ROWS, D), jnp.float32) ** block_scale(arg_keys[16], (VEC_ROWS, D), ((1, 2),), -0.2, 0.2)), 1568.0, 100352.0)
    return dict(x_tokens=x_tokens, out_grad=out_grad, w_qkv=w_qkv, w_out=w_out, w_up=w_up, w_down=w_down, vectors=vectors, qkv_mean=qkv_mean, qkv_square=qkv_square, out_mean=out_mean, out_square=out_square, up_mean=up_mean, up_square=up_square, down_mean=down_mean, down_square=down_square, vectors_mean=vectors_mean, vectors_square=vectors_square)


@jax.custom_vjp
def low(v):
    return lax.optimization_barrier(v.astype(jnp.bfloat16)).astype(jnp.float32)

@jax.custom_vjp
def low_back(v):
    return v

def low_keep(v):
    return (low(v), None)

def low_pass(kept, grad):
    return (grad,)

def back_keep(v):
    return (v, None)

def back_low(kept, grad):
    return (low(grad),)
low.defvjp(low_keep, low_pass)
low_back.defvjp(back_keep, back_low)
norm_epsilon = 1e-06
adam_epsilon = 1e-08
matrix_rate = 0.04
matrix_decay = 0.05
vector_rate = 0.2

def product(first_side, second_side):
    return jnp.dot(first_side, second_side, precision=lax.Precision.HIGHEST)

def normalize(values, norm_gain, norm_shift):
    row_mean = lax.optimization_barrier(jnp.mean(values, axis=-1, keepdims=True))
    centred = values - row_mean
    row_var = lax.optimization_barrier(jnp.mean(centred * centred, axis=-1, keepdims=True))
    return centred * lax.rsqrt(row_var + norm_epsilon) * norm_gain + norm_shift

def clip_layer(tokens, w_qkv, w_out, w_up, w_down, vectors):
    qkv_low = low(w_qkv)
    out_low = low(w_out)
    up_low = low(w_up)
    down_low = low(w_down)
    vector_rows = low(vectors)
    model_width = w_qkv.shape[0]
    head_count = model_width // HD
    seq_count = tokens.shape[0]
    norm_one = low(normalize(tokens, vector_rows[0], vector_rows[1]))
    qkv_shift = jnp.concatenate([vector_rows[2], jnp.zeros_like(vector_rows[2]), vector_rows[3]])
    projected = low(low_back(product(norm_one, qkv_low) + qkv_shift))
    query_rows = projected[:, :model_width].reshape(seq_count, head_count, HD)
    key_rows = projected[:, model_width:2 * model_width].reshape(seq_count, head_count, HD)
    value_rows = projected[:, 2 * model_width:].reshape(seq_count, head_count, HD)
    scores = jnp.einsum('qhd,khd->hqk', query_rows, key_rows, precision=lax.Precision.HIGHEST) * 0.125
    scores = low_back(scores)
    peak_score = lax.optimization_barrier(jnp.max(scores, axis=-1, keepdims=True))
    exponent = jnp.exp(scores - peak_score)
    probs_low = low(exponent / lax.optimization_barrier(jnp.sum(exponent, axis=-1, keepdims=True)))
    attended = jnp.einsum('hqk,khd->qhd', probs_low, value_rows, precision=lax.Precision.HIGHEST)
    attended = low(low_back(attended.reshape(seq_count, model_width)))
    branch = low_back(product(attended, out_low) + vector_rows[4])
    resid = tokens + branch
    norm_two = low(normalize(resid, vector_rows[5], vector_rows[6]))
    pre_act = low_back(product(norm_two, up_low) + vector_rows[8:].reshape(-1))
    act_low = low(jax.nn.gelu(pre_act, approximate=False))
    mlp_out = low_back(product(act_low, down_low) + vector_rows[7])
    return resid + mlp_out

def adam_update(weight, gradient, first_old, second_old, step_rate, decay_rate):
    first_new = 0.5 * first_old + 0.5 * gradient
    second_new = 0.5 * second_old + 0.5 * gradient * gradient
    correction = 1.0 - 0.5 ** STEP
    update = first_new / correction / (jnp.sqrt(second_new / correction) + adam_epsilon) + decay_rate * weight
    return (first_new, second_new, weight - step_rate * update)

def reference(x_tokens, out_grad, w_qkv, w_out, w_up, w_down, vectors, qkv_mean, qkv_square, out_mean, out_square, up_mean, up_square, down_mean, down_square, vectors_mean, vectors_square):
    parameters = (w_qkv, w_out, w_up, w_down, vectors)

    def per_clip(running, clip_pair):
        tokens, cotangent = clip_pair
        output, pullback = jax.vjp(clip_layer, tokens.astype(jnp.float32), *parameters)
        gradients = pullback(cotangent.astype(jnp.float32))
        running = tuple((earlier + added for earlier, added in zip(running, gradients[1:])))
        return (running, (output.astype(jnp.bfloat16), gradients[0].astype(jnp.bfloat16)))
    starting = tuple((jnp.zeros_like(member) for member in parameters))
    summed, (y_tokens, x_grad) = lax.scan(per_clip, starting, (x_tokens, out_grad))
    qkv_moment, qkv_second, qkv_master = adam_update(w_qkv, summed[0], qkv_mean, qkv_square, matrix_rate, matrix_decay)
    out_moment, out_second, out_master = adam_update(w_out, summed[1], out_mean, out_square, matrix_rate, matrix_decay)
    up_moment, up_second, up_master = adam_update(w_up, summed[2], up_mean, up_square, matrix_rate, matrix_decay)
    down_moment, down_second, down_master = adam_update(w_down, summed[3], down_mean, down_square, matrix_rate, matrix_decay)
    vectors_moment, vectors_second, vectors_master = adam_update(vectors, summed[4], vectors_mean, vectors_square, vector_rate, 0.0)
    return (y_tokens, x_grad, qkv_moment, qkv_second, qkv_master, out_moment, out_second, out_master, up_moment, up_second, up_master, down_moment, down_second, down_master, vectors_moment, vectors_second, vectors_master)
```

```python
import functools

import jax
import jax.numpy as jnp
from jax import lax
from jax.experimental import pallas as pl
from jax.experimental.pallas import tpu as pltpu
from jax.sharding import PartitionSpec as P

HD = 64
STEP = 10


norm_epsilon = 1e-06
adam_epsilon = 1e-08
matrix_rate = 0.04
matrix_decay = 0.05
vector_rate = 0.2


def normalize(values, norm_gain, norm_shift):
    row_mean = jnp.mean(values, axis=-1, keepdims=True)
    centred = values - row_mean
    row_var = jnp.mean(centred * centred, axis=-1, keepdims=True)
    inverse = lax.rsqrt(row_var + norm_epsilon)
    normed = centred * inverse
    return (normed * norm_gain + norm_shift, normed, inverse)


def norm_back(upstream, norm_gain, normed, inverse):
    scaled = upstream * norm_gain
    first_mean = jnp.mean(scaled, axis=-1, keepdims=True)
    second_mean = jnp.mean(scaled * normed, axis=-1, keepdims=True)
    return inverse * (scaled - first_mean - normed * second_mean)


def normal_cdf(values):
    return 0.5 * (1.0 + lax.erf(values * 0.7071067811865476))


def attend(operands):
    query_block, key_block, value_block = operands
    scores = (
        jnp.einsum("qhd,khd->hqk", query_block, key_block, preferred_element_type=jnp.float32)
        * 0.125
    )
    peak_score = jnp.max(scores, axis=-1, keepdims=True)
    exponent = jnp.exp(scores - peak_score)
    totals = jnp.sum(exponent, axis=-1, keepdims=True)
    probs_low = (exponent / totals).astype(jnp.bfloat16)
    attended = jnp.einsum(
        "hqk,khd->qhd", probs_low, value_block, preferred_element_type=jnp.float32
    )
    return (attended, peak_score + jnp.log(totals))


def attend_back(operands):
    query_block, key_block, value_block, log_total, grad_block = operands
    scores = (
        jnp.einsum("qhd,khd->hqk", query_block, key_block, preferred_element_type=jnp.float32)
        * 0.125
    )
    probs = jnp.exp(scores - log_total)
    grad_probs = jnp.einsum(
        "qhd,khd->hqk", grad_block, value_block, preferred_element_type=jnp.float32
    )
    delta = jnp.sum(probs * grad_probs, axis=-1, keepdims=True)
    grad_scores = (probs * (grad_probs - delta)).astype(jnp.bfloat16)
    grad_query = (
        jnp.einsum("hqk,khd->qhd", grad_scores, key_block, preferred_element_type=jnp.float32)
        * 0.125
    )
    grad_key = (
        jnp.einsum("hqk,qhd->khd", grad_scores, query_block, preferred_element_type=jnp.float32)
        * 0.125
    )
    grad_value = jnp.einsum(
        "hqk,qhd->khd", probs.astype(jnp.bfloat16), grad_block, preferred_element_type=jnp.float32
    )
    return (grad_query, grad_key, grad_value)


def adam_update(weight, gradient, first_old, second_old, step_rate, decay_rate):
    first_new = 0.5 * first_old + 0.5 * gradient
    second_new = 0.5 * second_old + 0.5 * gradient * gradient
    correction = 1.0 - 0.5**STEP
    update = (
        first_new / correction / (jnp.sqrt(second_new / correction) + adam_epsilon)
        + decay_rate * weight
    )
    return (first_new, second_new, weight - step_rate * update)


def per_device_split(
    x_tokens,
    out_grad,
    w_qkv,
    w_out,
    w_up,
    w_down,
    vectors,
    qkv_mean,
    qkv_square,
    out_mean,
    out_square,
    up_mean,
    up_square,
    down_mean,
    down_square,
    vectors_mean,
    vectors_square,
):
    masters = (w_qkv, w_out, w_up, w_down, vectors)
    lowered = tuple((member.astype(jnp.bfloat16) for member in masters))
    qkv_low, out_low, up_low, down_low, vector_low = (
        lax.all_gather(lowered[0], "ctx", axis=0, tiled=True),
        lax.all_gather(lowered[1], "ctx", axis=0, tiled=True),
        lax.all_gather(lowered[2], "ctx", axis=0, tiled=True),
        lax.all_gather(lowered[3], "ctx", axis=0, tiled=True),
        lax.all_gather(lowered[4], "ctx", axis=1, tiled=True),
    )
    vector_rows = vector_low.astype(jnp.float32)
    clip_count, row_count, model_width = x_tokens.shape
    head_count = model_width // HD
    token_total = clip_count * row_count
    flat_rows = x_tokens.reshape(token_total, model_width).astype(jnp.float32)
    norm_one, normed_one, inverse_one = normalize(flat_rows, vector_rows[0], vector_rows[1])
    norm_one_low = norm_one.astype(jnp.bfloat16)
    qkv_shift = jnp.concatenate([vector_rows[2], jnp.zeros_like(vector_rows[2]), vector_rows[3]])
    projected = (
        jnp.dot(norm_one_low, qkv_low, preferred_element_type=jnp.float32) + qkv_shift
    ).astype(jnp.bfloat16)
    query_rows = projected[:, :model_width].reshape(clip_count, row_count, head_count, HD)
    key_local = projected[:, model_width : 2 * model_width].reshape(
        clip_count, row_count, head_count, HD
    )
    value_local = projected[:, 2 * model_width :].reshape(clip_count, row_count, head_count, HD)
    key_rows, value_rows = (
        lax.all_gather(key_local, "ctx", axis=1, tiled=True),
        lax.all_gather(value_local, "ctx", axis=1, tiled=True),
    )
    attended, log_total = lax.map(attend, (query_rows, key_rows, value_rows))
    attended_low = attended.reshape(token_total, model_width).astype(jnp.bfloat16)
    branch = jnp.dot(attended_low, out_low, preferred_element_type=jnp.float32) + vector_rows[4]
    resid = flat_rows + branch
    norm_two, normed_two, inverse_two = normalize(resid, vector_rows[5], vector_rows[6])
    norm_two_low = norm_two.astype(jnp.bfloat16)
    pre_act = jnp.dot(norm_two_low, up_low, preferred_element_type=jnp.float32) + vector_rows[
        8:
    ].reshape(-1)
    act_low = (pre_act * normal_cdf(pre_act)).astype(jnp.bfloat16)
    mlp_out = jnp.dot(act_low, down_low, preferred_element_type=jnp.float32) + vector_rows[7]
    y_tokens = (resid + mlp_out).astype(jnp.bfloat16).reshape(clip_count, row_count, model_width)
    grad_output = out_grad.reshape(token_total, model_width)
    grad_float = grad_output.astype(jnp.float32)
    grad_down = jnp.einsum("tf,td->fd", act_low, grad_output, preferred_element_type=jnp.float32)
    down_shift = jnp.sum(grad_float, axis=0)
    grad_act = jnp.dot(grad_output, down_low.T, preferred_element_type=jnp.float32)
    density = jnp.exp(-0.5 * pre_act * pre_act) * 0.3989422804014327
    grad_pre = (grad_act * (normal_cdf(pre_act) + pre_act * density)).astype(jnp.bfloat16)
    grad_up = jnp.einsum("td,tf->df", norm_two_low, grad_pre, preferred_element_type=jnp.float32)
    up_shift = jnp.sum(grad_pre.astype(jnp.float32), axis=0)
    grad_norm_two = jnp.dot(grad_pre, up_low.T, preferred_element_type=jnp.float32)
    gain_two_grad = jnp.sum(grad_norm_two * normed_two, axis=0)
    shift_two_grad = jnp.sum(grad_norm_two, axis=0)
    grad_resid = grad_float + norm_back(grad_norm_two, vector_rows[5], normed_two, inverse_two)
    grad_branch = grad_resid.astype(jnp.bfloat16)
    grad_out = jnp.einsum(
        "td,te->de", attended_low, grad_branch, preferred_element_type=jnp.float32
    )
    out_shift = jnp.sum(grad_branch.astype(jnp.float32), axis=0)
    grad_attended = jnp.dot(grad_branch, out_low.T, preferred_element_type=jnp.float32).astype(
        jnp.bfloat16
    )
    grad_attended = grad_attended.reshape(clip_count, row_count, head_count, HD)
    grad_query, key_terms, value_terms = lax.map(
        attend_back, (query_rows, key_rows, value_rows, log_total, grad_attended)
    )
    grad_key, grad_value = (
        lax.psum_scatter(
            key_terms.astype(jnp.bfloat16), "ctx", scatter_dimension=1, tiled=True
        ).astype(jnp.float32),
        lax.psum_scatter(
            value_terms.astype(jnp.bfloat16), "ctx", scatter_dimension=1, tiled=True
        ).astype(jnp.float32),
    )
    grad_projected = jnp.concatenate(
        [
            grad_query.reshape(token_total, model_width),
            grad_key.reshape(token_total, model_width),
            grad_value.reshape(token_total, model_width),
        ],
        axis=1,
    ).astype(jnp.bfloat16)
    grad_qkv = jnp.einsum(
        "td,te->de", norm_one_low, grad_projected, preferred_element_type=jnp.float32
    )
    projected_sums = jnp.sum(grad_projected.astype(jnp.float32), axis=0)
    grad_norm_one = jnp.dot(grad_projected, qkv_low.T, preferred_element_type=jnp.float32)
    gain_one_grad = jnp.sum(grad_norm_one * normed_one, axis=0)
    shift_one_grad = jnp.sum(grad_norm_one, axis=0)
    x_grad = (
        grad_resid + norm_back(grad_norm_one, vector_rows[0], normed_one, inverse_one)
    ).astype(jnp.bfloat16)
    x_grad = x_grad.reshape(clip_count, row_count, model_width)
    first_rows = jnp.stack(
        [
            gain_one_grad,
            shift_one_grad,
            projected_sums[:model_width],
            projected_sums[2 * model_width :],
            out_shift,
            gain_two_grad,
            shift_two_grad,
            down_shift,
        ]
    )
    grad_vectors = jnp.concatenate([first_rows, up_shift.reshape(-1, model_width)], axis=0)
    group_size = lax.axis_size("ctx")
    vector_count = grad_vectors.shape[0]
    flat_vectors = (
        grad_vectors.reshape(vector_count, group_size, -1)
        .transpose(1, 0, 2)
        .reshape(group_size, -1)
    )
    shaped = (grad_qkv, grad_out, grad_up, grad_down, flat_vectors)
    spread = (
        lax.psum_scatter(
            shaped[0].astype(jnp.bfloat16), "dp", scatter_dimension=1, tiled=True
        ).astype(jnp.float32),
        lax.psum_scatter(
            shaped[1].astype(jnp.bfloat16), "dp", scatter_dimension=1, tiled=True
        ).astype(jnp.float32),
        lax.psum_scatter(
            shaped[2].astype(jnp.bfloat16), "dp", scatter_dimension=1, tiled=True
        ).astype(jnp.float32),
        lax.psum_scatter(
            shaped[3].astype(jnp.bfloat16), "dp", scatter_dimension=1, tiled=True
        ).astype(jnp.float32),
        lax.psum_scatter(
            shaped[4].astype(jnp.bfloat16), "dp", scatter_dimension=1, tiled=True
        ).astype(jnp.float32),
    )
    owned = (
        lax.psum_scatter(
            spread[0].astype(jnp.bfloat16), "ctx", scatter_dimension=0, tiled=True
        ).astype(jnp.float32),
        lax.psum_scatter(
            spread[1].astype(jnp.bfloat16), "ctx", scatter_dimension=0, tiled=True
        ).astype(jnp.float32),
        lax.psum_scatter(
            spread[2].astype(jnp.bfloat16), "ctx", scatter_dimension=0, tiled=True
        ).astype(jnp.float32),
        lax.psum_scatter(
            spread[3].astype(jnp.bfloat16), "ctx", scatter_dimension=0, tiled=True
        ).astype(jnp.float32),
        lax.psum_scatter(
            spread[4].astype(jnp.bfloat16), "ctx", scatter_dimension=0, tiled=True
        ).astype(jnp.float32),
    )
    collected = (
        lax.all_gather(owned[0].astype(jnp.bfloat16), "dp", axis=1, tiled=True).astype(jnp.float32),
        lax.all_gather(owned[1].astype(jnp.bfloat16), "dp", axis=1, tiled=True).astype(jnp.float32),
        lax.all_gather(owned[2].astype(jnp.bfloat16), "dp", axis=1, tiled=True).astype(jnp.float32),
        lax.all_gather(owned[3].astype(jnp.bfloat16), "dp", axis=1, tiled=True).astype(jnp.float32),
        lax.all_gather(owned[4].astype(jnp.bfloat16), "dp", axis=1, tiled=True).astype(jnp.float32),
    )
    shares = (
        collected[0],
        collected[1],
        collected[2],
        collected[3],
        collected[4].reshape(vector_count, -1),
    )
    qkv_moment, qkv_second, qkv_master = adam_update(
        w_qkv, shares[0], qkv_mean, qkv_square, matrix_rate, matrix_decay
    )
    out_moment, out_second, out_master = adam_update(
        w_out, shares[1], out_mean, out_square, matrix_rate, matrix_decay
    )
    up_moment, up_second, up_master = adam_update(
        w_up, shares[2], up_mean, up_square, matrix_rate, matrix_decay
    )
    down_moment, down_second, down_master = adam_update(
        w_down, shares[3], down_mean, down_square, matrix_rate, matrix_decay
    )
    vectors_moment, vectors_second, vectors_master = adam_update(
        vectors, shares[4], vectors_mean, vectors_square, vector_rate, 0.0
    )
    return (
        y_tokens,
        x_grad,
        qkv_moment,
        qkv_second,
        qkv_master,
        out_moment,
        out_second,
        out_master,
        up_moment,
        up_second,
        up_master,
        down_moment,
        down_second,
        down_master,
        vectors_moment,
        vectors_second,
        vectors_master,
    )


LOG2E = 1.4426950408889634
NT = (((1,), (1,)), ((), ()))
NN = (((1,), (0,)), ((), ()))
TN = (((0,), (0,)), ((), ()))
KERNEL_VMEM = 62 * 2**20


def attend_kernel(q_ref, k_ref, v_ref, o_ref, r_ref, p_ref, score_a, score_b):
    rows = score_a.shape[0]
    total = k_ref.shape[0]
    lane = lax.broadcasted_iota(jnp.int32, (1, 2 * HD), 1)
    held = (score_a, score_b)
    parts = total // rows
    items = [(head, part) for head in range(2) for part in range(parts)]

    def score(index):
        head, part = items[index]
        keys = jnp.where((lane // HD) == head, k_ref[...], 0).astype(jnp.bfloat16)
        held[index % 2][...] = lax.dot_general(
            q_ref[part * rows : (part + 1) * rows, :], keys, NT, preferred_element_type=jnp.float32
        )

    def soften(index):
        head, part = items[index]
        values = held[index % 2][...]
        peak = jnp.max(values, axis=1, keepdims=True)
        p_ref[head, part * rows : (part + 1) * rows, :] = jnp.exp2(
            (values - peak) * (0.125 * LOG2E)
        ).astype(jnp.bfloat16)

    def weigh(index):
        head, part = items[index]
        span = slice(part * rows, (part + 1) * rows)
        kept = jnp.where((lane // HD) == head, v_ref[...], 0).astype(jnp.bfloat16)
        table = jnp.concatenate([kept, jnp.ones((total, 2 * HD), jnp.bfloat16)], axis=1)
        out = lax.dot_general(p_ref[head, span, :], table, NN, preferred_element_type=jnp.float32)
        inverse = 1.0 / out[:, 2 * HD :]
        mixed = (out[:, : 2 * HD] * inverse).astype(jnp.bfloat16)
        if head == 0:
            o_ref[span, :] = mixed
            r_ref[span, :] = inverse
        else:
            o_ref[span, :] = jnp.where(lane < HD, o_ref[span, :], mixed)
            r_ref[span, :] = jnp.where(lane < HD, r_ref[span, :], inverse)

    score(0)
    for index in range(len(items)):
        if index + 1 < len(items):
            score(index + 1)
        soften(index)
        weigh(index)


def attend_call(projected, width):
    total = projected.shape[0]
    pairs = width // (2 * HD)

    def columns(start):
        return pl.BlockSpec((total, 2 * HD), lambda p: (0, start * pairs + p))

    return pl.pallas_call(
        attend_kernel,
        grid=(pairs,),
        in_specs=[columns(0), columns(1), columns(2)],
        out_specs=[
            columns(0),
            columns(0),
            pl.BlockSpec((2, total, total), lambda p: (p, 0, 0)),
        ],
        out_shape=[
            jax.ShapeDtypeStruct((total, width), jnp.bfloat16),
            jax.ShapeDtypeStruct((total, width), jnp.float32),
            jax.ShapeDtypeStruct((2 * pairs, total, total), jnp.bfloat16),
        ],
        scratch_shapes=[pltpu.VMEM((total // 2, total), jnp.float32)] * 2,
        compiler_params=pltpu.CompilerParams(vmem_limit_bytes=KERNEL_VMEM),
        cost_estimate=pl.CostEstimate(
            flops=16 * pairs * total * total * 2 * HD,
            bytes_accessed=4 * pairs * total * total,
            transcendentals=2 * pairs * total * total,
        ),
        name="attend",
    )(projected, projected, projected)


def attend_back_kernel(
    q_ref, k_ref, v_ref, g_ref, o_ref, r_ref, p_ref, dq_ref, dk_ref, dv_ref, ds, qt, gt, dkt, dvt
):
    head = pl.program_id(1)
    total = k_ref.shape[0]
    half = total // 2
    lane = lax.broadcasted_iota(jnp.int32, (1, 2 * HD), 1)
    keep = (lane // HD) == head
    scaled = g_ref[...].astype(jnp.float32) * r_ref[...]

    @pl.when(head == 0)
    def _():
        qt[...] = q_ref[...].T
        gt[...] = scaled.astype(jnp.bfloat16).T

    delta = jnp.sum(jnp.where(keep, scaled * o_ref[...].astype(jnp.float32), 0.0), axis=1, keepdims=True)
    values = jnp.where(keep, v_ref[...], 0).astype(jnp.bfloat16)
    grad_probs = lax.dot_general(
        scaled.astype(jnp.bfloat16), values, NT, preferred_element_type=jnp.float32
    )
    ds[...] = (p_ref[...].astype(jnp.float32) * (grad_probs - delta)).astype(jnp.bfloat16)
    span = pl.ds(pl.multiple_of(head * HD, HD), HD)
    dvt[span, :] = lax.dot_general(gt[span, :], p_ref[...], NN, preferred_element_type=jnp.float32)
    dkt[span, :] = 0.125 * lax.dot_general(
        qt[span, :], ds[...], NN, preferred_element_type=jnp.float32
    )
    keys = jnp.where(keep, k_ref[...], 0).astype(jnp.bfloat16)
    for part in range(2):
        rows = slice(part * half, (part + 1) * half)
        term = 0.125 * lax.dot_general(ds[rows, :], keys, NN, preferred_element_type=jnp.float32)
        dq_ref[rows, :] = jnp.where(keep, term.astype(jnp.bfloat16), dq_ref[rows, :])

    @pl.when(head == 1)
    def _():
        dk_ref[...] = dkt[...].T.astype(jnp.bfloat16)
        dv_ref[...] = dvt[...].T.astype(jnp.bfloat16)


def attend_back_call(projected, upstream, attended, inverse, exponent):
    total, width = attended.shape
    pairs = width // (2 * HD)

    def columns(start):
        return pl.BlockSpec((total, 2 * HD), lambda p, h: (0, start * pairs + p))

    return pl.pallas_call(
        attend_back_kernel,
        grid=(pairs, 2),
        in_specs=[columns(0), columns(1), columns(2), columns(0), columns(0), columns(0)]
        + [pl.BlockSpec((None, total, total), lambda p, h: (p * 2 + h, 0, 0))],
        out_specs=[columns(0)] * 3,
        out_shape=[jax.ShapeDtypeStruct((total, width), jnp.bfloat16)] * 3,
        scratch_shapes=[pltpu.VMEM((total, total), jnp.bfloat16)]
        + [pltpu.VMEM((2 * HD, total), jnp.bfloat16)] * 2
        + [pltpu.VMEM((2 * HD, total), jnp.float32)] * 2,
        compiler_params=pltpu.CompilerParams(vmem_limit_bytes=KERNEL_VMEM),
        cost_estimate=pl.CostEstimate(
            flops=32 * pairs * total * total * 2 * HD,
            bytes_accessed=4 * pairs * total * total,
            transcendentals=0,
        ),
        name="attend_back",
    )(projected, projected, projected, upstream, attended, inverse, exponent)


def swap(values, axis_name, mask):
    count = lax.axis_size(axis_name)
    return lax.ppermute(values, axis_name, [(i, i ^ mask) for i in range(count)])


def own_bits():
    place = lax.axis_index("dp")
    z = place // 4
    return {
        "core": place % 2,
        "x": (place // 2) % 2,
        "a": (z % 2 + z // 2) % 2,
        "b": z // 2,
        "y": lax.axis_index("ctx"),
    }


MASKS = {"core": ("dp", 1), "x": ("dp", 2), "a": ("dp", 4), "b": ("dp", 12), "y": ("ctx", 1)}


def scatter_sum(buffer, names, order, bits):
    names = list(names)
    for name in order:
        at = names.index(name)
        sent = lax.dynamic_index_in_dim(buffer, 1 - bits[name], at, keepdims=False)
        kept = lax.dynamic_index_in_dim(buffer, bits[name], at, keepdims=False)
        got = swap(sent, *MASKS[name])
        buffer = (kept.astype(jnp.float32) + got.astype(jnp.float32)).astype(jnp.bfloat16)
        names.remove(name)
    return buffer


def gather_all(piece, names, order, bits):
    present = []
    for name in order:
        got = swap(piece, *MASKS[name])
        at = sum(1 for other in present if names.index(other) < names.index(name))
        piece = jnp.where(
            bits[name] == 0, jnp.stack([piece, got], axis=at), jnp.stack([got, piece], axis=at)
        )
        present.append(name)
    return piece


RINGS = ("x", "y", "a", "b")


def rotated(names, start):
    start = start % len(names)
    return tuple(names[start:]) + tuple(names[:start])


def sum_streams(streams, names_of, bits):
    results = []
    for index, (buffer, names) in enumerate(zip(streams, names_of)):
        piece = scatter_sum(buffer, names, ("core",) + rotated(RINGS, index), bits)
        left = tuple(name for name in names if name != "y")
        order = rotated(("x", "a", "b"), index) + ("core",)
        results.append(gather_all(piece, left, order, bits))
    return results


def gather_shard(shard, bits):
    low = shard.astype(jnp.bfloat16)
    rows, cols = low.shape
    quarters = low.reshape(4, rows // 4, cols)
    mine = lax.dynamic_index_in_dim(quarters, bits["x"] * 2 + bits["core"], 0, keepdims=False)
    got = swap(mine, *MASKS["y"])
    other = gather_all(got, ("x", "core"), ("x", "core"), bits).reshape(rows, cols)
    return jnp.where(
        bits["y"] == 0,
        jnp.concatenate([low, other], axis=0),
        jnp.concatenate([other, low], axis=0),
    )


def per_device_clips(
    x_tokens,
    out_grad,
    w_qkv,
    w_out,
    w_up,
    w_down,
    vectors,
    qkv_mean,
    qkv_square,
    out_mean,
    out_square,
    up_mean,
    up_square,
    down_mean,
    down_square,
    vectors_mean,
    vectors_square,
):
    bits = own_bits()
    me = bits["y"]

    def trade(halves):
        own = lax.dynamic_index_in_dim(halves, me, 0, keepdims=False)
        sent = lax.dynamic_index_in_dim(halves, 1 - me, 0, keepdims=False)
        return jnp.concatenate([own, swap(sent, *MASKS["y"])], axis=0)

    def trade_back(rows):
        count = rows.shape[0] // 2
        got = swap(rows[count:], *MASKS["y"])
        own = rows[:count]
        return jnp.where(me == 0, jnp.stack([own, got]), jnp.stack([got, own]))

    width = x_tokens.shape[2]
    qkv_low = gather_shard(w_qkv, bits)
    x_low = trade(x_tokens)
    out_low = gather_shard(w_out, bits)
    up_low = gather_shard(w_up, bits)
    down_low = gather_shard(w_down, bits)
    grad_output = trade(out_grad)
    vector_own = vectors.astype(jnp.bfloat16)
    vector_other = swap(vector_own, *MASKS["y"])
    vector_rows = jnp.where(
        me == 0,
        jnp.concatenate([vector_own, vector_other], axis=1),
        jnp.concatenate([vector_other, vector_own], axis=1),
    ).astype(jnp.float32)

    flat_rows = x_low.astype(jnp.float32)
    norm_one, normed_one, inverse_one = normalize(flat_rows, vector_rows[0], vector_rows[1])
    norm_one_low = norm_one.astype(jnp.bfloat16)
    qkv_shift = jnp.concatenate([vector_rows[2], jnp.zeros_like(vector_rows[2]), vector_rows[3]])
    projected = (
        jnp.dot(norm_one_low, qkv_low, preferred_element_type=jnp.float32) + qkv_shift
    ).astype(jnp.bfloat16)
    attended_low, inverse_total, exponent = attend_call(projected, width)
    branch = jnp.dot(attended_low, out_low, preferred_element_type=jnp.float32) + vector_rows[4]
    resid = flat_rows + branch
    norm_two, normed_two, inverse_two = normalize(resid, vector_rows[5], vector_rows[6])
    norm_two_low = norm_two.astype(jnp.bfloat16)
    pre_act = jnp.dot(norm_two_low, up_low, preferred_element_type=jnp.float32) + vector_rows[
        8:
    ].reshape(-1)
    act_low = (pre_act * normal_cdf(pre_act)).astype(jnp.bfloat16)
    mlp_out = jnp.dot(act_low, down_low, preferred_element_type=jnp.float32) + vector_rows[7]
    y_tokens = trade_back((resid + mlp_out).astype(jnp.bfloat16))

    grad_float = grad_output.astype(jnp.float32)
    grad_down = jnp.einsum(
        "tf,td->fd", act_low, grad_output, preferred_element_type=jnp.float32
    ).astype(jnp.bfloat16)
    down_shift = jnp.sum(grad_float, axis=0)
    grad_act = jnp.dot(grad_output, down_low.T, preferred_element_type=jnp.float32)
    density = jnp.exp(-0.5 * pre_act * pre_act) * 0.3989422804014327
    grad_pre = (grad_act * (normal_cdf(pre_act) + pre_act * density)).astype(jnp.bfloat16)
    up_blocks = [
        jnp.einsum(
            "td,tf->df",
            norm_two_low,
            grad_pre[:, i * width : (i + 1) * width],
            preferred_element_type=jnp.float32,
        ).astype(jnp.bfloat16)
        for i in range(4)
    ]
    down_view = grad_down.reshape(2, 2, 2, 2, 2, 2, -1, width)
    up_names = ("core", "y", "x", "a", "b")
    down_names = ("y", "core", "x", "a", "b")
    early = sum_streams(
        [down_view[:, 0], down_view[:, 1]]
        + [
            jnp.stack(up_blocks[2 * i : 2 * i + 2]).reshape(2, 2, 2, 2, 2, -1, width)
            for i in range(2)
        ],
        [down_names, down_names, up_names, up_names],
        bits,
    )
    down_share = jnp.stack(early[:2]).reshape(-1, width).astype(jnp.float32)
    up_share = jnp.concatenate(
        [early[2 + i][j].reshape(-1, width) for i in range(2) for j in range(2)], axis=1
    ).astype(jnp.float32)

    up_shift = jnp.sum(grad_pre.astype(jnp.float32), axis=0)
    grad_norm_two = jnp.dot(grad_pre, up_low.T, preferred_element_type=jnp.float32)
    gain_two_grad = jnp.sum(grad_norm_two * normed_two, axis=0)
    shift_two_grad = jnp.sum(grad_norm_two, axis=0)
    grad_resid = grad_float + norm_back(grad_norm_two, vector_rows[5], normed_two, inverse_two)
    grad_branch = grad_resid.astype(jnp.bfloat16)
    grad_out = jnp.einsum(
        "td,te->de", attended_low, grad_branch, preferred_element_type=jnp.float32
    ).astype(jnp.bfloat16)
    out_shift = jnp.sum(grad_branch.astype(jnp.float32), axis=0)
    grad_attended = jnp.dot(grad_branch, out_low.T, preferred_element_type=jnp.float32).astype(
        jnp.bfloat16
    )
    grad_parts = attend_back_call(projected, grad_attended, attended_low, inverse_total, exponent)
    grad_projected = jnp.concatenate(grad_parts, axis=1)
    grad_qkv = [
        jnp.einsum(
            "td,te->de", norm_one_low, part, preferred_element_type=jnp.float32
        ).astype(jnp.bfloat16)
        for part in grad_parts
    ]
    late_names = ("y", "x", "a", "b", "core")
    late = sum_streams(
        [member.reshape(2, 2, 2, 2, 2, -1, width) for member in grad_qkv + [grad_out]],
        [late_names] * 4,
        bits,
    )
    late = [member.reshape(-1, width).astype(jnp.float32) for member in late]
    qkv_share = jnp.concatenate(late[:3], axis=1)
    out_share = late[3]

    projected_sums = jnp.sum(grad_projected.astype(jnp.float32), axis=0)
    grad_norm_one = jnp.dot(grad_projected, qkv_low.T, preferred_element_type=jnp.float32)
    gain_one_grad = jnp.sum(grad_norm_one * normed_one, axis=0)
    shift_one_grad = jnp.sum(grad_norm_one, axis=0)
    x_grad = trade_back(
        (
            grad_resid + norm_back(grad_norm_one, vector_rows[0], normed_one, inverse_one)
        ).astype(jnp.bfloat16)
    )
    first_rows = jnp.stack(
        [
            gain_one_grad,
            shift_one_grad,
            projected_sums[:width],
            projected_sums[2 * width :],
            out_shift,
            gain_two_grad,
            shift_two_grad,
            down_shift,
        ]
    )
    grad_vectors = jnp.concatenate([first_rows, up_shift.reshape(-1, width)], axis=0)
    summed_vectors = lax.psum(grad_vectors, ("dp", "ctx"))
    vector_share = lax.dynamic_slice_in_dim(summed_vectors, me * (width // 2), width // 2, axis=1)

    qkv_new = adam_update(w_qkv, qkv_share, qkv_mean, qkv_square, matrix_rate, matrix_decay)
    out_new = adam_update(w_out, out_share, out_mean, out_square, matrix_rate, matrix_decay)
    up_new = adam_update(w_up, up_share, up_mean, up_square, matrix_rate, matrix_decay)
    down_new = adam_update(w_down, down_share, down_mean, down_square, matrix_rate, matrix_decay)
    vectors_new = adam_update(
        vectors, vector_share, vectors_mean, vectors_square, vector_rate, 0.0
    )
    return (y_tokens, x_grad) + qkv_new + out_new + up_new + down_new + vectors_new


def per_device(x_tokens, *others):
    clips = x_tokens.shape[0]
    if lax.axis_size("ctx") == 2 and lax.axis_size("dp") == 16 and clips == 2:
        return per_device_clips(x_tokens, *others)
    return per_device_split(x_tokens, *others)


def solution(mesh):
    return jax.shard_map(
        per_device,
        mesh=mesh,
        in_specs=(
            P("dp", "ctx", None),
            P("dp", "ctx", None),
            P("ctx", None),
            P("ctx", None),
            P("ctx", None),
            P("ctx", None),
            P(None, "ctx"),
            P("ctx", None),
            P("ctx", None),
            P("ctx", None),
            P("ctx", None),
            P("ctx", None),
            P("ctx", None),
            P("ctx", None),
            P("ctx", None),
            P(None, "ctx"),
            P(None, "ctx"),
        ),
        out_specs=(
            P("dp", "ctx", None),
            P("dp", "ctx", None),
            P("ctx", None),
            P("ctx", None),
            P("ctx", None),
            P("ctx", None),
            P("ctx", None),
            P("ctx", None),
            P("ctx", None),
            P("ctx", None),
            P("ctx", None),
            P("ctx", None),
            P("ctx", None),
            P("ctx", None),
            P(None, "ctx"),
            P(None, "ctx"),
            P(None, "ctx"),
        ),
        check_vma=False,
    )
```

```python
import functools

import jax
import jax.numpy as jnp
from jax import lax
from jax.experimental import pallas as pl
from jax.experimental.pallas import tpu as pltpu
from jax.sharding import PartitionSpec as P

HD = 64
STEP = 10


norm_epsilon = 1e-06
adam_epsilon = 1e-08
matrix_rate = 0.04
matrix_decay = 0.05
vector_rate = 0.2


def normalize(values, norm_gain, norm_shift):
    row_mean = jnp.mean(values, axis=-1, keepdims=True)
    centred = values - row_mean
    row_var = jnp.mean(centred * centred, axis=-1, keepdims=True)
    inverse = lax.rsqrt(row_var + norm_epsilon)
    normed = centred * inverse
    return (normed * norm_gain + norm_shift, normed, inverse)


def norm_back(upstream, norm_gain, normed, inverse):
    scaled = upstream * norm_gain
    first_mean = jnp.mean(scaled, axis=-1, keepdims=True)
    second_mean = jnp.mean(scaled * normed, axis=-1, keepdims=True)
    return inverse * (scaled - first_mean - normed * second_mean)


def normal_cdf(values):
    return 0.5 * (1.0 + lax.erf(values * 0.7071067811865476))


def attend(operands):
    query_block, key_block, value_block = operands
    scores = (
        jnp.einsum("qhd,khd->hqk", query_block, key_block, preferred_element_type=jnp.float32)
        * 0.125
    )
    peak_score = jnp.max(scores, axis=-1, keepdims=True)
    exponent = jnp.exp(scores - peak_score)
    totals = jnp.sum(exponent, axis=-1, keepdims=True)
    probs_low = (exponent / totals).astype(jnp.bfloat16)
    attended = jnp.einsum(
        "hqk,khd->qhd", probs_low, value_block, preferred_element_type=jnp.float32
    )
    return (attended, peak_score + jnp.log(totals))


def attend_back(operands):
    query_block, key_block, value_block, log_total, grad_block = operands
    scores = (
        jnp.einsum("qhd,khd->hqk", query_block, key_block, preferred_element_type=jnp.float32)
        * 0.125
    )
    probs = jnp.exp(scores - log_total)
    grad_probs = jnp.einsum(
        "qhd,khd->hqk", grad_block, value_block, preferred_element_type=jnp.float32
    )
    delta = jnp.sum(probs * grad_probs, axis=-1, keepdims=True)
    grad_scores = (probs * (grad_probs - delta)).astype(jnp.bfloat16)
    grad_query = (
        jnp.einsum("hqk,khd->qhd", grad_scores, key_block, preferred_element_type=jnp.float32)
        * 0.125
    )
    grad_key = (
        jnp.einsum("hqk,qhd->khd", grad_scores, query_block, preferred_element_type=jnp.float32)
        * 0.125
    )
    grad_value = jnp.einsum(
        "hqk,qhd->khd", probs.astype(jnp.bfloat16), grad_block, preferred_element_type=jnp.float32
    )
    return (grad_query, grad_key, grad_value)


def adam_update(weight, gradient, first_old, second_old, step_rate, decay_rate):
    first_new = 0.5 * first_old + 0.5 * gradient
    second_new = 0.5 * second_old + 0.5 * gradient * gradient
    correction = 1.0 - 0.5**STEP
    update = (
        first_new / correction / (jnp.sqrt(second_new / correction) + adam_epsilon)
        + decay_rate * weight
    )
    return (first_new, second_new, weight - step_rate * update)


def per_device_split(
    x_tokens,
    out_grad,
    w_qkv,
    w_out,
    w_up,
    w_down,
    vectors,
    qkv_mean,
    qkv_square,
    out_mean,
    out_square,
    up_mean,
    up_square,
    down_mean,
    down_square,
    vectors_mean,
    vectors_square,
):
    masters = (w_qkv, w_out, w_up, w_down, vectors)
    lowered = tuple((member.astype(jnp.bfloat16) for member in masters))
    qkv_low, out_low, up_low, down_low, vector_low = (
        lax.all_gather(lowered[0], "ctx", axis=0, tiled=True),
        lax.all_gather(lowered[1], "ctx", axis=0, tiled=True),
        lax.all_gather(lowered[2], "ctx", axis=0, tiled=True),
        lax.all_gather(lowered[3], "ctx", axis=0, tiled=True),
        lax.all_gather(lowered[4], "ctx", axis=1, tiled=True),
    )
    vector_rows = vector_low.astype(jnp.float32)
    clip_count, row_count, model_width = x_tokens.shape
    head_count = model_width // HD
    token_total = clip_count * row_count
    flat_rows = x_tokens.reshape(token_total, model_width).astype(jnp.float32)
    norm_one, normed_one, inverse_one = normalize(flat_rows, vector_rows[0], vector_rows[1])
    norm_one_low = norm_one.astype(jnp.bfloat16)
    qkv_shift = jnp.concatenate([vector_rows[2], jnp.zeros_like(vector_rows[2]), vector_rows[3]])
    projected = (
        jnp.dot(norm_one_low, qkv_low, preferred_element_type=jnp.float32) + qkv_shift
    ).astype(jnp.bfloat16)
    query_rows = projected[:, :model_width].reshape(clip_count, row_count, head_count, HD)
    key_local = projected[:, model_width : 2 * model_width].reshape(
        clip_count, row_count, head_count, HD
    )
    value_local = projected[:, 2 * model_width :].reshape(clip_count, row_count, head_count, HD)
    key_rows, value_rows = (
        lax.all_gather(key_local, "ctx", axis=1, tiled=True),
        lax.all_gather(value_local, "ctx", axis=1, tiled=True),
    )
    attended, log_total = lax.map(attend, (query_rows, key_rows, value_rows))
    attended_low = attended.reshape(token_total, model_width).astype(jnp.bfloat16)
    branch = jnp.dot(attended_low, out_low, preferred_element_type=jnp.float32) + vector_rows[4]
    resid = flat_rows + branch
    norm_two, normed_two, inverse_two = normalize(resid, vector_rows[5], vector_rows[6])
    norm_two_low = norm_two.astype(jnp.bfloat16)
    pre_act = jnp.dot(norm_two_low, up_low, preferred_element_type=jnp.float32) + vector_rows[
        8:
    ].reshape(-1)
    act_low = (pre_act * normal_cdf(pre_act)).astype(jnp.bfloat16)
    mlp_out = jnp.dot(act_low, down_low, preferred_element_type=jnp.float32) + vector_rows[7]
    y_tokens = (resid + mlp_out).astype(jnp.bfloat16).reshape(clip_count, row_count, model_width)
    grad_output = out_grad.reshape(token_total, model_width)
    grad_float = grad_output.astype(jnp.float32)
    grad_down = jnp.einsum("tf,td->fd", act_low, grad_output, preferred_element_type=jnp.float32)
    down_shift = jnp.sum(grad_float, axis=0)
    grad_act = jnp.dot(grad_output, down_low.T, preferred_element_type=jnp.float32)
    density = jnp.exp(-0.5 * pre_act * pre_act) * 0.3989422804014327
    grad_pre = (grad_act * (normal_cdf(pre_act) + pre_act * density)).astype(jnp.bfloat16)
    grad_up = jnp.einsum("td,tf->df", norm_two_low, grad_pre, preferred_element_type=jnp.float32)
    up_shift = jnp.sum(grad_pre.astype(jnp.float32), axis=0)
    grad_norm_two = jnp.dot(grad_pre, up_low.T, preferred_element_type=jnp.float32)
    gain_two_grad = jnp.sum(grad_norm_two * normed_two, axis=0)
    shift_two_grad = jnp.sum(grad_norm_two, axis=0)
    grad_resid = grad_float + norm_back(grad_norm_two, vector_rows[5], normed_two, inverse_two)
    grad_branch = grad_resid.astype(jnp.bfloat16)
    grad_out = jnp.einsum(
        "td,te->de", attended_low, grad_branch, preferred_element_type=jnp.float32
    )
    out_shift = jnp.sum(grad_branch.astype(jnp.float32), axis=0)
    grad_attended = jnp.dot(grad_branch, out_low.T, preferred_element_type=jnp.float32).astype(
        jnp.bfloat16
    )
    grad_attended = grad_attended.reshape(clip_count, row_count, head_count, HD)
    grad_query, key_terms, value_terms = lax.map(
        attend_back, (query_rows, key_rows, value_rows, log_total, grad_attended)
    )
    grad_key, grad_value = (
        lax.psum_scatter(
            key_terms.astype(jnp.bfloat16), "ctx", scatter_dimension=1, tiled=True
        ).astype(jnp.float32),
        lax.psum_scatter(
            value_terms.astype(jnp.bfloat16), "ctx", scatter_dimension=1, tiled=True
        ).astype(jnp.float32),
    )
    grad_projected = jnp.concatenate(
        [
            grad_query.reshape(token_total, model_width),
            grad_key.reshape(token_total, model_width),
            grad_value.reshape(token_total, model_width),
        ],
        axis=1,
    ).astype(jnp.bfloat16)
    grad_qkv = jnp.einsum(
        "td,te->de", norm_one_low, grad_projected, preferred_element_type=jnp.float32
    )
    projected_sums = jnp.sum(grad_projected.astype(jnp.float32), axis=0)
    grad_norm_one = jnp.dot(grad_projected, qkv_low.T, preferred_element_type=jnp.float32)
    gain_one_grad = jnp.sum(grad_norm_one * normed_one, axis=0)
    shift_one_grad = jnp.sum(grad_norm_one, axis=0)
    x_grad = (
        grad_resid + norm_back(grad_norm_one, vector_rows[0], normed_one, inverse_one)
    ).astype(jnp.bfloat16)
    x_grad = x_grad.reshape(clip_count, row_count, model_width)
    first_rows = jnp.stack(
        [
            gain_one_grad,
            shift_one_grad,
            projected_sums[:model_width],
            projected_sums[2 * model_width :],
            out_shift,
            gain_two_grad,
            shift_two_grad,
            down_shift,
        ]
    )
    grad_vectors = jnp.concatenate([first_rows, up_shift.reshape(-1, model_width)], axis=0)
    group_size = lax.axis_size("ctx")
    vector_count = grad_vectors.shape[0]
    flat_vectors = (
        grad_vectors.reshape(vector_count, group_size, -1)
        .transpose(1, 0, 2)
        .reshape(group_size, -1)
    )
    shaped = (grad_qkv, grad_out, grad_up, grad_down, flat_vectors)
    spread = (
        lax.psum_scatter(
            shaped[0].astype(jnp.bfloat16), "dp", scatter_dimension=1, tiled=True
        ).astype(jnp.float32),
        lax.psum_scatter(
            shaped[1].astype(jnp.bfloat16), "dp", scatter_dimension=1, tiled=True
        ).astype(jnp.float32),
        lax.psum_scatter(
            shaped[2].astype(jnp.bfloat16), "dp", scatter_dimension=1, tiled=True
        ).astype(jnp.float32),
        lax.psum_scatter(
            shaped[3].astype(jnp.bfloat16), "dp", scatter_dimension=1, tiled=True
        ).astype(jnp.float32),
        lax.psum_scatter(
            shaped[4].astype(jnp.bfloat16), "dp", scatter_dimension=1, tiled=True
        ).astype(jnp.float32),
    )
    owned = (
        lax.psum_scatter(
            spread[0].astype(jnp.bfloat16), "ctx", scatter_dimension=0, tiled=True
        ).astype(jnp.float32),
        lax.psum_scatter(
            spread[1].astype(jnp.bfloat16), "ctx", scatter_dimension=0, tiled=True
        ).astype(jnp.float32),
        lax.psum_scatter(
            spread[2].astype(jnp.bfloat16), "ctx", scatter_dimension=0, tiled=True
        ).astype(jnp.float32),
        lax.psum_scatter(
            spread[3].astype(jnp.bfloat16), "ctx", scatter_dimension=0, tiled=True
        ).astype(jnp.float32),
        lax.psum_scatter(
            spread[4].astype(jnp.bfloat16), "ctx", scatter_dimension=0, tiled=True
        ).astype(jnp.float32),
    )
    collected = (
        lax.all_gather(owned[0].astype(jnp.bfloat16), "dp", axis=1, tiled=True).astype(jnp.float32),
        lax.all_gather(owned[1].astype(jnp.bfloat16), "dp", axis=1, tiled=True).astype(jnp.float32),
        lax.all_gather(owned[2].astype(jnp.bfloat16), "dp", axis=1, tiled=True).astype(jnp.float32),
        lax.all_gather(owned[3].astype(jnp.bfloat16), "dp", axis=1, tiled=True).astype(jnp.float32),
        lax.all_gather(owned[4].astype(jnp.bfloat16), "dp", axis=1, tiled=True).astype(jnp.float32),
    )
    shares = (
        collected[0],
        collected[1],
        collected[2],
        collected[3],
        collected[4].reshape(vector_count, -1),
    )
    qkv_moment, qkv_second, qkv_master = adam_update(
        w_qkv, shares[0], qkv_mean, qkv_square, matrix_rate, matrix_decay
    )
    out_moment, out_second, out_master = adam_update(
        w_out, shares[1], out_mean, out_square, matrix_rate, matrix_decay
    )
    up_moment, up_second, up_master = adam_update(
        w_up, shares[2], up_mean, up_square, matrix_rate, matrix_decay
    )
    down_moment, down_second, down_master = adam_update(
        w_down, shares[3], down_mean, down_square, matrix_rate, matrix_decay
    )
    vectors_moment, vectors_second, vectors_master = adam_update(
        vectors, shares[4], vectors_mean, vectors_square, vector_rate, 0.0
    )
    return (
        y_tokens,
        x_grad,
        qkv_moment,
        qkv_second,
        qkv_master,
        out_moment,
        out_second,
        out_master,
        up_moment,
        up_second,
        up_master,
        down_moment,
        down_second,
        down_master,
        vectors_moment,
        vectors_second,
        vectors_master,
    )


LOG2E = 1.4426950408889634
NT = (((1,), (1,)), ((), ()))
NN = (((1,), (0,)), ((), ()))
TN = (((0,), (0,)), ((), ()))
KERNEL_VMEM = 62 * 2**20


def attend_kernel(q_ref, k_ref, v_ref, o_ref, r_ref, p_ref, score_a, score_b):
    rows = score_a.shape[0]
    total = k_ref.shape[0]
    lane = lax.broadcasted_iota(jnp.int32, (1, 2 * HD), 1)
    held = (score_a, score_b)
    parts = total // rows
    items = [(head, part) for head in range(2) for part in range(parts)]

    def score(index):
        head, part = items[index]
        keys = jnp.where((lane // HD) == head, k_ref[...], 0).astype(jnp.bfloat16)
        held[index % 2][...] = lax.dot_general(
            q_ref[part * rows : (part + 1) * rows, :], keys, NT, preferred_element_type=jnp.float32
        )

    def soften(index):
        head, part = items[index]
        values = held[index % 2][...]
        peak = jnp.max(values, axis=1, keepdims=True)
        p_ref[head, part * rows : (part + 1) * rows, :] = jnp.exp2(
            (values - peak) * (0.125 * LOG2E)
        ).astype(jnp.bfloat16)

    def weigh(index):
        head, part = items[index]
        span = slice(part * rows, (part + 1) * rows)
        kept = jnp.where((lane // HD) == head, v_ref[...], 0).astype(jnp.bfloat16)
        table = jnp.concatenate([kept, jnp.ones((total, 2 * HD), jnp.bfloat16)], axis=1)
        out = lax.dot_general(p_ref[head, span, :], table, NN, preferred_element_type=jnp.float32)
        inverse = 1.0 / out[:, 2 * HD :]
        mixed = (out[:, : 2 * HD] * inverse).astype(jnp.bfloat16)
        if head == 0:
            o_ref[span, :] = mixed
            r_ref[span, :] = inverse
        else:
            o_ref[span, :] = jnp.where(lane < HD, o_ref[span, :], mixed)
            r_ref[span, :] = jnp.where(lane < HD, r_ref[span, :], inverse)

    score(0)
    for index in range(len(items)):
        if index + 1 < len(items):
            score(index + 1)
        soften(index)
        weigh(index)


def attend_back_kernel(
    q_ref, k_ref, v_ref, g_ref, o_ref, r_ref, p_ref, dq_ref, dk_ref, dv_ref, ds, qt, gt, dkt, dvt
):
    head = pl.program_id(1)
    total = k_ref.shape[0]
    half = total // 2
    lane = lax.broadcasted_iota(jnp.int32, (1, 2 * HD), 1)
    keep = (lane // HD) == head
    scaled = g_ref[...].astype(jnp.float32) * r_ref[...]

    @pl.when(head == 0)
    def _():
        qt[...] = q_ref[...].T
        gt[...] = scaled.astype(jnp.bfloat16).T

    delta = jnp.sum(jnp.where(keep, scaled * o_ref[...].astype(jnp.float32), 0.0), axis=1, keepdims=True)
    values = jnp.where(keep, v_ref[...], 0).astype(jnp.bfloat16)
    grad_probs = lax.dot_general(
        scaled.astype(jnp.bfloat16), values, NT, preferred_element_type=jnp.float32
    )
    ds[...] = (p_ref[...].astype(jnp.float32) * (grad_probs - delta)).astype(jnp.bfloat16)
    span = pl.ds(pl.multiple_of(head * HD, HD), HD)
    dvt[span, :] = lax.dot_general(gt[span, :], p_ref[...], NN, preferred_element_type=jnp.float32)
    dkt[span, :] = 0.125 * lax.dot_general(
        qt[span, :], ds[...], NN, preferred_element_type=jnp.float32
    )
    keys = jnp.where(keep, k_ref[...], 0).astype(jnp.bfloat16)
    for part in range(2):
        rows = slice(part * half, (part + 1) * half)
        term = 0.125 * lax.dot_general(ds[rows, :], keys, NN, preferred_element_type=jnp.float32)
        dq_ref[rows, :] = jnp.where(keep, term.astype(jnp.bfloat16), dq_ref[rows, :])

    @pl.when(head == 1)
    def _():
        dk_ref[...] = dkt[...].T.astype(jnp.bfloat16)
        dv_ref[...] = dvt[...].T.astype(jnp.bfloat16)


MESH = pl.DeviceIdType.MESH
STREAMS = (("x", "a", "b"), ("a", "b", "x"), ("b", "x", "a"))


def own_bits():
    place = lax.axis_index("dp")
    z = place // 4
    return {
        "core": place % 2,
        "x": (place // 2) % 2,
        "a": (z % 2 + z // 2) % 2,
        "b": z // 2,
        "y": lax.axis_index("ctx"),
    }


def partner(name):
    place, group = lax.axis_index("dp"), lax.axis_index("ctx")
    z = place // 4
    if name == "core":
        return (place + 1 - 2 * (place % 2), group)
    if name == "x":
        return (place + 2 - 4 * ((place // 2) % 2), group)
    if name == "a":
        return (place + 4 - 8 * (z % 2), group)
    if name == "b":
        return (place + 4 * (3 - 2 * z), group)
    return (place, 1 - group)


def meet_partners():
    barrier = pltpu.get_barrier_semaphore()
    names = ("core", "x", "a", "b", "y")
    for name in names:
        pl.semaphore_signal(barrier, inc=1, device_id=partner(name), device_id_type=MESH)
    pl.semaphore_wait(barrier, len(names))


def remote(source, target, name, send_sem, recv_sem):
    return pltpu.make_async_remote_copy(
        src_ref=source,
        dst_ref=target,
        send_sem=send_sem,
        recv_sem=recv_sem,
        device_id=partner(name),
        device_id_type=MESH,
    )


def block_of(stream, bits):
    first, second, third = STREAMS[stream]
    return bits[first] * 4 + bits[second] * 2 + bits[third]


class Gather:
    stages = 4

    def __init__(self, buffer, send, recv):
        self.buffer, self.send, self.recv = buffer, send, recv

    def copy(self, stage, stream):
        bits = own_bits()
        block = block_of(stream, bits)
        size = (1, 2, 4, 8)[stage]
        name = (STREAMS[stream][::-1] + ("core",))[stage]
        region = self.buffer.at[bits["core"], stream, pl.ds(block // size * size, size)]
        return remote(region, region, name, self.send.at[stage, stream], self.recv.at[stage, stream])

    def begin(self):
        for stream in range(3):
            self.copy(0, stream).start()

    def advance(self, stage):
        for stream in range(3):
            self.copy(stage, stream).wait()
            if stage + 1 < self.stages:
                self.copy(stage + 1, stream).start()


class ScatterSum:
    stages = 5

    def __init__(self, source, total, landing, send, recv, local):
        self.source, self.total, self.landing = source, total, landing
        self.send, self.recv, self.local = send, recv, local

    def kept(self, stream):
        core = own_bits()["core"]
        return pltpu.make_async_copy(
            self.source.at[:, core, stream], self.total.at[:, stream], self.local.at[stream]
        )

    def offsets(self, stage, stream):
        bits = own_bits()
        first, second, third = (bits[name] for name in STREAMS[stream])
        if stage == 1:
            return 4 * (1 - first), 4 * first, 4
        if stage == 2:
            return 4 * first + 2 * (1 - second), 4 * first + 2 * second, 2
        return 4 * first + 2 * second + 1 - third, 4 * first + 2 * second + third, 1

    def copy(self, stage, stream):
        bits = own_bits()
        sems = (self.send.at[stage, stream], self.recv.at[stage, stream])
        if stage == 0:
            source = self.source.at[:, 1 - bits["core"], stream]
            return remote(source, self.landing[0].at[:, stream], "core", *sems)
        if stage == 4:
            block = block_of(stream, bits)
            source = self.total.at[1 - bits["y"], stream, block]
            return remote(source, self.landing[4].at[stream], "y", *sems)
        start, _, size = self.offsets(stage, stream)
        source = self.total.at[:, stream, pl.ds(start, size)]
        return remote(
            source, self.landing[stage].at[:, stream], STREAMS[stream][stage - 1], *sems
        )

    def begin(self):
        for stream in range(3):
            self.copy(0, stream).start()
            self.kept(stream).start()

    def add(self, stage, stream):
        if stage == 4:
            bits = own_bits()
            at = (bits["y"], stream, block_of(stream, bits))
            self.total[at] = (
                self.total[at].astype(jnp.float32)
                + self.landing[4][stream].astype(jnp.float32)
            ).astype(jnp.bfloat16)
            return
        start, size = 0, 8
        if stage > 0:
            _, start, size = self.offsets(stage, stream)

        @pl.loop(0, 2)
        def _(half):
            @pl.loop(0, size)
            def _(block):
                at = (half, stream, start + block)
                self.total[at] = (
                    self.total[at].astype(jnp.float32)
                    + self.landing[stage][half, stream, block].astype(jnp.float32)
                ).astype(jnp.bfloat16)

    def advance(self, stage):
        for stream in range(3):
            self.copy(stage, stream).wait()
            if stage == 0:
                self.kept(stream).wait()
            self.add(stage, stream)
            if stage + 1 < self.stages:
                self.copy(stage + 1, stream).start()

    def place(self, gathered, sems):
        bits = own_bits()
        copies = []
        for stream in range(3):
            block = block_of(stream, bits)
            copies.append(
                pltpu.make_async_copy(
                    self.total.at[bits["y"], stream, block],
                    gathered.at[bits["core"], stream, block],
                    sems.at[stream],
                )
            )
        return copies


def sum_scratch(rows, columns):
    low = jnp.bfloat16
    return [
        pltpu.VMEM((2, 3, 8, rows, columns), low),
        pltpu.VMEM((2, 3, 8, rows, columns), low),
        pltpu.VMEM((2, 3, 4, rows, columns), low),
        pltpu.VMEM((2, 3, 2, rows, columns), low),
        pltpu.VMEM((2, 3, 1, rows, columns), low),
        pltpu.VMEM((3, rows, columns), low),
        pltpu.SemaphoreType.DMA((5, 3)),
        pltpu.SemaphoreType.DMA((5, 3)),
        pltpu.SemaphoreType.DMA((3,)),
    ]


def gather_scratch():
    return [pltpu.SemaphoreType.DMA((4, 3)), pltpu.SemaphoreType.DMA((4, 3))]


def local_copy(source, target, sem):
    return pltpu.make_async_copy(source, target, sem)


def start_kernel(
    x_ref, w_ref, vec_ref, x2_ref, proj_ref, wqkv_ref, wout_ref, vecs_ref,
    norm, other, vec_other, g_send, g_recv, w_send, w_recv, x_send, x_recv, v_sem, l_sem,
):
    bits = own_bits()
    me = bits["y"]
    half, width = x_ref.shape[1], x_ref.shape[2]
    gather = Gather(other, g_send, g_recv)
    meet_partners()
    vec_copy = remote(vec_ref, vec_other, "y", v_sem.at[0], v_sem.at[1])
    vec_copy.start()
    own_x = local_copy(x_ref.at[me], x2_ref.at[pl.ds(0, half)], l_sem)
    own_x.start()
    pieces = []
    for stream in range(3):
        block = block_of(stream, bits)
        piece = remote(
            w_ref.at[bits["core"], stream, block],
            other.at[bits["core"], stream, block],
            "y",
            w_send.at[stream],
            w_recv.at[stream],
        )
        piece.start()
        pieces.append(piece)
    first = half // 32 * 16 + 16
    spans = [(0, first), (first, half - first)]
    trades = [
        remote(
            x_ref.at[1 - me, pl.ds(at, size)],
            x2_ref.at[pl.ds(half + at, size)],
            "y",
            x_send.at[index],
            x_recv.at[index],
        )
        for index, (at, size) in enumerate(spans)
    ]
    for piece in pieces:
        piece.wait()
    gather.begin()
    trades[0].start()
    vec_copy.wait()
    mine, others = vec_ref[...], vec_other[...]
    vecs_ref[...] = jnp.where(
        me == 0,
        jnp.concatenate([mine, others], axis=1),
        jnp.concatenate([others, mine], axis=1),
    )
    gather.advance(0)
    trades[1].start()

    def norm_rows(at, size):
        values = x2_ref[at : at + size, :].astype(jnp.float32)
        normed, _, _ = normalize(values, vecs_ref[0:1, :], vecs_ref[1:2, :])
        norm[at : at + size, :] = normed.astype(jnp.bfloat16)

    own_x.wait()
    norm_rows(0, half)
    for stage in range(1, 4):
        gather.advance(stage)
    part = width // 2

    for source, at in ((w_ref, me * part), (other, (1 - me) * part)):
        for matrix in range(4):
            for index in range(12):
                flat = matrix * 12 + index
                block = source[flat // 24, flat // 8 % 3, flat % 8]
                rows = pl.ds(pl.multiple_of(at + index * 32, 32), 32)
                if matrix < 3:
                    wqkv_ref[rows, matrix * width : (matrix + 1) * width] = block
                else:
                    wout_ref[rows, :] = block

    def project(at, size):
        @pl.loop(0, 3)
        def _(matrix):
            cols = pl.ds(pl.multiple_of(matrix * width, 128), width)
            shift = jnp.where(matrix == 0, vecs_ref[2:3, :], vecs_ref[3:4, :])
            shift = jnp.where(matrix == 1, 0.0, shift)
            proj_ref[at : at + size, cols] = (
                lax.dot_general(
                    norm[at : at + size, :], wqkv_ref[:, cols], NN, preferred_element_type=jnp.float32
                )
                + shift
            ).astype(jnp.bfloat16)

    project(0, half)
    for trade, (at, size) in zip(trades, spans):
        trade.wait()
        norm_rows(half + at, size)
        project(half + at, size)


def start_call(x_tokens, weights, vector_own):
    _, half, width = x_tokens.shape
    low = jnp.bfloat16
    anywhere = pl.BlockSpec(memory_space=pl.ANY)
    vmem = pl.BlockSpec(memory_space=pltpu.VMEM)
    dma = pltpu.SemaphoreType.DMA
    return pl.pallas_call(
        start_kernel,
        in_specs=[anywhere, vmem, vmem],
        out_specs=[vmem] * 5,
        out_shape=[
            jax.ShapeDtypeStruct((2 * half, width), low),
            jax.ShapeDtypeStruct((2 * half, 3 * width), low),
            jax.ShapeDtypeStruct((width, 3 * width), low),
            jax.ShapeDtypeStruct((width, width), low),
            jax.ShapeDtypeStruct((16, width), jnp.float32),
        ],
        scratch_shapes=[
            pltpu.VMEM((2 * half, width), low),
            pltpu.VMEM(weights.shape, low),
            pltpu.VMEM(vector_own.shape, jnp.float32),
        ]
        + gather_scratch()
        + [dma((3,)), dma((3,)), dma((2,)), dma((2,)), dma((2,)), dma],
        compiler_params=pltpu.CompilerParams(
            vmem_limit_bytes=KERNEL_VMEM, collective_id=1, has_side_effects=True
        ),
        name="start",
    )(x_tokens, weights, vector_own)


def attend_gather_kernel(
    q_ref, k_ref, v_ref, w_ref, grad_ref, o_ref, r_ref, p_ref, other_ref, grad2_ref,
    score_a, score_b, g_send, g_recv, w_send, w_recv, t_send, t_recv, l_sem,
):
    step = pl.program_id(0)
    last = pl.num_programs(0) - 1
    bits = own_bits()
    me = bits["y"]
    half = grad_ref.shape[1]
    gather = Gather(other_ref, g_send, g_recv)

    def piece(stream):
        block = block_of(stream, bits)
        return remote(
            w_ref.at[bits["core"], stream, block],
            other_ref.at[bits["core"], stream, block],
            "y",
            w_send.at[stream],
            w_recv.at[stream],
        )

    trade = remote(
        grad_ref.at[1 - me], grad2_ref.at[pl.ds(half, half)], "y", t_send, t_recv
    )
    own = local_copy(grad_ref.at[me], grad2_ref.at[pl.ds(0, half)], l_sem)

    @pl.when(step == 0)
    def _():
        meet_partners()
        for stream in range(3):
            piece(stream).start()
        own.start()

    @pl.when(step == 1)
    def _():
        for stream in range(3):
            piece(stream).wait()
        gather.begin()
        trade.start()

    for stage in range(3):
        @pl.when(step == 2 + stage)
        def _(stage=stage):
            gather.advance(stage)

    attend_kernel(q_ref, k_ref, v_ref, o_ref, r_ref, p_ref, score_a, score_b)

    @pl.when(step == last)
    def _():
        gather.advance(3)
        trade.wait()
        own.wait()


def attend_call(projected, weights, out_grad, width):
    total = projected.shape[0]
    pairs = width // (2 * HD)
    half = out_grad.shape[1]
    anywhere = pl.BlockSpec(memory_space=pl.ANY)
    dma = pltpu.SemaphoreType.DMA

    def columns(start):
        return pl.BlockSpec((total, 2 * HD), lambda p: (0, start * pairs + p))

    return pl.pallas_call(
        attend_gather_kernel,
        grid=(pairs,),
        in_specs=[columns(0), columns(1), columns(2), anywhere, anywhere],
        out_specs=[
            columns(0),
            columns(0),
            pl.BlockSpec((2, total, total), lambda p: (p, 0, 0)),
            anywhere,
            anywhere,
        ],
        out_shape=[
            jax.ShapeDtypeStruct((total, width), jnp.bfloat16),
            jax.ShapeDtypeStruct((total, width), jnp.float32),
            jax.ShapeDtypeStruct((2 * pairs, total, total), jnp.bfloat16),
            jax.ShapeDtypeStruct(weights.shape, jnp.bfloat16),
            jax.ShapeDtypeStruct((2 * half, width), jnp.bfloat16),
        ],
        scratch_shapes=[pltpu.VMEM((total // 2, total), jnp.float32)] * 2
        + gather_scratch()
        + [dma((3,)), dma((3,)), dma, dma, dma],
        compiler_params=pltpu.CompilerParams(
            vmem_limit_bytes=KERNEL_VMEM, collective_id=2, has_side_effects=True
        ),
        cost_estimate=pl.CostEstimate(
            flops=16 * pairs * total * total * 2 * HD,
            bytes_accessed=4 * pairs * total * total,
            transcendentals=2 * pairs * total * total,
        ),
        name="attend",
    )(projected, projected, projected, weights, out_grad)


def attend_back_sum_kernel(
    q_ref, k_ref, v_ref, g_ref, o_ref, r_ref, p_ref, grads_ref, y2_ref,
    dq_ref, dk_ref, dv_ref, shared_ref, tokens_ref,
    ds, qt, gt, dkt, dvt,
    total, land0, land1, land2, land3, land4, s_send, s_recv, s_local,
    g_send, g_recv, p_sem, t_send, t_recv, l_sem,
):
    step = pl.program_id(0) * 2 + pl.program_id(1)
    last = pl.num_programs(0) * 2 - 1
    bits = own_bits()
    me = bits["y"]
    half = tokens_ref.shape[1]
    summing = ScatterSum(
        grads_ref, total, (land0, land1, land2, land3, land4), s_send, s_recv, s_local
    )
    gather = Gather(shared_ref, g_send, g_recv)
    trade = remote(y2_ref.at[pl.ds(half, half)], tokens_ref.at[me], "y", t_send, t_recv)
    own = local_copy(y2_ref.at[pl.ds(0, half)], tokens_ref.at[me], l_sem)

    @pl.when(step == 0)
    def _():
        meet_partners()
        summing.begin()
        own.start()
        trade.start()

    for stage, at in enumerate((2, 6, 8, 9, 11)):
        @pl.when(step == at)
        def _(stage=stage):
            summing.advance(stage)
            if stage == 4:
                placed = summing.place(shared_ref, p_sem)
                for copy in placed:
                    copy.start()
                for copy in placed:
                    copy.wait()
                gather.begin()

    attend_back_kernel(
        q_ref, k_ref, v_ref, g_ref, o_ref, r_ref, p_ref, dq_ref, dk_ref, dv_ref, ds, qt, gt, dkt, dvt
    )

    @pl.when(step == last)
    def _():
        for stage in range(4):
            gather.advance(stage)
        trade.wait()
        own.wait()


def attend_back_call(projected, upstream, attended, inverse, exponent, grads, y2):
    total, width = attended.shape
    pairs = width // (2 * HD)
    rows = grads.shape[4]
    anywhere = pl.BlockSpec(memory_space=pl.ANY)
    dma = pltpu.SemaphoreType.DMA

    def columns(start):
        return pl.BlockSpec((total, 2 * HD), lambda p, h: (0, start * pairs + p))

    return pl.pallas_call(
        attend_back_sum_kernel,
        grid=(pairs, 2),
        in_specs=[columns(0), columns(1), columns(2), columns(0), columns(0), columns(0)]
        + [pl.BlockSpec((None, total, total), lambda p, h: (p * 2 + h, 0, 0))]
        + [anywhere, anywhere],
        out_specs=[columns(0)] * 3 + [anywhere, anywhere],
        out_shape=[jax.ShapeDtypeStruct((total, width), jnp.bfloat16)] * 3
        + [
            jax.ShapeDtypeStruct(grads.shape[1:], jnp.bfloat16),
            jax.ShapeDtypeStruct((2, total // 2, width), jnp.bfloat16),
        ],
        scratch_shapes=[pltpu.VMEM((total, total), jnp.bfloat16)]
        + [pltpu.VMEM((2 * HD, total), jnp.bfloat16)] * 2
        + [pltpu.VMEM((2 * HD, total), jnp.float32)] * 2
        + sum_scratch(rows, width)
        + gather_scratch()
        + [dma((3,)), dma, dma, dma],
        compiler_params=pltpu.CompilerParams(
            vmem_limit_bytes=KERNEL_VMEM, collective_id=3, has_side_effects=True
        ),
        cost_estimate=pl.CostEstimate(
            flops=32 * pairs * total * total * 2 * HD,
            bytes_accessed=4 * pairs * total * total,
            transcendentals=0,
        ),
        name="attend_back",
    )(projected, projected, projected, upstream, attended, inverse, exponent, grads, y2)


def finish_kernel(
    dq_ref, dk_ref, dv_ref, x_ref, w_ref, vec_ref, resid_ref, out_ref, part_ref,
    xg_ref, shared_ref, vsum_ref,
    grads, turned, sent_rows, own_rows,
    total, land0, land1, land2, land3, land4, s_send, s_recv, s_local,
    g_send, g_recv, p_sem, t_send, t_recv, l_sem, v_land, v_send, v_recv,
):
    bits = own_bits()
    me = bits["y"]
    rows, width = x_ref.shape
    half = rows // 2
    summing = ScatterSum(
        grads, total, (land0, land1, land2, land3, land4), s_send, s_recv, s_local
    )
    gather = Gather(shared_ref, g_send, g_recv)
    gain, shift = vec_ref[0:1, :], vec_ref[1:2, :]
    meet_partners()

    def place(matrix, values):
        for side in range(2):
            for index in range(12):
                flat = matrix * 12 + index
                at = side * (width // 2) + index * 32
                grads[side, flat // 24, flat // 8 % 3, flat % 8] = values[at : at + 32, :]

    place(3, out_ref[...])
    norm_one, _, _ = normalize(x_ref[...].astype(jnp.float32), gain, shift)
    turned[...] = norm_one.astype(jnp.bfloat16).T
    for matrix, part in enumerate((dq_ref, dk_ref, dv_ref)):
        place(
            matrix,
            lax.dot_general(turned[...], part[...], NN, preferred_element_type=jnp.float32).astype(
                jnp.bfloat16
            ),
        )
    summing.begin()

    def input_rows(at, target):
        span = slice(at, at + half)
        upstream = None
        for matrix, part in enumerate((dq_ref, dk_ref, dv_ref)):
            term = lax.dot_general(
                part[span, :],
                w_ref[:, matrix * width : (matrix + 1) * width],
                NT,
                preferred_element_type=jnp.float32,
            )
            upstream = term if upstream is None else upstream + term
        _, normed, inverse = normalize(x_ref[span, :].astype(jnp.float32), gain, shift)
        target[...] = (resid_ref[span, :] + norm_back(upstream, gain, normed, inverse)).astype(
            jnp.bfloat16
        )
        return (
            jnp.sum(upstream * normed, axis=0, keepdims=True),
            jnp.sum(upstream, axis=0, keepdims=True),
        )

    other_sums = input_rows(half, sent_rows)
    trade = remote(sent_rows, xg_ref.at[me], "y", t_send, t_recv)
    trade.start()
    summing.advance(0)
    own_sums = input_rows(0, own_rows)
    own = local_copy(own_rows, xg_ref.at[me], l_sem)
    own.start()
    summing.advance(1)
    vsum_ref[...] = part_ref[...]
    vsum_ref[0:1, :] = own_sums[0] + other_sums[0]
    vsum_ref[1:2, :] = own_sums[1] + other_sums[1]
    vsum_ref[2:3, :] = jnp.sum(dq_ref[...].astype(jnp.float32), axis=0, keepdims=True)
    vsum_ref[3:4, :] = jnp.sum(dv_ref[...].astype(jnp.float32), axis=0, keepdims=True)

    def vector_step(stage):
        name = ("core", "x", "a", "b", "y")[stage]
        return remote(vsum_ref, v_land.at[stage], name, v_send.at[stage], v_recv.at[stage])

    def vector_add(stage):
        vector_step(stage).wait()
        vsum_ref[...] += v_land[stage]
        if stage < 4:
            vector_step(stage + 1).start()

    vector_step(0).start()
    summing.advance(2)
    vector_add(0)
    summing.advance(3)
    vector_add(1)
    summing.advance(4)
    placed = summing.place(shared_ref, p_sem)
    for copy in placed:
        copy.start()
    for copy in placed:
        copy.wait()
    gather.begin()
    vector_add(2)
    gather.advance(0)
    vector_add(3)
    gather.advance(1)
    vector_add(4)
    gather.advance(2)
    gather.advance(3)
    trade.wait()
    own.wait()


def finish_call(grad_parts, x2, wqkv, vecs, grad_resid, grad_out, part_sums):
    total, width = x2.shape
    low = jnp.bfloat16
    anywhere = pl.BlockSpec(memory_space=pl.ANY)
    vmem = pl.BlockSpec(memory_space=pltpu.VMEM)
    dma = pltpu.SemaphoreType.DMA
    rows = width // 24
    return pl.pallas_call(
        finish_kernel,
        in_specs=[vmem] * 9,
        out_specs=[anywhere, anywhere, vmem],
        out_shape=[
            jax.ShapeDtypeStruct((2, total // 2, width), low),
            jax.ShapeDtypeStruct((2, 3, 8, rows, width), low),
            jax.ShapeDtypeStruct((16, width), jnp.float32),
        ],
        scratch_shapes=[
            pltpu.VMEM((2, 2, 3, 8, rows, width), low),
            pltpu.VMEM((width, total), low),
            pltpu.VMEM((total // 2, width), low),
            pltpu.VMEM((total // 2, width), low),
        ]
        + sum_scratch(rows, width)
        + gather_scratch()
        + [dma((3,)), dma, dma, dma, pltpu.VMEM((5, 16, width), jnp.float32), dma((5,)), dma((5,))],
        compiler_params=pltpu.CompilerParams(
            vmem_limit_bytes=KERNEL_VMEM, collective_id=4, has_side_effects=True
        ),
        name="finish",
    )(*grad_parts, x2, wqkv, vecs, grad_resid, grad_out, part_sums)


def per_device_clips(
    x_tokens,
    out_grad,
    w_qkv,
    w_out,
    w_up,
    w_down,
    vectors,
    qkv_mean,
    qkv_square,
    out_mean,
    out_square,
    up_mean,
    up_square,
    down_mean,
    down_square,
    vectors_mean,
    vectors_square,
):
    me = lax.axis_index("ctx")
    width = x_tokens.shape[2]
    low = jnp.bfloat16
    side = width // 2

    def blocks(values, start, count):
        return [values[:, (start + i) * width : (start + i + 1) * width] for i in range(count)]

    first_weights = jnp.concatenate(blocks(w_qkv, 0, 3) + [w_out], axis=0).astype(low)
    first_weights = first_weights.reshape(2, 3, 8, -1, width)
    late_weights = jnp.concatenate([w_down] + blocks(w_up, 0, 4), axis=0).astype(low)
    late_weights = late_weights.reshape(2, 3, 8, -1, width)
    vector_own = jnp.pad(vectors.astype(low).astype(jnp.float32), ((0, 4), (0, 0)))

    x_low, projected, qkv_low, out_low, vector_rows = start_call(
        x_tokens, first_weights, vector_own
    )
    attended_low, inverse_total, exponent, late_other, grad_output = attend_call(
        projected, late_weights, out_grad, width
    )
    mine, other = late_weights.reshape(-1, width), late_other.reshape(-1, width)
    sides = [jnp.where(me == 0, mine, other), jnp.where(me == 0, other, mine)]
    down_low = jnp.concatenate([part[: 4 * side] for part in sides], axis=0)
    up_low = jnp.concatenate(
        [
            jnp.concatenate(
                [part[(4 + i) * side : (5 + i) * side] for i in range(4)], axis=1
            )
            for part in sides
        ],
        axis=0,
    )

    flat_rows = x_low.astype(jnp.float32)
    branch = jnp.dot(attended_low, out_low, preferred_element_type=jnp.float32) + vector_rows[4]
    resid = flat_rows + branch
    norm_two, normed_two, inverse_two = normalize(resid, vector_rows[5], vector_rows[6])
    norm_two_low = norm_two.astype(jnp.bfloat16)
    pre_act = jnp.dot(norm_two_low, up_low, preferred_element_type=jnp.float32) + vector_rows[
        8:12
    ].reshape(-1)
    act_low = (pre_act * normal_cdf(pre_act)).astype(jnp.bfloat16)
    mlp_out = jnp.dot(act_low, down_low, preferred_element_type=jnp.float32) + vector_rows[7]
    y_rows = (resid + mlp_out).astype(jnp.bfloat16)

    grad_float = grad_output.astype(jnp.float32)
    grad_down = jnp.einsum(
        "tf,td->fd", act_low, grad_output, preferred_element_type=jnp.float32
    ).astype(jnp.bfloat16)
    down_shift = jnp.sum(grad_float, axis=0)
    grad_act = jnp.dot(grad_output, down_low.T, preferred_element_type=jnp.float32)
    density = jnp.exp(-0.5 * pre_act * pre_act) * 0.3989422804014327
    grad_pre = (grad_act * (normal_cdf(pre_act) + pre_act * density)).astype(jnp.bfloat16)
    grad_up = jnp.einsum(
        "td,tf->df", norm_two_low, grad_pre, preferred_element_type=jnp.float32
    ).astype(jnp.bfloat16)
    late_grads = jnp.stack(
        [
            jnp.concatenate(
                [grad_down[i * 4 * side : (i + 1) * 4 * side]]
                + blocks(grad_up[i * side : (i + 1) * side], 0, 4),
                axis=0,
            )
            for i in range(2)
        ]
    ).reshape(2, 2, 3, 8, -1, width)

    up_shift = jnp.sum(grad_pre.astype(jnp.float32), axis=0)
    grad_norm_two = jnp.dot(grad_pre, up_low.T, preferred_element_type=jnp.float32)
    gain_two_grad = jnp.sum(grad_norm_two * normed_two, axis=0)
    shift_two_grad = jnp.sum(grad_norm_two, axis=0)
    grad_resid = grad_float + norm_back(grad_norm_two, vector_rows[5], normed_two, inverse_two)
    grad_branch = grad_resid.astype(jnp.bfloat16)
    grad_out = jnp.einsum(
        "td,te->de", attended_low, grad_branch, preferred_element_type=jnp.float32
    ).astype(jnp.bfloat16)
    out_shift = jnp.sum(grad_branch.astype(jnp.float32), axis=0)
    grad_attended = jnp.dot(grad_branch, out_low.T, preferred_element_type=jnp.float32).astype(
        jnp.bfloat16
    )
    part_sums = jnp.concatenate(
        [
            jnp.zeros((4, width), jnp.float32),
            jnp.stack([out_shift, gain_two_grad, shift_two_grad, down_shift]),
            up_shift.reshape(-1, width),
            jnp.zeros((4, width), jnp.float32),
        ],
        axis=0,
    )
    *grad_parts, late_shared, y_tokens = attend_back_call(
        projected,
        grad_attended,
        attended_low,
        inverse_total,
        exponent,
        late_grads,
        y_rows,
    )
    x_grad, first_shared, summed_vectors = finish_call(
        grad_parts, x_low, qkv_low, vector_rows, grad_resid, grad_out, part_sums
    )

    late_share = late_shared.reshape(-1, width).astype(jnp.float32)
    first_share = first_shared.reshape(4, side, width).astype(jnp.float32)
    down_share = late_share[: 4 * side]
    up_share = jnp.concatenate(
        [late_share[(4 + i) * side : (5 + i) * side] for i in range(4)], axis=1
    )
    qkv_share = jnp.concatenate([first_share[i] for i in range(3)], axis=1)
    vector_share = lax.dynamic_slice_in_dim(summed_vectors[:12], me * side, side, axis=1)

    qkv_new = adam_update(w_qkv, qkv_share, qkv_mean, qkv_square, matrix_rate, matrix_decay)
    out_new = adam_update(w_out, first_share[3], out_mean, out_square, matrix_rate, matrix_decay)
    up_new = adam_update(w_up, up_share, up_mean, up_square, matrix_rate, matrix_decay)
    down_new = adam_update(w_down, down_share, down_mean, down_square, matrix_rate, matrix_decay)
    vectors_new = adam_update(
        vectors, vector_share, vectors_mean, vectors_square, vector_rate, 0.0
    )
    return (y_tokens, x_grad) + qkv_new + out_new + up_new + down_new + vectors_new


def per_device(x_tokens, *others):
    clips = x_tokens.shape[0]
    if lax.axis_size("ctx") == 2 and lax.axis_size("dp") == 16 and clips == 2:
        return per_device_clips(x_tokens, *others)
    return per_device_split(x_tokens, *others)


def solution(mesh):
    return jax.shard_map(
        per_device,
        mesh=mesh,
        in_specs=(
            P("dp", "ctx", None),
            P("dp", "ctx", None),
            P("ctx", None),
            P("ctx", None),
            P("ctx", None),
            P("ctx", None),
            P(None, "ctx"),
            P("ctx", None),
            P("ctx", None),
            P("ctx", None),
            P("ctx", None),
            P("ctx", None),
            P("ctx", None),
            P("ctx", None),
            P("ctx", None),
            P(None, "ctx"),
            P(None, "ctx"),
        ),
        out_specs=(
            P("dp", "ctx", None),
            P("dp", "ctx", None),
            P("ctx", None),
            P("ctx", None),
            P("ctx", None),
            P("ctx", None),
            P("ctx", None),
            P("ctx", None),
            P("ctx", None),
            P("ctx", None),
            P("ctx", None),
            P("ctx", None),
            P("ctx", None),
            P("ctx", None),
            P(None, "ctx"),
            P(None, "ctx"),
            P(None, "ctx"),
        ),
        check_vma=False,
    )
```

```python
import functools

import jax
import jax.numpy as jnp
from jax import lax
from jax.experimental import pallas as pl
from jax.experimental.pallas import tpu as pltpu
from jax.sharding import PartitionSpec as P

HD = 64
STEP = 10


norm_epsilon = 1e-06
adam_epsilon = 1e-08
matrix_rate = 0.04
matrix_decay = 0.05
vector_rate = 0.2


def normalize(values, norm_gain, norm_shift):
    row_mean = jnp.mean(values, axis=-1, keepdims=True)
    centred = values - row_mean
    row_var = jnp.mean(centred * centred, axis=-1, keepdims=True)
    inverse = lax.rsqrt(row_var + norm_epsilon)
    normed = centred * inverse
    return (normed * norm_gain + norm_shift, normed, inverse)


def norm_back(upstream, norm_gain, normed, inverse):
    scaled = upstream * norm_gain
    first_mean = jnp.mean(scaled, axis=-1, keepdims=True)
    second_mean = jnp.mean(scaled * normed, axis=-1, keepdims=True)
    return inverse * (scaled - first_mean - normed * second_mean)


def normal_cdf(values):
    return 0.5 * (1.0 + lax.erf(values * 0.7071067811865476))


def attend(operands):
    query_block, key_block, value_block = operands
    scores = (
        jnp.einsum("qhd,khd->hqk", query_block, key_block, preferred_element_type=jnp.float32)
        * 0.125
    )
    peak_score = jnp.max(scores, axis=-1, keepdims=True)
    exponent = jnp.exp(scores - peak_score)
    totals = jnp.sum(exponent, axis=-1, keepdims=True)
    probs_low = (exponent / totals).astype(jnp.bfloat16)
    attended = jnp.einsum(
        "hqk,khd->qhd", probs_low, value_block, preferred_element_type=jnp.float32
    )
    return (attended, peak_score + jnp.log(totals))


def attend_back(operands):
    query_block, key_block, value_block, log_total, grad_block = operands
    scores = (
        jnp.einsum("qhd,khd->hqk", query_block, key_block, preferred_element_type=jnp.float32)
        * 0.125
    )
    probs = jnp.exp(scores - log_total)
    grad_probs = jnp.einsum(
        "qhd,khd->hqk", grad_block, value_block, preferred_element_type=jnp.float32
    )
    delta = jnp.sum(probs * grad_probs, axis=-1, keepdims=True)
    grad_scores = (probs * (grad_probs - delta)).astype(jnp.bfloat16)
    grad_query = (
        jnp.einsum("hqk,khd->qhd", grad_scores, key_block, preferred_element_type=jnp.float32)
        * 0.125
    )
    grad_key = (
        jnp.einsum("hqk,qhd->khd", grad_scores, query_block, preferred_element_type=jnp.float32)
        * 0.125
    )
    grad_value = jnp.einsum(
        "hqk,qhd->khd", probs.astype(jnp.bfloat16), grad_block, preferred_element_type=jnp.float32
    )
    return (grad_query, grad_key, grad_value)


def adam_update(weight, gradient, first_old, second_old, step_rate, decay_rate):
    first_new = 0.5 * first_old + 0.5 * gradient
    second_new = 0.5 * second_old + 0.5 * gradient * gradient
    correction = 1.0 - 0.5**STEP
    update = (
        first_new / correction / (jnp.sqrt(second_new / correction) + adam_epsilon)
        + decay_rate * weight
    )
    return (first_new, second_new, weight - step_rate * update)


def per_device_split(
    x_tokens,
    out_grad,
    w_qkv,
    w_out,
    w_up,
    w_down,
    vectors,
    qkv_mean,
    qkv_square,
    out_mean,
    out_square,
    up_mean,
    up_square,
    down_mean,
    down_square,
    vectors_mean,
    vectors_square,
):
    masters = (w_qkv, w_out, w_up, w_down, vectors)
    lowered = tuple((member.astype(jnp.bfloat16) for member in masters))
    qkv_low, out_low, up_low, down_low, vector_low = (
        lax.all_gather(lowered[0], "ctx", axis=0, tiled=True),
        lax.all_gather(lowered[1], "ctx", axis=0, tiled=True),
        lax.all_gather(lowered[2], "ctx", axis=0, tiled=True),
        lax.all_gather(lowered[3], "ctx", axis=0, tiled=True),
        lax.all_gather(lowered[4], "ctx", axis=1, tiled=True),
    )
    vector_rows = vector_low.astype(jnp.float32)
    clip_count, row_count, model_width = x_tokens.shape
    head_count = model_width // HD
    token_total = clip_count * row_count
    flat_rows = x_tokens.reshape(token_total, model_width).astype(jnp.float32)
    norm_one, normed_one, inverse_one = normalize(flat_rows, vector_rows[0], vector_rows[1])
    norm_one_low = norm_one.astype(jnp.bfloat16)
    qkv_shift = jnp.concatenate([vector_rows[2], jnp.zeros_like(vector_rows[2]), vector_rows[3]])
    projected = (
        jnp.dot(norm_one_low, qkv_low, preferred_element_type=jnp.float32) + qkv_shift
    ).astype(jnp.bfloat16)
    query_rows = projected[:, :model_width].reshape(clip_count, row_count, head_count, HD)
    key_local = projected[:, model_width : 2 * model_width].reshape(
        clip_count, row_count, head_count, HD
    )
    value_local = projected[:, 2 * model_width :].reshape(clip_count, row_count, head_count, HD)
    key_rows, value_rows = (
        lax.all_gather(key_local, "ctx", axis=1, tiled=True),
        lax.all_gather(value_local, "ctx", axis=1, tiled=True),
    )
    attended, log_total = lax.map(attend, (query_rows, key_rows, value_rows))
    attended_low = attended.reshape(token_total, model_width).astype(jnp.bfloat16)
    branch = jnp.dot(attended_low, out_low, preferred_element_type=jnp.float32) + vector_rows[4]
    resid = flat_rows + branch
    norm_two, normed_two, inverse_two = normalize(resid, vector_rows[5], vector_rows[6])
    norm_two_low = norm_two.astype(jnp.bfloat16)
    pre_act = jnp.dot(norm_two_low, up_low, preferred_element_type=jnp.float32) + vector_rows[
        8:
    ].reshape(-1)
    act_low = (pre_act * normal_cdf(pre_act)).astype(jnp.bfloat16)
    mlp_out = jnp.dot(act_low, down_low, preferred_element_type=jnp.float32) + vector_rows[7]
    y_tokens = (resid + mlp_out).astype(jnp.bfloat16).reshape(clip_count, row_count, model_width)
    grad_output = out_grad.reshape(token_total, model_width)
    grad_float = grad_output.astype(jnp.float32)
    grad_down = jnp.einsum("tf,td->fd", act_low, grad_output, preferred_element_type=jnp.float32)
    down_shift = jnp.sum(grad_float, axis=0)
    grad_act = jnp.dot(grad_output, down_low.T, preferred_element_type=jnp.float32)
    density = jnp.exp(-0.5 * pre_act * pre_act) * 0.3989422804014327
    grad_pre = (grad_act * (normal_cdf(pre_act) + pre_act * density)).astype(jnp.bfloat16)
    grad_up = jnp.einsum("td,tf->df", norm_two_low, grad_pre, preferred_element_type=jnp.float32)
    up_shift = jnp.sum(grad_pre.astype(jnp.float32), axis=0)
    grad_norm_two = jnp.dot(grad_pre, up_low.T, preferred_element_type=jnp.float32)
    gain_two_grad = jnp.sum(grad_norm_two * normed_two, axis=0)
    shift_two_grad = jnp.sum(grad_norm_two, axis=0)
    grad_resid = grad_float + norm_back(grad_norm_two, vector_rows[5], normed_two, inverse_two)
    grad_branch = grad_resid.astype(jnp.bfloat16)
    grad_out = jnp.einsum(
        "td,te->de", attended_low, grad_branch, preferred_element_type=jnp.float32
    )
    out_shift = jnp.sum(grad_branch.astype(jnp.float32), axis=0)
    grad_attended = jnp.dot(grad_branch, out_low.T, preferred_element_type=jnp.float32).astype(
        jnp.bfloat16
    )
    grad_attended = grad_attended.reshape(clip_count, row_count, head_count, HD)
    grad_query, key_terms, value_terms = lax.map(
        attend_back, (query_rows, key_rows, value_rows, log_total, grad_attended)
    )
    grad_key, grad_value = (
        lax.psum_scatter(
            key_terms.astype(jnp.bfloat16), "ctx", scatter_dimension=1, tiled=True
        ).astype(jnp.float32),
        lax.psum_scatter(
            value_terms.astype(jnp.bfloat16), "ctx", scatter_dimension=1, tiled=True
        ).astype(jnp.float32),
    )
    grad_projected = jnp.concatenate(
        [
            grad_query.reshape(token_total, model_width),
            grad_key.reshape(token_total, model_width),
            grad_value.reshape(token_total, model_width),
        ],
        axis=1,
    ).astype(jnp.bfloat16)
    grad_qkv = jnp.einsum(
        "td,te->de", norm_one_low, grad_projected, preferred_element_type=jnp.float32
    )
    projected_sums = jnp.sum(grad_projected.astype(jnp.float32), axis=0)
    grad_norm_one = jnp.dot(grad_projected, qkv_low.T, preferred_element_type=jnp.float32)
    gain_one_grad = jnp.sum(grad_norm_one * normed_one, axis=0)
    shift_one_grad = jnp.sum(grad_norm_one, axis=0)
    x_grad = (
        grad_resid + norm_back(grad_norm_one, vector_rows[0], normed_one, inverse_one)
    ).astype(jnp.bfloat16)
    x_grad = x_grad.reshape(clip_count, row_count, model_width)
    first_rows = jnp.stack(
        [
            gain_one_grad,
            shift_one_grad,
            projected_sums[:model_width],
            projected_sums[2 * model_width :],
            out_shift,
            gain_two_grad,
            shift_two_grad,
            down_shift,
        ]
    )
    grad_vectors = jnp.concatenate([first_rows, up_shift.reshape(-1, model_width)], axis=0)
    group_size = lax.axis_size("ctx")
    vector_count = grad_vectors.shape[0]
    flat_vectors = (
        grad_vectors.reshape(vector_count, group_size, -1)
        .transpose(1, 0, 2)
        .reshape(group_size, -1)
    )
    shaped = (grad_qkv, grad_out, grad_up, grad_down, flat_vectors)
    spread = (
        lax.psum_scatter(
            shaped[0].astype(jnp.bfloat16), "dp", scatter_dimension=1, tiled=True
        ).astype(jnp.float32),
        lax.psum_scatter(
            shaped[1].astype(jnp.bfloat16), "dp", scatter_dimension=1, tiled=True
        ).astype(jnp.float32),
        lax.psum_scatter(
            shaped[2].astype(jnp.bfloat16), "dp", scatter_dimension=1, tiled=True
        ).astype(jnp.float32),
        lax.psum_scatter(
            shaped[3].astype(jnp.bfloat16), "dp", scatter_dimension=1, tiled=True
        ).astype(jnp.float32),
        lax.psum_scatter(
            shaped[4].astype(jnp.bfloat16), "dp", scatter_dimension=1, tiled=True
        ).astype(jnp.float32),
    )
    owned = (
        lax.psum_scatter(
            spread[0].astype(jnp.bfloat16), "ctx", scatter_dimension=0, tiled=True
        ).astype(jnp.float32),
        lax.psum_scatter(
            spread[1].astype(jnp.bfloat16), "ctx", scatter_dimension=0, tiled=True
        ).astype(jnp.float32),
        lax.psum_scatter(
            spread[2].astype(jnp.bfloat16), "ctx", scatter_dimension=0, tiled=True
        ).astype(jnp.float32),
        lax.psum_scatter(
            spread[3].astype(jnp.bfloat16), "ctx", scatter_dimension=0, tiled=True
        ).astype(jnp.float32),
        lax.psum_scatter(
            spread[4].astype(jnp.bfloat16), "ctx", scatter_dimension=0, tiled=True
        ).astype(jnp.float32),
    )
    collected = (
        lax.all_gather(owned[0].astype(jnp.bfloat16), "dp", axis=1, tiled=True).astype(jnp.float32),
        lax.all_gather(owned[1].astype(jnp.bfloat16), "dp", axis=1, tiled=True).astype(jnp.float32),
        lax.all_gather(owned[2].astype(jnp.bfloat16), "dp", axis=1, tiled=True).astype(jnp.float32),
        lax.all_gather(owned[3].astype(jnp.bfloat16), "dp", axis=1, tiled=True).astype(jnp.float32),
        lax.all_gather(owned[4].astype(jnp.bfloat16), "dp", axis=1, tiled=True).astype(jnp.float32),
    )
    shares = (
        collected[0],
        collected[1],
        collected[2],
        collected[3],
        collected[4].reshape(vector_count, -1),
    )
    qkv_moment, qkv_second, qkv_master = adam_update(
        w_qkv, shares[0], qkv_mean, qkv_square, matrix_rate, matrix_decay
    )
    out_moment, out_second, out_master = adam_update(
        w_out, shares[1], out_mean, out_square, matrix_rate, matrix_decay
    )
    up_moment, up_second, up_master = adam_update(
        w_up, shares[2], up_mean, up_square, matrix_rate, matrix_decay
    )
    down_moment, down_second, down_master = adam_update(
        w_down, shares[3], down_mean, down_square, matrix_rate, matrix_decay
    )
    vectors_moment, vectors_second, vectors_master = adam_update(
        vectors, shares[4], vectors_mean, vectors_square, vector_rate, 0.0
    )
    return (
        y_tokens,
        x_grad,
        qkv_moment,
        qkv_second,
        qkv_master,
        out_moment,
        out_second,
        out_master,
        up_moment,
        up_second,
        up_master,
        down_moment,
        down_second,
        down_master,
        vectors_moment,
        vectors_second,
        vectors_master,
    )


LOG2E = 1.4426950408889634
NT = (((1,), (1,)), ((), ()))
NN = (((1,), (0,)), ((), ()))
TN = (((0,), (0,)), ((), ()))
KERNEL_VMEM = 62 * 2**20


def attend_kernel(q_ref, k_ref, v_ref, o_ref, r_ref, p_ref, score_a, score_b):
    rows = score_a.shape[0]
    total = k_ref.shape[0]
    lane = lax.broadcasted_iota(jnp.int32, (1, 2 * HD), 1)
    held = (score_a, score_b)
    parts = total // rows
    items = [(head, part) for head in range(2) for part in range(parts)]

    def score(index):
        head, part = items[index]
        keys = jnp.where((lane // HD) == head, k_ref[...], 0).astype(jnp.bfloat16)
        held[index % 2][...] = lax.dot_general(
            q_ref[part * rows : (part + 1) * rows, :], keys, NT, preferred_element_type=jnp.float32
        )

    def soften(index):
        head, part = items[index]
        values = held[index % 2][...]
        peak = jnp.max(values, axis=1, keepdims=True)
        p_ref[head, part * rows : (part + 1) * rows, :] = jnp.exp2(
            (values - peak) * (0.125 * LOG2E)
        ).astype(jnp.bfloat16)

    def weigh(index):
        head, part = items[index]
        span = slice(part * rows, (part + 1) * rows)
        kept = jnp.where((lane // HD) == head, v_ref[...], 0).astype(jnp.bfloat16)
        table = jnp.concatenate([kept, jnp.ones((total, 2 * HD), jnp.bfloat16)], axis=1)
        out = lax.dot_general(p_ref[head, span, :], table, NN, preferred_element_type=jnp.float32)
        inverse = 1.0 / out[:, 2 * HD :]
        mixed = (out[:, : 2 * HD] * inverse).astype(jnp.bfloat16)
        if head == 0:
            o_ref[span, :] = mixed
            r_ref[span, :] = inverse
        else:
            o_ref[span, :] = jnp.where(lane < HD, o_ref[span, :], mixed)
            r_ref[span, :] = jnp.where(lane < HD, r_ref[span, :], inverse)

    score(0)
    for index in range(len(items)):
        if index + 1 < len(items):
            score(index + 1)
        soften(index)
        weigh(index)


def attend_back_kernel(
    q_ref, k_ref, v_ref, g_ref, o_ref, r_ref, p_ref, dq_ref, dk_ref, dv_ref, ds, qt, gt, dkt, dvt
):
    head = pl.program_id(1)
    total = k_ref.shape[0]
    half = total // 2
    lane = lax.broadcasted_iota(jnp.int32, (1, 2 * HD), 1)
    keep = (lane // HD) == head
    scaled = g_ref[...].astype(jnp.float32) * r_ref[...]

    @pl.when(head == 0)
    def _():
        qt[...] = q_ref[...].T
        gt[...] = scaled.astype(jnp.bfloat16).T

    delta = jnp.sum(jnp.where(keep, scaled * o_ref[...].astype(jnp.float32), 0.0), axis=1, keepdims=True)
    values = jnp.where(keep, v_ref[...], 0).astype(jnp.bfloat16)
    grad_probs = lax.dot_general(
        scaled.astype(jnp.bfloat16), values, NT, preferred_element_type=jnp.float32
    )
    ds[...] = (p_ref[...].astype(jnp.float32) * (grad_probs - delta)).astype(jnp.bfloat16)
    span = pl.ds(pl.multiple_of(head * HD, HD), HD)
    dvt[span, :] = lax.dot_general(gt[span, :], p_ref[...], NN, preferred_element_type=jnp.float32)
    dkt[span, :] = 0.125 * lax.dot_general(
        qt[span, :], ds[...], NN, preferred_element_type=jnp.float32
    )
    keys = jnp.where(keep, k_ref[...], 0).astype(jnp.bfloat16)
    for part in range(2):
        rows = slice(part * half, (part + 1) * half)
        term = 0.125 * lax.dot_general(ds[rows, :], keys, NN, preferred_element_type=jnp.float32)
        dq_ref[rows, :] = jnp.where(keep, term.astype(jnp.bfloat16), dq_ref[rows, :])

    @pl.when(head == 1)
    def _():
        dk_ref[...] = dkt[...].T.astype(jnp.bfloat16)
        dv_ref[...] = dvt[...].T.astype(jnp.bfloat16)


MESH = pl.DeviceIdType.MESH
GATHER_ORDERS = ("xab", "axb", "abx")
LATE_ORDERS = ("xaby", "yaxb", "xaby", "yxab")
FIRST_ORDERS = ("abxy", "xaby", "yabx")


def own_bits():
    place = lax.axis_index("dp")
    z = place // 4
    return {
        "core": place % 2,
        "x": (place // 2) % 2,
        "a": (z % 2 + z // 2) % 2,
        "b": z // 2,
        "y": lax.axis_index("ctx"),
    }


def partner(name):
    place, group = lax.axis_index("dp"), lax.axis_index("ctx")
    z = place // 4
    if name == "core":
        return (place + 1 - 2 * (place % 2), group)
    if name == "x":
        return (place + 2 - 4 * ((place // 2) % 2), group)
    if name == "a":
        return (place + 4 - 8 * (z % 2), group)
    if name == "b":
        return (place + 4 * (3 - 2 * z), group)
    return (place, 1 - group)


def meet_partners():
    barrier = pltpu.get_barrier_semaphore()
    names = ("core", "x", "a", "b", "y")
    for name in names:
        pl.semaphore_signal(barrier, inc=1, device_id=partner(name), device_id_type=MESH)
    pl.semaphore_wait(barrier, len(names))


def remote(source, target, name, send_sem, recv_sem):
    return pltpu.make_async_remote_copy(
        src_ref=source,
        dst_ref=target,
        send_sem=send_sem,
        recv_sem=recv_sem,
        device_id=partner(name),
        device_id_type=MESH,
    )


def local_copy(source, target, sem):
    return pltpu.make_async_copy(source, target, sem)


def block_of(order, bits):
    first, second, third = (bits[name] for name in order if name != "y")
    return first * 4 + second * 2 + third


class Gather:
    stages = 4

    def __init__(self, buffer, orders, send, recv):
        self.buffer, self.orders, self.send, self.recv = buffer, orders, send, recv

    def copy(self, stage, stream):
        bits = own_bits()
        order = self.orders[stream].replace("y", "")
        block = block_of(order, bits)
        size = (1, 2, 4, 8)[stage]
        name = "core" if stage == 3 else order[2 - stage]
        region = self.buffer.at[bits["core"], stream, pl.ds(block // size * size, size)]
        return remote(region, region, name, self.send.at[stage, stream], self.recv.at[stage, stream])

    def start(self, stage, stream):
        self.copy(stage, stream).start()

    def advance(self, stage, stream):
        self.copy(stage, stream).wait()
        if stage + 1 < self.stages:
            self.copy(stage + 1, stream).start()

    def begin(self):
        for stream in range(len(self.orders)):
            self.start(0, stream)

    def advance_all(self, stage):
        for stream in range(len(self.orders)):
            self.advance(stage, stream)


class StreamSum:
    def __init__(self, order, total, landing, send, recv):
        self.order, self.total, self.landing = order, total, landing
        self.send, self.recv = send, recv

    def region(self, stage):
        bits = own_bits()
        done = self.order[: stage - 1]
        start, size = 0, 8
        for name in done:
            if name != "y":
                size //= 2
                start = start + bits[name] * size
        return start, size, "y" in done

    def views(self, stage):
        bits = own_bits()
        start, size, settled = self.region(stage)
        name = self.order[stage - 1]
        if name == "y":
            span = pl.ds(start, size)
            return self.total.at[span, 1 - bits["y"]], (start, size, True)
        size //= 2
        sent = pl.ds(start + (1 - bits[name]) * size, size)
        kept = start + bits[name] * size
        if settled:
            return self.total.at[sent, bits["y"]], (kept, size, True)
        return self.total.at[sent], (kept, size, False)

    def copy(self, stage):
        source, _ = self.views(stage)
        name = self.order[stage - 1]
        return remote(source, self.landing[stage], name, self.send.at[stage], self.recv.at[stage])

    def start(self, stage):
        self.copy(stage).start()

    def add(self, stage):
        _, (start, size, settled) = self.views(stage)
        bits = own_bits()
        landed = self.landing[stage]

        @pl.loop(0, size)
        def _(block):
            at = (start + block, bits["y"]) if settled else (start + block,)
            self.total[at] = (
                self.total[at].astype(jnp.float32) + landed[block].astype(jnp.float32)
            ).astype(jnp.bfloat16)

    def finish(self, stage):
        self.copy(stage).wait()
        self.add(stage)

    def advance(self, stage):
        self.finish(stage)
        if stage < 4:
            self.start(stage + 1)

    def own_block(self):
        bits = own_bits()
        return self.total.at[block_of(self.order, bits), bits["y"]]


def landing_shapes(order, stages, rows, columns):
    shapes = []
    for stage in stages:
        if stage == 0:
            lead = (8, 2)
        else:
            done = order[:stage]
            blocks = 8
            for name in done:
                if name != "y":
                    blocks //= 2
            lead = (blocks,) if "y" in done else (blocks, 2)
        shapes.append(pltpu.VMEM(lead + (rows, columns), jnp.bfloat16))
    return shapes


def gather_sems(streams):
    return [pltpu.SemaphoreType.DMA((4, streams)), pltpu.SemaphoreType.DMA((4, streams))]


def start_kernel(
    x_ref, w_ref, vec_ref, x2_ref, proj_ref, wqkv_ref, wout_ref, vecs_ref,
    norm, other, vec_other, g_send, g_recv, w_send, w_recv, x_send, x_recv, v_sem, l_sem,
):
    bits = own_bits()
    me = bits["y"]
    half, width = x_ref.shape[1], x_ref.shape[2]
    gather = Gather(other, GATHER_ORDERS, g_send, g_recv)
    meet_partners()
    vec_copy = remote(vec_ref, vec_other, "y", v_sem.at[0], v_sem.at[1])
    vec_copy.start()
    own_x = local_copy(x_ref.at[me], x2_ref.at[pl.ds(0, half)], l_sem)
    own_x.start()
    pieces = []
    for stream in range(3):
        block = block_of(GATHER_ORDERS[stream], bits)
        piece = remote(
            w_ref.at[bits["core"], stream, block],
            other.at[bits["core"], stream, block],
            "y",
            w_send.at[stream],
            w_recv.at[stream],
        )
        piece.start()
        pieces.append(piece)
    first = half // 32 * 16 + 16
    spans = [(0, first), (first, half - first)]
    trades = [
        remote(
            x_ref.at[1 - me, pl.ds(at, size)],
            x2_ref.at[pl.ds(half + at, size)],
            "y",
            x_send.at[index],
            x_recv.at[index],
        )
        for index, (at, size) in enumerate(spans)
    ]
    for piece in pieces:
        piece.wait()
    gather.begin()
    trades[0].start()
    vec_copy.wait()
    mine, others = vec_ref[...], vec_other[...]
    vecs_ref[...] = jnp.where(
        me == 0,
        jnp.concatenate([mine, others], axis=1),
        jnp.concatenate([others, mine], axis=1),
    )
    for c in range(4):
        half_at = slice(c % 2 * (width // 2), (c % 2 + 1) * (width // 2))
        vecs_ref[12 + c : 13 + c, :] = jnp.concatenate(
            [vecs_ref[8 + c // 2 : 9 + c // 2, half_at], vecs_ref[10 + c // 2 : 11 + c // 2, half_at]],
            axis=1,
        )
    gather.advance_all(0)
    trades[1].start()

    def norm_rows(at, size):
        values = x2_ref[at : at + size, :].astype(jnp.float32)
        normed, _, _ = normalize(values, vecs_ref[0:1, :], vecs_ref[1:2, :])
        norm[at : at + size, :] = normed.astype(jnp.bfloat16)

    own_x.wait()
    norm_rows(0, half)
    for stage in range(1, 4):
        gather.advance_all(stage)
    part = width // 2

    for source, at in ((w_ref, me * part), (other, (1 - me) * part)):
        for matrix in range(4):
            for index in range(12):
                flat = matrix * 12 + index
                block = source[flat // 24, flat // 8 % 3, flat % 8]
                rows = pl.ds(pl.multiple_of(at + index * 32, 32), 32)
                if matrix < 3:
                    wqkv_ref[rows, matrix * width : (matrix + 1) * width] = block
                else:
                    wout_ref[rows, :] = block

    def project(at, size):
        @pl.loop(0, 3)
        def _(matrix):
            cols = pl.ds(pl.multiple_of(matrix * width, 128), width)
            shift = jnp.where(matrix == 0, vecs_ref[2:3, :], vecs_ref[3:4, :])
            shift = jnp.where(matrix == 1, 0.0, shift)
            proj_ref[at : at + size, cols] = (
                lax.dot_general(
                    norm[at : at + size, :], wqkv_ref[:, cols], NN, preferred_element_type=jnp.float32
                )
                + shift
            ).astype(jnp.bfloat16)

    project(0, half)
    for trade, (at, size) in zip(trades, spans):
        trade.wait()
        norm_rows(half + at, size)
        project(half + at, size)


def start_call(x_tokens, weights, vector_own):
    _, half, width = x_tokens.shape
    low = jnp.bfloat16
    anywhere = pl.BlockSpec(memory_space=pl.ANY)
    vmem = pl.BlockSpec(memory_space=pltpu.VMEM)
    dma = pltpu.SemaphoreType.DMA
    return pl.pallas_call(
        start_kernel,
        in_specs=[anywhere, vmem, vmem],
        out_specs=[vmem] * 5,
        out_shape=[
            jax.ShapeDtypeStruct((2 * half, width), low),
            jax.ShapeDtypeStruct((2 * half, 3 * width), low),
            jax.ShapeDtypeStruct((width, 3 * width), low),
            jax.ShapeDtypeStruct((width, width), low),
            jax.ShapeDtypeStruct((16, width), jnp.float32),
        ],
        scratch_shapes=[
            pltpu.VMEM((2 * half, width), low),
            pltpu.VMEM(weights.shape, low),
            pltpu.VMEM(vector_own.shape, jnp.float32),
        ]
        + gather_sems(3)
        + [dma((3,)), dma((3,)), dma((2,)), dma((2,)), dma((2,)), dma],
        compiler_params=pltpu.CompilerParams(
            vmem_limit_bytes=KERNEL_VMEM, collective_id=1, has_side_effects=True
        ),
        name="start",
    )(x_tokens, weights, vector_own)


def attend_gather_kernel(
    q_ref, k_ref, v_ref, w_ref, grad_ref, o_ref, r_ref, p_ref, other_ref, grad2_ref,
    score_a, score_b, g_send, g_recv, w_send, w_recv, t_send, t_recv, l_sem,
):
    step = pl.program_id(0)
    last = pl.num_programs(0) - 1
    bits = own_bits()
    me = bits["y"]
    half = grad_ref.shape[1]
    gather = Gather(other_ref, GATHER_ORDERS, g_send, g_recv)

    def piece(stream):
        block = block_of(GATHER_ORDERS[stream], bits)
        return remote(
            w_ref.at[bits["core"], stream, block],
            other_ref.at[bits["core"], stream, block],
            "y",
            w_send.at[stream],
            w_recv.at[stream],
        )

    trade = remote(
        grad_ref.at[1 - me], grad2_ref.at[pl.ds(half, half)], "y", t_send, t_recv
    )
    own = local_copy(grad_ref.at[me], grad2_ref.at[pl.ds(0, half)], l_sem)

    @pl.when(step == 0)
    def _():
        meet_partners()
        for stream in range(3):
            piece(stream).start()
        own.start()

    @pl.when(step == 1)
    def _():
        for stream in range(3):
            piece(stream).wait()
        gather.begin()
        trade.start()

    for stage in range(3):
        @pl.when(step == 2 + stage)
        def _(stage=stage):
            gather.advance_all(stage)

    attend_kernel(q_ref, k_ref, v_ref, o_ref, r_ref, p_ref, score_a, score_b)

    @pl.when(step == last)
    def _():
        gather.advance_all(3)
        trade.wait()
        own.wait()


def attend_call(projected, weights, out_grad, width):
    total = projected.shape[0]
    pairs = width // (2 * HD)
    half = out_grad.shape[1]
    anywhere = pl.BlockSpec(memory_space=pl.ANY)
    dma = pltpu.SemaphoreType.DMA

    def columns(start):
        return pl.BlockSpec((total, 2 * HD), lambda p: (0, start * pairs + p))

    return pl.pallas_call(
        attend_gather_kernel,
        grid=(pairs,),
        in_specs=[columns(0), columns(1), columns(2), anywhere, anywhere],
        out_specs=[
            columns(0),
            columns(0),
            pl.BlockSpec((2, total, total), lambda p: (p, 0, 0)),
            anywhere,
            anywhere,
        ],
        out_shape=[
            jax.ShapeDtypeStruct((total, width), jnp.bfloat16),
            jax.ShapeDtypeStruct((total, width), jnp.float32),
            jax.ShapeDtypeStruct((2 * pairs, total, total), jnp.bfloat16),
            jax.ShapeDtypeStruct(weights.shape, jnp.bfloat16),
            jax.ShapeDtypeStruct((2 * half, width), jnp.bfloat16),
        ],
        scratch_shapes=[pltpu.VMEM((total // 2, total), jnp.float32)] * 2
        + gather_sems(3)
        + [dma((3,)), dma((3,)), dma, dma, dma],
        compiler_params=pltpu.CompilerParams(
            vmem_limit_bytes=KERNEL_VMEM, collective_id=2, has_side_effects=True
        ),
        cost_estimate=pl.CostEstimate(
            flops=16 * pairs * total * total * 2 * HD,
            bytes_accessed=4 * pairs * total * total,
            transcendentals=2 * pairs * total * total,
        ),
        name="attend",
    )(projected, projected, projected, weights, out_grad)


def attend_back_sum_kernel(
    q_ref, k_ref, v_ref, g_ref, o_ref, r_ref, p_ref, partial_ref, y2_ref,
    dq_ref, dk_ref, dv_ref, shared_ref, tokens_ref,
    ds, qt, gt, dkt, dvt, total, *rest,
):
    landing, rest = rest[:-8], rest[-8:]
    s_send, s_recv, g_send, g_recv, p_sem, t_send, t_recv, l_sem = rest
    step = pl.program_id(0) * 2 + pl.program_id(1)
    last = pl.num_programs(0) * 2 - 1
    bits = own_bits()
    me = bits["y"]
    half = tokens_ref.shape[1]
    streams, held = [], list(landing)
    for index, order in enumerate(LATE_ORDERS):
        buffers = {stage: held.pop(0) for stage in LATE_STAGES[index]}
        streams.append(
            StreamSum(order, total.at[index], buffers, s_send.at[index], s_recv.at[index])
        )
    gather = Gather(shared_ref, LATE_ORDERS, g_send, g_recv)
    trade = remote(y2_ref.at[pl.ds(half, half)], tokens_ref.at[me], "y", t_send, t_recv)
    own = local_copy(y2_ref.at[pl.ds(0, half)], tokens_ref.at[me], l_sem.at[0])
    load = local_copy(partial_ref, total, l_sem.at[1])

    def place(index):
        copy = local_copy(
            streams[index].own_block(),
            shared_ref.at[bits["core"], index, block_of(LATE_ORDERS[index], bits)],
            p_sem.at[index],
        )
        copy.start()
        copy.wait()

    def move(index, stage):
        if stage < 4:
            streams[index].advance(stage)
        elif stage == 4:
            streams[index].finish(4)
            place(index)
            gather.start(0, index)
        else:
            gather.advance(stage - 5, index)

    @pl.when(step == 0)
    def _():
        meet_partners()
        load.start()
        own.start()
        load.wait()
        for index in range(len(LATE_ORDERS)):
            streams[index].start(LATE_STAGES[index][0])

    for at, moves in enumerate(BACK_MOVES):
        @pl.when(step == at)
        def _(at=at, moves=moves):
            for index, stage in moves:
                move(index, stage)
            if at == 2:
                trade.start()

    attend_back_kernel(
        q_ref, k_ref, v_ref, g_ref, o_ref, r_ref, p_ref, dq_ref, dk_ref, dv_ref, ds, qt, gt, dkt, dvt
    )

    @pl.when(step == last)
    def _():
        move(3, 8)
        trade.wait()
        own.wait()


LATE_STAGES = ((4,), (3, 4), (2, 3, 4), (1, 2, 3, 4))
BACK_MOVES = (
    (),
    ((0, 4), (2, 2)),
    ((1, 3), (0, 5)),
    ((3, 1), (2, 3), (1, 4)),
    ((0, 6), (2, 4), (1, 5), (3, 2)),
    ((1, 6), (2, 5), (3, 3)),
    ((0, 7), (2, 6), (3, 4)),
    ((1, 7), (3, 5)),
    ((0, 8), (2, 7), (3, 6)),
    ((1, 8),),
    ((2, 8), (3, 7)),
    (),
)


def attend_back_call(projected, upstream, attended, inverse, exponent, partial, y2):
    total, width = attended.shape
    pairs = width // (2 * HD)
    streams, _, _, rows, _ = partial.shape
    anywhere = pl.BlockSpec(memory_space=pl.ANY)
    dma = pltpu.SemaphoreType.DMA

    def columns(start):
        return pl.BlockSpec((total, 2 * HD), lambda p, h: (0, start * pairs + p))

    landing = []
    for order, stages in zip(LATE_ORDERS, LATE_STAGES):
        landing += landing_shapes(order, stages, rows, width)
    return pl.pallas_call(
        attend_back_sum_kernel,
        grid=(pairs, 2),
        in_specs=[columns(0), columns(1), columns(2), columns(0), columns(0), columns(0)]
        + [pl.BlockSpec((None, total, total), lambda p, h: (p * 2 + h, 0, 0))]
        + [anywhere, anywhere],
        out_specs=[columns(0)] * 3 + [anywhere, anywhere],
        out_shape=[jax.ShapeDtypeStruct((total, width), jnp.bfloat16)] * 3
        + [
            jax.ShapeDtypeStruct((2, streams, 8, rows, width), jnp.bfloat16),
            jax.ShapeDtypeStruct((2, total // 2, width), jnp.bfloat16),
        ],
        scratch_shapes=[pltpu.VMEM((total, total), jnp.bfloat16)]
        + [pltpu.VMEM((2 * HD, total), jnp.bfloat16)] * 2
        + [pltpu.VMEM((2 * HD, total), jnp.float32)] * 2
        + [pltpu.VMEM(partial.shape, jnp.bfloat16)]
        + landing
        + [dma((streams, 5)), dma((streams, 5))]
        + gather_sems(streams)
        + [dma((streams,)), dma, dma, dma((2,))],
        compiler_params=pltpu.CompilerParams(
            vmem_limit_bytes=KERNEL_VMEM, collective_id=3, has_side_effects=True
        ),
        cost_estimate=pl.CostEstimate(
            flops=32 * pairs * total * total * 2 * HD,
            bytes_accessed=4 * pairs * total * total,
            transcendentals=0,
        ),
        name="attend_back",
    )(projected, projected, projected, upstream, attended, inverse, exponent, partial, y2)


LAST_MOVES = (
    ((0, 0), (1, 0), (2, 0)),
    ((0, 1), (1, 1), (2, 1)),
    ((0, 2), (1, 2), (0, 3), (2, 2), (1, 3)),
    ((0, 4), (1, 4), (0, 5), (2, 3)),
    ((2, 4), (1, 5), (2, 5), (0, 6)),
    ((1, 6), (2, 6)),
    ((1, 7), (0, 7), (1, 8), (0, 8), (2, 7), (2, 8)),
)


def finish_kernel(
    dq_ref, dk_ref, dv_ref, x_ref, w_ref, vec_ref, resid_ref, out_ref, part_ref,
    xg_ref, shared_ref, vsum_ref,
    grads, turned, sent_rows, own_rows, total, *rest,
):
    landing, rest = rest[:-11], rest[-11:]
    s_send, s_recv, g_send, g_recv, p_sem, t_send, t_recv, l_sem, v_land, v_send, v_recv = rest
    bits = own_bits()
    me = bits["y"]
    rows, width = x_ref.shape
    half = rows // 2
    streams, held = [], list(landing)
    for index, order in enumerate(FIRST_ORDERS):
        buffers = {stage: held.pop(0) for stage in range(5)}
        streams.append(
            StreamSum(order, total.at[index], buffers, s_send.at[index], s_recv.at[index])
        )
    gather = Gather(shared_ref, FIRST_ORDERS, g_send, g_recv)
    gain, shift = vec_ref[0:1, :], vec_ref[1:2, :]
    meet_partners()

    def core_copy(index):
        return remote(
            grads.at[1 - bits["core"], index],
            streams[index].landing[0],
            "core",
            s_send.at[index, 0],
            s_recv.at[index, 0],
        )

    def move(index, stage):
        if stage == 0:
            core_copy(index).wait()

            @pl.loop(0, 8)
            def _(block):
                total[index, block] = (
                    grads[bits["core"], index, block].astype(jnp.float32)
                    + streams[index].landing[0][block].astype(jnp.float32)
                ).astype(jnp.bfloat16)

            streams[index].start(1)
        elif stage < 4:
            streams[index].advance(stage)
        elif stage == 4:
            streams[index].finish(4)
            copy = local_copy(
                streams[index].own_block(),
                shared_ref.at[bits["core"], index, block_of(FIRST_ORDERS[index], bits)],
                p_sem.at[index],
            )
            copy.start()
            copy.wait()
            gather.start(0, index)
        else:
            gather.advance(stage - 5, index)

    def put(matrix, values):
        for side in range(2):
            for index in range(12):
                flat = matrix * 12 + index
                at = side * (width // 2) + index * 32
                grads[flat // 24, flat // 8 % 3, flat % 8, side] = values[at : at + 32, :]

    put(3, out_ref[...])
    norm_one, _, _ = normalize(x_ref[...].astype(jnp.float32), gain, shift)
    turned[...] = norm_one.astype(jnp.bfloat16).T
    for matrix, part in enumerate((dq_ref, dk_ref, dv_ref)):
        put(
            matrix,
            lax.dot_general(turned[...], part[...], NN, preferred_element_type=jnp.float32).astype(
                jnp.bfloat16
            ),
        )
    for index in range(3):
        core_copy(index).start()

    def input_rows(at, target):
        span = slice(at, at + half)
        upstream = None
        for matrix, part in enumerate((dq_ref, dk_ref, dv_ref)):
            term = lax.dot_general(
                part[span, :],
                w_ref[:, matrix * width : (matrix + 1) * width],
                NT,
                preferred_element_type=jnp.float32,
            )
            upstream = term if upstream is None else upstream + term
        _, normed, inverse = normalize(x_ref[span, :].astype(jnp.float32), gain, shift)
        target[...] = (resid_ref[span, :] + norm_back(upstream, gain, normed, inverse)).astype(
            jnp.bfloat16
        )
        return (
            jnp.sum(upstream * normed, axis=0, keepdims=True),
            jnp.sum(upstream, axis=0, keepdims=True),
        )

    other_sums = input_rows(half, sent_rows)
    trade = remote(sent_rows, xg_ref.at[me], "y", t_send, t_recv)
    trade.start()
    for index, stage in LAST_MOVES[0]:
        move(index, stage)
    own_sums = input_rows(0, own_rows)
    own = local_copy(own_rows, xg_ref.at[me], l_sem)
    own.start()
    vsum_ref[...] = part_ref[...]
    vsum_ref[0:1, :] = own_sums[0] + other_sums[0]
    vsum_ref[1:2, :] = own_sums[1] + other_sums[1]
    vsum_ref[2:3, :] = jnp.sum(dq_ref[...].astype(jnp.float32), axis=0, keepdims=True)
    vsum_ref[3:4, :] = jnp.sum(dv_ref[...].astype(jnp.float32), axis=0, keepdims=True)

    def vector_step(stage):
        name = ("core", "x", "a", "b", "y")[stage]
        return remote(vsum_ref, v_land.at[stage], name, v_send.at[stage], v_recv.at[stage])

    vector_step(0).start()
    for turn in range(1, 7):
        for index, stage in LAST_MOVES[turn]:
            move(index, stage)
        if turn <= 5:
            vector_step(turn - 1).wait()
            vsum_ref[...] += v_land[turn - 1]
            if turn < 5:
                vector_step(turn).start()
    trade.wait()
    own.wait()


def finish_call(grad_parts, x2, wqkv, vecs, grad_resid, grad_out, part_sums):
    total, width = x2.shape
    low = jnp.bfloat16
    anywhere = pl.BlockSpec(memory_space=pl.ANY)
    vmem = pl.BlockSpec(memory_space=pltpu.VMEM)
    dma = pltpu.SemaphoreType.DMA
    rows = width // 24
    landing = []
    for order in FIRST_ORDERS:
        landing += landing_shapes(order, range(5), rows, width)
    return pl.pallas_call(
        finish_kernel,
        in_specs=[vmem] * 9,
        out_specs=[anywhere, anywhere, vmem],
        out_shape=[
            jax.ShapeDtypeStruct((2, total // 2, width), low),
            jax.ShapeDtypeStruct((2, 3, 8, rows, width), low),
            jax.ShapeDtypeStruct((16, width), jnp.float32),
        ],
        scratch_shapes=[
            pltpu.VMEM((2, 3, 8, 2, rows, width), low),
            pltpu.VMEM((width, total), low),
            pltpu.VMEM((total // 2, width), low),
            pltpu.VMEM((total // 2, width), low),
            pltpu.VMEM((3, 8, 2, rows, width), low),
        ]
        + landing
        + [dma((3, 5)), dma((3, 5))]
        + gather_sems(3)
        + [dma((3,)), dma, dma, dma, pltpu.VMEM((5, 16, width), jnp.float32), dma((5,)), dma((5,))],
        compiler_params=pltpu.CompilerParams(
            vmem_limit_bytes=KERNEL_VMEM, collective_id=4, has_side_effects=True
        ),
        name="finish",
    )(*grad_parts, x2, wqkv, vecs, grad_resid, grad_out, part_sums)


def middle_kernel(
    att_ref, x_ref, g_ref, vec_ref, wo_ref, mine_ref, other_ref,
    y_ref, gr_ref, ga_ref, partial_ref, go_ref, sums_ref,
    up_w, down_w, mlp, upstream, acts, grads_pre, grads, total, *rest,
):
    landing, rest = rest[:-5], rest[-5:]
    s_send, s_recv, w_sem, x_sem, o_sem = rest
    bits = own_bits()
    me, core = bits["y"], bits["core"]
    rows, width = g_ref.shape
    half = rows // 2
    side = width // 2
    chunks = total.shape[0]
    piece = total.shape[3]
    resid, low_rows = gr_ref, ga_ref
    streams, held = [], list(landing[2:])
    for index, order in enumerate(LATE_ORDERS):
        buffers = {stage: held.pop(0) for stage in MIDDLE_STAGES[index]}
        buffers[0] = landing[index % 2]
        streams.append(
            StreamSum(order, total.at[index], buffers, s_send.at[index], s_recv.at[index])
        )

    def core_copy(index):
        return remote(
            grads.at[1 - core], landing[index % 2], "core", s_send.at[index, 0], s_recv.at[index, 0]
        )

    def end_core(index, start_next=True):
        core_copy(index).wait()

        @pl.loop(0, 8)
        def _(block):
            total[index, block] = (
                grads[core, block].astype(jnp.float32)
                + landing[index % 2][block].astype(jnp.float32)
            ).astype(jnp.bfloat16)

        if start_next:
            streams[index].start(1)

    own_x = local_copy(x_ref, y_ref, x_sem)
    own_x.start()
    loads = []
    for index, (source, at) in enumerate(((mine_ref, me), (other_ref, 1 - me))):
        for c in range(chunks):
            part = pl.ds(pl.multiple_of(c * width + at * side, 16), side)
            loads.append(
                local_copy(source.at[pl.ds(c * side, side)], down_w.at[part], w_sem.at[index, c])
            )
            part = pl.ds(pl.multiple_of(at * side, 16), side)
            loads.append(
                local_copy(
                    source.at[pl.ds((chunks + c) * side, side)],
                    up_w.at[part, pl.ds(c * width, width)],
                    w_sem.at[index, chunks + c],
                )
            )
    for load in loads:
        load.start()
    meet_partners()
    own_x.wait()
    gain = vec_ref[5:6, :]
    step = rows // 7

    resid[...] = lax.dot_general(att_ref[...], wo_ref[...], NN, preferred_element_type=jnp.float32)

    @pl.loop(0, 7)
    def _(index):
        span = pl.ds(pl.multiple_of(index * step, 16), step)
        resid[span, :] = y_ref[span, :].astype(jnp.float32) + (resid[span, :] + vec_ref[4:5, :])
        normed_two, _, _ = normalize(resid[span, :], gain, vec_ref[6:7, :])
        low_rows[span, :] = normed_two.astype(jnp.bfloat16)

    for load in loads:
        load.wait()
    sums_ref[...] = jnp.zeros_like(sums_ref)
    mlp[...] = jnp.zeros_like(mlp)
    upstream[...] = jnp.zeros_like(upstream)

    def column_sum(values):
        return jnp.sum(values, axis=0, keepdims=True)

    @pl.loop(0, chunks)
    def _(c):
        cols = pl.ds(pl.multiple_of(c * width, 128), width)
        shift = vec_ref[pl.ds(12 + c, 1), :]
        for part in range(2):
            span = slice(part * half, (part + 1) * half)
            pre = (
                lax.dot_general(
                    low_rows[span, :], up_w[:, cols], NN, preferred_element_type=jnp.float32
                )
                + shift
            )
            below = normal_cdf(pre)
            acts[span, :] = (pre * below).astype(jnp.bfloat16)
            density = jnp.exp(-0.5 * pre * pre) * 0.3989422804014327
            grad_act = lax.dot_general(
                g_ref[span, :], down_w[cols, :], NT, preferred_element_type=jnp.float32
            )
            grad_pre = (grad_act * (below + pre * density)).astype(jnp.bfloat16)
            grads_pre[span, :] = grad_pre
            sums_ref[pl.ds(12 + c, 1), :] += column_sum(grad_pre.astype(jnp.float32))
            mlp[span, :] += lax.dot_general(
                acts[span, :], down_w[cols, :], NN, preferred_element_type=jnp.float32
            )
            upstream[span, :] += lax.dot_general(
                grads_pre[span, :], up_w[:, cols], NT, preferred_element_type=jnp.float32
            )

        @pl.when(c == 1)
        def _():
            end_core(0)

        @pl.when(c == 2)
        def _():
            streams[0].advance(1)
            end_core(1)

        @pl.when(c == 3)
        def _():
            streams[0].advance(2)
            streams[1].advance(1)
            end_core(2)

        def put(which, values):
            for part in range(2):
                for block in range(8):
                    at = part * side + block * piece
                    grads[which, block, part] = values[at : at + piece, :].astype(jnp.bfloat16)

        put(0, lax.dot_general(acts[...], g_ref[...], TN, preferred_element_type=jnp.float32))
        put(
            1, lax.dot_general(low_rows[...], grads_pre[...], TN, preferred_element_type=jnp.float32)
        )
        for index in range(len(LATE_ORDERS)):
            @pl.when(c == index)
            def _(index=index):
                core_copy(index).start()

    for c in range(chunks):
        at = slice(c % 2 * side, (c % 2 + 1) * side)
        sums_ref[8 + c // 2 : 9 + c // 2, at] = sums_ref[12 + c : 13 + c, :side]
        sums_ref[10 + c // 2 : 11 + c // 2, at] = sums_ref[12 + c : 13 + c, side:]

    @pl.loop(0, 7)
    def _(index):
        span = pl.ds(pl.multiple_of(index * step, 16), step)
        y_ref[span, :] = (resid[span, :] + mlp[span, :] + vec_ref[7:8, :]).astype(jnp.bfloat16)
        _, normed, inverse = normalize(resid[span, :], gain, vec_ref[6:7, :])
        coming = upstream[span, :]
        grads_out = g_ref[span, :].astype(jnp.float32)
        sums_ref[5:6, :] += column_sum(coming * normed)
        sums_ref[6:7, :] += column_sum(coming)
        sums_ref[7:8, :] += column_sum(grads_out)
        grad_resid = grads_out + norm_back(coming, gain, normed, inverse)
        gr_ref[span, :] = grad_resid
        acts[span, :] = grad_resid.astype(jnp.bfloat16)
        sums_ref[4:5, :] += column_sum(acts[span, :].astype(jnp.float32))

    end_core(3, start_next=False)
    ga_ref[...] = lax.dot_general(
        acts[...], wo_ref[...], NT, preferred_element_type=jnp.float32
    ).astype(jnp.bfloat16)
    go_ref[...] = lax.dot_general(
        att_ref[...], acts[...], TN, preferred_element_type=jnp.float32
    ).astype(jnp.bfloat16)
    streams[0].finish(3)
    streams[1].finish(2)
    streams[2].finish(1)
    store = local_copy(total, partial_ref, o_sem)
    store.start()
    store.wait()


MIDDLE_STAGES = ((1, 2, 3), (1, 2), (1,), ())


def middle_call(attended, x_rows, grad_rows, vecs, out_low, mine, other):
    rows, width = x_rows.shape
    hidden = mine.shape[0]
    low = jnp.bfloat16
    anywhere = pl.BlockSpec(memory_space=pl.ANY)
    vmem = pl.BlockSpec(memory_space=pltpu.VMEM)
    dma = pltpu.SemaphoreType.DMA
    chunks = len(LATE_ORDERS)
    piece = hidden // (2 * chunks * 8)
    landing = landing_shapes(LATE_ORDERS[0], (0,), piece, width) * 2
    for order, stages in zip(LATE_ORDERS, MIDDLE_STAGES):
        landing += landing_shapes(order, stages, piece, width)
    return pl.pallas_call(
        middle_kernel,
        in_specs=[vmem, anywhere, vmem, vmem, vmem, anywhere, anywhere],
        out_specs=[vmem] * 3 + [anywhere] + [vmem] * 2,
        out_shape=[
            jax.ShapeDtypeStruct((rows, width), low),
            jax.ShapeDtypeStruct((rows, width), jnp.float32),
            jax.ShapeDtypeStruct((rows, width), low),
            jax.ShapeDtypeStruct((chunks, 8, 2, piece, width), low),
            jax.ShapeDtypeStruct((width, width), low),
            jax.ShapeDtypeStruct((16, width), jnp.float32),
        ],
        scratch_shapes=[
            pltpu.VMEM((width, hidden), low),
            pltpu.VMEM((hidden, width), low),
            pltpu.VMEM((rows, width), jnp.float32),
            pltpu.VMEM((rows, width), jnp.float32),
            pltpu.VMEM((rows, hidden // chunks), low),
            pltpu.VMEM((rows, hidden // chunks), low),
            pltpu.VMEM((2, 8, 2, piece, width), low),
            pltpu.VMEM((chunks, 8, 2, piece, width), low),
        ]
        + landing
        + [dma((chunks, 5)), dma((chunks, 5)), dma((2, 2 * chunks)), dma, dma],
        compiler_params=pltpu.CompilerParams(
            vmem_limit_bytes=KERNEL_VMEM, collective_id=5, has_side_effects=True
        ),
        name="middle",
    )(attended, x_rows, grad_rows, vecs, out_low, mine, other)


def per_device_clips(
    x_tokens,
    out_grad,
    w_qkv,
    w_out,
    w_up,
    w_down,
    vectors,
    qkv_mean,
    qkv_square,
    out_mean,
    out_square,
    up_mean,
    up_square,
    down_mean,
    down_square,
    vectors_mean,
    vectors_square,
):
    me = lax.axis_index("ctx")
    width = x_tokens.shape[2]
    low = jnp.bfloat16
    side = width // 2

    def blocks(values, start, count):
        return [values[:, (start + i) * width : (start + i + 1) * width] for i in range(count)]

    first_weights = jnp.concatenate(blocks(w_qkv, 0, 3) + [w_out], axis=0).astype(low)
    first_weights = first_weights.reshape(2, 3, 8, -1, width)
    hidden = w_up.shape[1]
    mixed = [
        jnp.concatenate(
            [w_up[:, start + i * side : start + (i + 1) * side] for start in (0, hidden // 2)], axis=1
        )
        for i in range(4)
    ]
    late_weights = jnp.concatenate([w_down] + mixed, axis=0).astype(low)
    late_weights = late_weights.reshape(2, 3, 8, -1, width)
    vector_own = jnp.pad(vectors.astype(low).astype(jnp.float32), ((0, 4), (0, 0)))

    x_low, projected, qkv_low, out_low, vector_rows = start_call(
        x_tokens, first_weights, vector_own
    )
    attended_low, inverse_total, exponent, late_other, grad_output = attend_call(
        projected, late_weights, out_grad, width
    )
    y_rows, grad_resid, grad_attended, partial, grad_out, part_sums = middle_call(
        attended_low,
        x_low,
        grad_output,
        vector_rows,
        out_low,
        late_weights.reshape(-1, width),
        late_other.reshape(-1, width),
    )
    *grad_parts, late_shared, y_tokens = attend_back_call(
        projected, grad_attended, attended_low, inverse_total, exponent, partial, y_rows
    )
    x_grad, first_shared, summed_vectors = finish_call(
        grad_parts, x_low, qkv_low, vector_rows, grad_resid, grad_out, part_sums
    )

    down_share = late_shared[0].reshape(-1, width).astype(jnp.float32)
    up_blocks = late_shared[1].reshape(4, side, width).astype(jnp.float32)
    up_share = jnp.concatenate(
        [up_blocks[i][:, j * side : (j + 1) * side] for j in range(2) for i in range(4)], axis=1
    )
    first_share = first_shared.reshape(4, side, width).astype(jnp.float32)
    qkv_share = jnp.concatenate([first_share[i] for i in range(3)], axis=1)
    vector_share = lax.dynamic_slice_in_dim(summed_vectors[:12], me * side, side, axis=1)

    qkv_new = adam_update(w_qkv, qkv_share, qkv_mean, qkv_square, matrix_rate, matrix_decay)
    out_new = adam_update(w_out, first_share[3], out_mean, out_square, matrix_rate, matrix_decay)
    up_new = adam_update(w_up, up_share, up_mean, up_square, matrix_rate, matrix_decay)
    down_new = adam_update(w_down, down_share, down_mean, down_square, matrix_rate, matrix_decay)
    vectors_new = adam_update(
        vectors, vector_share, vectors_mean, vectors_square, vector_rate, 0.0
    )
    return (y_tokens, x_grad) + qkv_new + out_new + up_new + down_new + vectors_new


def per_device(x_tokens, *others):
    clips = x_tokens.shape[0]
    if lax.axis_size("ctx") == 2 and lax.axis_size("dp") == 16 and clips == 2:
        return per_device_clips(x_tokens, *others)
    return per_device_split(x_tokens, *others)


def solution(mesh):
    return jax.shard_map(
        per_device,
        mesh=mesh,
        in_specs=(
            P("dp", "ctx", None),
            P("dp", "ctx", None),
            P("ctx", None),
            P("ctx", None),
            P("ctx", None),
            P("ctx", None),
            P(None, "ctx"),
            P("ctx", None),
            P("ctx", None),
            P("ctx", None),
            P("ctx", None),
            P("ctx", None),
            P("ctx", None),
            P("ctx", None),
            P("ctx", None),
            P(None, "ctx"),
            P(None, "ctx"),
        ),
        out_specs=(
            P("dp", "ctx", None),
            P("dp", "ctx", None),
            P("ctx", None),
            P("ctx", None),
            P("ctx", None),
            P("ctx", None),
            P("ctx", None),
            P("ctx", None),
            P("ctx", None),
            P("ctx", None),
            P("ctx", None),
            P("ctx", None),
            P("ctx", None),
            P("ctx", None),
            P(None, "ctx"),
            P(None, "ctx"),
            P(None, "ctx"),
        ),
        check_vma=False,
    )
```

```python
import functools

import jax
import jax.numpy as jnp
from jax import lax
from jax.experimental import pallas as pl
from jax.experimental.pallas import tpu as pltpu
from jax.sharding import PartitionSpec as P

HD = 64
STEP = 10


norm_epsilon = 1e-06
adam_epsilon = 1e-08
matrix_rate = 0.04
matrix_decay = 0.05
vector_rate = 0.2


def normalize(values, norm_gain, norm_shift):
    row_mean = jnp.mean(values, axis=-1, keepdims=True)
    centred = values - row_mean
    row_var = jnp.mean(centred * centred, axis=-1, keepdims=True)
    inverse = lax.rsqrt(row_var + norm_epsilon)
    normed = centred * inverse
    return (normed * norm_gain + norm_shift, normed, inverse)


def norm_back(upstream, norm_gain, normed, inverse):
    scaled = upstream * norm_gain
    first_mean = jnp.mean(scaled, axis=-1, keepdims=True)
    second_mean = jnp.mean(scaled * normed, axis=-1, keepdims=True)
    return inverse * (scaled - first_mean - normed * second_mean)


def normal_cdf(values):
    return 0.5 * (1.0 + lax.erf(values * 0.7071067811865476))


def attend(operands):
    query_block, key_block, value_block = operands
    scores = (
        jnp.einsum("qhd,khd->hqk", query_block, key_block, preferred_element_type=jnp.float32)
        * 0.125
    )
    peak_score = jnp.max(scores, axis=-1, keepdims=True)
    exponent = jnp.exp(scores - peak_score)
    totals = jnp.sum(exponent, axis=-1, keepdims=True)
    probs_low = (exponent / totals).astype(jnp.bfloat16)
    attended = jnp.einsum(
        "hqk,khd->qhd", probs_low, value_block, preferred_element_type=jnp.float32
    )
    return (attended, peak_score + jnp.log(totals))


def attend_back(operands):
    query_block, key_block, value_block, log_total, grad_block = operands
    scores = (
        jnp.einsum("qhd,khd->hqk", query_block, key_block, preferred_element_type=jnp.float32)
        * 0.125
    )
    probs = jnp.exp(scores - log_total)
    grad_probs = jnp.einsum(
        "qhd,khd->hqk", grad_block, value_block, preferred_element_type=jnp.float32
    )
    delta = jnp.sum(probs * grad_probs, axis=-1, keepdims=True)
    grad_scores = (probs * (grad_probs - delta)).astype(jnp.bfloat16)
    grad_query = (
        jnp.einsum("hqk,khd->qhd", grad_scores, key_block, preferred_element_type=jnp.float32)
        * 0.125
    )
    grad_key = (
        jnp.einsum("hqk,qhd->khd", grad_scores, query_block, preferred_element_type=jnp.float32)
        * 0.125
    )
    grad_value = jnp.einsum(
        "hqk,qhd->khd", probs.astype(jnp.bfloat16), grad_block, preferred_element_type=jnp.float32
    )
    return (grad_query, grad_key, grad_value)


def adam_update(weight, gradient, first_old, second_old, step_rate, decay_rate):
    first_new = 0.5 * first_old + 0.5 * gradient
    second_new = 0.5 * second_old + 0.5 * gradient * gradient
    correction = 1.0 - 0.5**STEP
    update = (
        first_new / correction / (jnp.sqrt(second_new / correction) + adam_epsilon)
        + decay_rate * weight
    )
    return (first_new, second_new, weight - step_rate * update)


def per_device_split(
    x_tokens,
    out_grad,
    w_qkv,
    w_out,
    w_up,
    w_down,
    vectors,
    qkv_mean,
    qkv_square,
    out_mean,
    out_square,
    up_mean,
    up_square,
    down_mean,
    down_square,
    vectors_mean,
    vectors_square,
):
    masters = (w_qkv, w_out, w_up, w_down, vectors)
    lowered = tuple((member.astype(jnp.bfloat16) for member in masters))
    qkv_low, out_low, up_low, down_low, vector_low = (
        lax.all_gather(lowered[0], "ctx", axis=0, tiled=True),
        lax.all_gather(lowered[1], "ctx", axis=0, tiled=True),
        lax.all_gather(lowered[2], "ctx", axis=0, tiled=True),
        lax.all_gather(lowered[3], "ctx", axis=0, tiled=True),
        lax.all_gather(lowered[4], "ctx", axis=1, tiled=True),
    )
    vector_rows = vector_low.astype(jnp.float32)
    clip_count, row_count, model_width = x_tokens.shape
    head_count = model_width // HD
    token_total = clip_count * row_count
    flat_rows = x_tokens.reshape(token_total, model_width).astype(jnp.float32)
    norm_one, normed_one, inverse_one = normalize(flat_rows, vector_rows[0], vector_rows[1])
    norm_one_low = norm_one.astype(jnp.bfloat16)
    qkv_shift = jnp.concatenate([vector_rows[2], jnp.zeros_like(vector_rows[2]), vector_rows[3]])
    projected = (
        jnp.dot(norm_one_low, qkv_low, preferred_element_type=jnp.float32) + qkv_shift
    ).astype(jnp.bfloat16)
    query_rows = projected[:, :model_width].reshape(clip_count, row_count, head_count, HD)
    key_local = projected[:, model_width : 2 * model_width].reshape(
        clip_count, row_count, head_count, HD
    )
    value_local = projected[:, 2 * model_width :].reshape(clip_count, row_count, head_count, HD)
    key_rows, value_rows = (
        lax.all_gather(key_local, "ctx", axis=1, tiled=True),
        lax.all_gather(value_local, "ctx", axis=1, tiled=True),
    )
    attended, log_total = lax.map(attend, (query_rows, key_rows, value_rows))
    attended_low = attended.reshape(token_total, model_width).astype(jnp.bfloat16)
    branch = jnp.dot(attended_low, out_low, preferred_element_type=jnp.float32) + vector_rows[4]
    resid = flat_rows + branch
    norm_two, normed_two, inverse_two = normalize(resid, vector_rows[5], vector_rows[6])
    norm_two_low = norm_two.astype(jnp.bfloat16)
    pre_act = jnp.dot(norm_two_low, up_low, preferred_element_type=jnp.float32) + vector_rows[
        8:
    ].reshape(-1)
    act_low = (pre_act * normal_cdf(pre_act)).astype(jnp.bfloat16)
    mlp_out = jnp.dot(act_low, down_low, preferred_element_type=jnp.float32) + vector_rows[7]
    y_tokens = (resid + mlp_out).astype(jnp.bfloat16).reshape(clip_count, row_count, model_width)
    grad_output = out_grad.reshape(token_total, model_width)
    grad_float = grad_output.astype(jnp.float32)
    grad_down = jnp.einsum("tf,td->fd", act_low, grad_output, preferred_element_type=jnp.float32)
    down_shift = jnp.sum(grad_float, axis=0)
    grad_act = jnp.dot(grad_output, down_low.T, preferred_element_type=jnp.float32)
    density = jnp.exp(-0.5 * pre_act * pre_act) * 0.3989422804014327
    grad_pre = (grad_act * (normal_cdf(pre_act) + pre_act * density)).astype(jnp.bfloat16)
    grad_up = jnp.einsum("td,tf->df", norm_two_low, grad_pre, preferred_element_type=jnp.float32)
    up_shift = jnp.sum(grad_pre.astype(jnp.float32), axis=0)
    grad_norm_two = jnp.dot(grad_pre, up_low.T, preferred_element_type=jnp.float32)
    gain_two_grad = jnp.sum(grad_norm_two * normed_two, axis=0)
    shift_two_grad = jnp.sum(grad_norm_two, axis=0)
    grad_resid = grad_float + norm_back(grad_norm_two, vector_rows[5], normed_two, inverse_two)
    grad_branch = grad_resid.astype(jnp.bfloat16)
    grad_out = jnp.einsum(
        "td,te->de", attended_low, grad_branch, preferred_element_type=jnp.float32
    )
    out_shift = jnp.sum(grad_branch.astype(jnp.float32), axis=0)
    grad_attended = jnp.dot(grad_branch, out_low.T, preferred_element_type=jnp.float32).astype(
        jnp.bfloat16
    )
    grad_attended = grad_attended.reshape(clip_count, row_count, head_count, HD)
    grad_query, key_terms, value_terms = lax.map(
        attend_back, (query_rows, key_rows, value_rows, log_total, grad_attended)
    )
    grad_key, grad_value = (
        lax.psum_scatter(
            key_terms.astype(jnp.bfloat16), "ctx", scatter_dimension=1, tiled=True
        ).astype(jnp.float32),
        lax.psum_scatter(
            value_terms.astype(jnp.bfloat16), "ctx", scatter_dimension=1, tiled=True
        ).astype(jnp.float32),
    )
    grad_projected = jnp.concatenate(
        [
            grad_query.reshape(token_total, model_width),
            grad_key.reshape(token_total, model_width),
            grad_value.reshape(token_total, model_width),
        ],
        axis=1,
    ).astype(jnp.bfloat16)
    grad_qkv = jnp.einsum(
        "td,te->de", norm_one_low, grad_projected, preferred_element_type=jnp.float32
    )
    projected_sums = jnp.sum(grad_projected.astype(jnp.float32), axis=0)
    grad_norm_one = jnp.dot(grad_projected, qkv_low.T, preferred_element_type=jnp.float32)
    gain_one_grad = jnp.sum(grad_norm_one * normed_one, axis=0)
    shift_one_grad = jnp.sum(grad_norm_one, axis=0)
    x_grad = (
        grad_resid + norm_back(grad_norm_one, vector_rows[0], normed_one, inverse_one)
    ).astype(jnp.bfloat16)
    x_grad = x_grad.reshape(clip_count, row_count, model_width)
    first_rows = jnp.stack(
        [
            gain_one_grad,
            shift_one_grad,
            projected_sums[:model_width],
            projected_sums[2 * model_width :],
            out_shift,
            gain_two_grad,
            shift_two_grad,
            down_shift,
        ]
    )
    grad_vectors = jnp.concatenate([first_rows, up_shift.reshape(-1, model_width)], axis=0)
    group_size = lax.axis_size("ctx")
    vector_count = grad_vectors.shape[0]
    flat_vectors = (
        grad_vectors.reshape(vector_count, group_size, -1)
        .transpose(1, 0, 2)
        .reshape(group_size, -1)
    )
    shaped = (grad_qkv, grad_out, grad_up, grad_down, flat_vectors)
    spread = (
        lax.psum_scatter(
            shaped[0].astype(jnp.bfloat16), "dp", scatter_dimension=1, tiled=True
        ).astype(jnp.float32),
        lax.psum_scatter(
            shaped[1].astype(jnp.bfloat16), "dp", scatter_dimension=1, tiled=True
        ).astype(jnp.float32),
        lax.psum_scatter(
            shaped[2].astype(jnp.bfloat16), "dp", scatter_dimension=1, tiled=True
        ).astype(jnp.float32),
        lax.psum_scatter(
            shaped[3].astype(jnp.bfloat16), "dp", scatter_dimension=1, tiled=True
        ).astype(jnp.float32),
        lax.psum_scatter(
            shaped[4].astype(jnp.bfloat16), "dp", scatter_dimension=1, tiled=True
        ).astype(jnp.float32),
    )
    owned = (
        lax.psum_scatter(
            spread[0].astype(jnp.bfloat16), "ctx", scatter_dimension=0, tiled=True
        ).astype(jnp.float32),
        lax.psum_scatter(
            spread[1].astype(jnp.bfloat16), "ctx", scatter_dimension=0, tiled=True
        ).astype(jnp.float32),
        lax.psum_scatter(
            spread[2].astype(jnp.bfloat16), "ctx", scatter_dimension=0, tiled=True
        ).astype(jnp.float32),
        lax.psum_scatter(
            spread[3].astype(jnp.bfloat16), "ctx", scatter_dimension=0, tiled=True
        ).astype(jnp.float32),
        lax.psum_scatter(
            spread[4].astype(jnp.bfloat16), "ctx", scatter_dimension=0, tiled=True
        ).astype(jnp.float32),
    )
    collected = (
        lax.all_gather(owned[0].astype(jnp.bfloat16), "dp", axis=1, tiled=True).astype(jnp.float32),
        lax.all_gather(owned[1].astype(jnp.bfloat16), "dp", axis=1, tiled=True).astype(jnp.float32),
        lax.all_gather(owned[2].astype(jnp.bfloat16), "dp", axis=1, tiled=True).astype(jnp.float32),
        lax.all_gather(owned[3].astype(jnp.bfloat16), "dp", axis=1, tiled=True).astype(jnp.float32),
        lax.all_gather(owned[4].astype(jnp.bfloat16), "dp", axis=1, tiled=True).astype(jnp.float32),
    )
    shares = (
        collected[0],
        collected[1],
        collected[2],
        collected[3],
        collected[4].reshape(vector_count, -1),
    )
    qkv_moment, qkv_second, qkv_master = adam_update(
        w_qkv, shares[0], qkv_mean, qkv_square, matrix_rate, matrix_decay
    )
    out_moment, out_second, out_master = adam_update(
        w_out, shares[1], out_mean, out_square, matrix_rate, matrix_decay
    )
    up_moment, up_second, up_master = adam_update(
        w_up, shares[2], up_mean, up_square, matrix_rate, matrix_decay
    )
    down_moment, down_second, down_master = adam_update(
        w_down, shares[3], down_mean, down_square, matrix_rate, matrix_decay
    )
    vectors_moment, vectors_second, vectors_master = adam_update(
        vectors, shares[4], vectors_mean, vectors_square, vector_rate, 0.0
    )
    return (
        y_tokens,
        x_grad,
        qkv_moment,
        qkv_second,
        qkv_master,
        out_moment,
        out_second,
        out_master,
        up_moment,
        up_second,
        up_master,
        down_moment,
        down_second,
        down_master,
        vectors_moment,
        vectors_second,
        vectors_master,
    )


LOG2E = 1.4426950408889634
NT = (((1,), (1,)), ((), ()))
NN = (((1,), (0,)), ((), ()))
TN = (((0,), (0,)), ((), ()))
KERNEL_VMEM = 62 * 2**20


def attend_kernel(q_ref, k_ref, v_ref, o_ref, r_ref, p_ref, score_a, score_b):
    rows = score_a.shape[0]
    total = k_ref.shape[0]
    lane = lax.broadcasted_iota(jnp.int32, (1, 2 * HD), 1)
    held = (score_a, score_b)
    parts = total // rows
    items = [(head, part) for head in range(2) for part in range(parts)]

    def score(index):
        head, part = items[index]
        keys = jnp.where((lane // HD) == head, k_ref[...], 0).astype(jnp.bfloat16)
        held[index % 2][...] = lax.dot_general(
            q_ref[part * rows : (part + 1) * rows, :], keys, NT, preferred_element_type=jnp.float32
        )

    def soften(index):
        head, part = items[index]
        values = held[index % 2][...]
        peak = jnp.max(values, axis=1, keepdims=True)
        p_ref[head, part * rows : (part + 1) * rows, :] = jnp.exp2(
            (values - peak) * (0.125 * LOG2E)
        ).astype(jnp.bfloat16)

    def weigh(index):
        head, part = items[index]
        span = slice(part * rows, (part + 1) * rows)
        kept = jnp.where((lane // HD) == head, v_ref[...], 0).astype(jnp.bfloat16)
        table = jnp.concatenate([kept, jnp.ones((total, 2 * HD), jnp.bfloat16)], axis=1)
        out = lax.dot_general(p_ref[head, span, :], table, NN, preferred_element_type=jnp.float32)
        inverse = 1.0 / out[:, 2 * HD :]
        mixed = (out[:, : 2 * HD] * inverse).astype(jnp.bfloat16)
        if head == 0:
            o_ref[span, :] = mixed
            r_ref[span, :] = inverse
        else:
            o_ref[span, :] = jnp.where(lane < HD, o_ref[span, :], mixed)
            r_ref[span, :] = jnp.where(lane < HD, r_ref[span, :], inverse)

    score(0)
    for index in range(len(items)):
        if index + 1 < len(items):
            score(index + 1)
        soften(index)
        weigh(index)


def attend_back_kernel(
    q_ref, k_ref, v_ref, g_ref, o_ref, r_ref, p_ref, dq_ref, dk_ref, dv_ref, ds, qt, gt, dkt, dvt
):
    head = pl.program_id(1)
    total = k_ref.shape[0]
    half = total // 2
    lane = lax.broadcasted_iota(jnp.int32, (1, 2 * HD), 1)
    keep = (lane // HD) == head
    scaled = g_ref[...].astype(jnp.float32) * r_ref[...]

    @pl.when(head == 0)
    def _():
        qt[...] = q_ref[...].T
        gt[...] = scaled.astype(jnp.bfloat16).T

    delta = jnp.sum(jnp.where(keep, scaled * o_ref[...].astype(jnp.float32), 0.0), axis=1, keepdims=True)
    values = jnp.where(keep, v_ref[...], 0).astype(jnp.bfloat16)
    grad_probs = lax.dot_general(
        scaled.astype(jnp.bfloat16), values, NT, preferred_element_type=jnp.float32
    )
    ds[...] = (p_ref[...].astype(jnp.float32) * (grad_probs - delta)).astype(jnp.bfloat16)
    span = pl.ds(pl.multiple_of(head * HD, HD), HD)
    dvt[span, :] = lax.dot_general(gt[span, :], p_ref[...], NN, preferred_element_type=jnp.float32)
    dkt[span, :] = 0.125 * lax.dot_general(
        qt[span, :], ds[...], NN, preferred_element_type=jnp.float32
    )
    keys = jnp.where(keep, k_ref[...], 0).astype(jnp.bfloat16)
    for part in range(2):
        rows = slice(part * half, (part + 1) * half)
        term = 0.125 * lax.dot_general(ds[rows, :], keys, NN, preferred_element_type=jnp.float32)
        dq_ref[rows, :] = jnp.where(keep, term.astype(jnp.bfloat16), dq_ref[rows, :])

    @pl.when(head == 1)
    def _():
        dk_ref[...] = dkt[...].T.astype(jnp.bfloat16)
        dv_ref[...] = dvt[...].T.astype(jnp.bfloat16)


MESH = pl.DeviceIdType.MESH
GATHER_ORDERS = ("xab", "axb", "abx")


def own_bits():
    place = lax.axis_index("dp")
    z = place // 4
    return {
        "z": z,
        "core": place % 2,
        "x": (place // 2) % 2,
        "a": (z % 2 + z // 2) % 2,
        "b": z // 2,
        "y": lax.axis_index("ctx"),
    }


def partner(name):
    place, group = lax.axis_index("dp"), lax.axis_index("ctx")
    z = place // 4
    if name == "core":
        return (place + 1 - 2 * (place % 2), group)
    if name == "x":
        return (place + 2 - 4 * ((place // 2) % 2), group)
    if name == "a":
        return (place + 4 - 8 * (z % 2), group)
    if name == "b":
        return (place + 4 * (3 - 2 * z), group)
    if name in ("z1", "z2", "z3"):
        return (place + 4 * ((z + int(name[1])) % 4 - z), group)
    return (place, 1 - group)


def meet_partners():
    barrier = pltpu.get_barrier_semaphore()
    names = ("core", "x", "y", "z1", "z2", "z3")
    for name in names:
        pl.semaphore_signal(barrier, inc=1, device_id=partner(name), device_id_type=MESH)
    pl.semaphore_wait(barrier, len(names))


def remote(source, target, name, send_sem, recv_sem):
    return pltpu.make_async_remote_copy(
        src_ref=source,
        dst_ref=target,
        send_sem=send_sem,
        recv_sem=recv_sem,
        device_id=partner(name),
        device_id_type=MESH,
    )


def local_copy(source, target, sem):
    return pltpu.make_async_copy(source, target, sem)


def block_of(order, bits):
    first, second, third = (bits[name] for name in order if name != "y")
    return first * 4 + second * 2 + third


class Gather:
    stages = 4

    def __init__(self, buffer, orders, send, recv):
        self.buffer, self.orders, self.send, self.recv = buffer, orders, send, recv

    def copy(self, stage, stream):
        bits = own_bits()
        order = self.orders[stream].replace("y", "")
        block = block_of(order, bits)
        size = (1, 2, 4, 8)[stage]
        name = "core" if stage == 3 else order[2 - stage]
        region = self.buffer.at[bits["core"], stream, pl.ds(block // size * size, size)]
        return remote(region, region, name, self.send.at[stage, stream], self.recv.at[stage, stream])

    def start(self, stage, stream):
        self.copy(stage, stream).start()

    def advance(self, stage, stream):
        self.copy(stage, stream).wait()
        if stage + 1 < self.stages:
            self.copy(stage + 1, stream).start()

    def begin(self):
        for stream in range(len(self.orders)):
            self.start(0, stream)

    def advance_all(self, stage):
        for stream in range(len(self.orders)):
            self.advance(stage, stream)


class StreamSum:
    def __init__(self, total, landing, shared, send, recv, local):
        self.total, self.landing, self.shared = total, landing, shared
        self.send, self.recv, self.local = send, recv, local

    def copies(self, stage):
        bits = own_bits()
        x, y, z = bits["x"], bits["y"], bits["z"]

        def make(source, target, name, at):
            return remote(source, target, name, self.send.at[at], self.recv.at[at])

        if stage == 1:
            return [make(self.total.at[:, 1 - y], self.landing[1], "y", 1)]
        if stage == 2:
            return [make(self.total.at[pl.ds((1 - x) * 4, 4), y], self.landing[2], "x", 2)]
        if stage == 3:
            return [
                make(
                    self.total.at[x * 4 + (z + d) % 4, y],
                    self.landing[3].at[d - 1],
                    "z" + str(d),
                    2 + d,
                )
                for d in (1, 2, 3)
            ]
        if stage == 4:
            return [
                make(
                    self.total.at[x * 4 + z, y],
                    self.shared.at[x * 4 + z],
                    "z" + str(d),
                    5 + d,
                )
                for d in (1, 2, 3)
            ]
        if stage == 5:
            region = self.shared.at[pl.ds(x * 4, 4)]
            return [make(region, region, "x", 9)]
        return [make(self.shared, self.shared, "core", 10)]

    def own_copy(self):
        bits = own_bits()
        block = bits["x"] * 4 + bits["z"]
        return local_copy(self.total.at[block, bits["y"]], self.shared.at[block], self.local)

    def start(self, stage):
        for copy in self.copies(stage):
            copy.start()
        if stage == 4:
            self.own_copy().start()

    def finish(self, stage):
        for copy in self.copies(stage):
            copy.wait()
        if stage == 4:
            self.own_copy().wait()
        if stage > 3:
            return
        bits = own_bits()
        x, y, z = bits["x"], bits["y"], bits["z"]
        start, size = ((0, 8), (x * 4, 4), (x * 4 + z, 1))[stage - 1]
        landed = self.landing[stage]

        @pl.loop(0, size)
        def _(block):
            here = self.total[start + block, y].astype(jnp.float32)
            if stage == 3:
                for d in range(3):
                    here = here + landed[d].astype(jnp.float32)
            else:
                here = here + landed[block].astype(jnp.float32)
            self.total[start + block, y] = here.astype(jnp.bfloat16)

    def move(self, stage):
        self.finish(stage)
        if stage < 6:
            self.start(stage + 1)


class CoreSum:
    def __init__(self, parts, total, landed, send, recv, local=None):
        self.parts, self.total, self.landed = parts, total, landed
        self.send, self.recv, self.local = send, recv, local

    def copy(self):
        away = 1 - own_bits()["core"]
        return remote(self.parts.at[away], self.landed, "core", self.send, self.recv)

    def start(self):
        self.copy().start()

    def finish(self):
        self.copy().wait()
        core = own_bits()["core"]

        @pl.loop(0, 8)
        def _(block):
            self.total[block] = (
                self.parts[core, block].astype(jnp.float32) + self.landed[block].astype(jnp.float32)
            ).astype(jnp.bfloat16)


def landing_shapes(stages, rows, columns):
    leads = {0: (8, 2), 1: (8,), 2: (4,), 3: (3,)}
    return [pltpu.VMEM(leads[stage] + (rows, columns), jnp.bfloat16) for stage in stages]


def sum_sems(streams):
    dma = pltpu.SemaphoreType.DMA
    return [dma((streams, 11)), dma((streams, 11)), dma((streams,))]


def gather_sems(streams):
    return [pltpu.SemaphoreType.DMA((4, streams)), pltpu.SemaphoreType.DMA((4, streams))]


def start_kernel(
    x_ref, vec_ref, wqkv_in, wout_in, wup_in, wdown_in,
    x2_out, proj_out, wqkv_out, wout_out, vecs_ref, norm_out, late_out,
    x2_ref, proj_ref, wqkv_ref, wout_ref, norm, late_ref, w_ref, other, wide, vec_other, g_send, g_recv, w_send, w_recv, x_send, x_recv, v_sem, l_sem, f_sem, o_sem,
):
    bits = own_bits()
    me = bits["y"]
    half, width = x_ref.shape[1], x_ref.shape[2]
    gather = Gather(other, GATHER_ORDERS, g_send, g_recv)
    side = width // 2
    leaving = []

    def leave(source, target):
        copy = local_copy(source, target, o_sem.at[len(leaving)])
        copy.start()
        leaving.append(copy)

    def leave_rows(source, target, at, size):
        leave(source.at[pl.ds(at, size)], target.at[pl.ds(at, size)])

    pieces_in = [[(wqkv_in.at[:, pl.ds(i * width, width)], 0, width)] for i in range(3)]
    pieces_in.append([(wout_in, 0, width)])
    pieces_in += [[(wdown_in.at[pl.ds(i * side, side)], 0, width)] for i in range(4)]
    pieces_in += [
        [(wup_in.at[:, pl.ds((i + 4 * j) * side, side)], j * side, side) for j in range(2)]
        for i in range(4)
    ]

    def fetch(index):
        slot = index % 4
        return [
            local_copy(source, wide.at[slot, :, pl.ds(at, size)], f_sem.at[index, k])
            for k, (source, at, size) in enumerate(pieces_in[index])
        ]

    def lower(index):
        for copy in fetch(index):
            copy.wait()
        rows = 32 if index < 4 else 64
        target = w_ref if index < 4 else late_ref
        count = side // rows
        for block in range(count):
            flat = index % 4 * count + block if index < 4 else (index - 4) * count + block
            target[flat // 24, flat // 8 % 3, flat % 8] = wide[
                index % 4, block * rows : (block + 1) * rows, :
            ].astype(jnp.bfloat16)
        if index + 4 < len(pieces_in):
            for copy in fetch(index + 4):
                copy.start()

    for index in range(4):
        for copy in fetch(index):
            copy.start()
    meet_partners()
    vec_copy = remote(vec_ref, vec_other, "y", v_sem.at[0], v_sem.at[1])
    vec_copy.start()
    own_x = local_copy(x_ref.at[me], x2_ref.at[pl.ds(0, half)], l_sem)
    own_x.start()
    for index in range(4):
        lower(index)
    pieces = []
    for stream in range(3):
        block = block_of(GATHER_ORDERS[stream], bits)
        piece = remote(
            w_ref.at[bits["core"], stream, block],
            other.at[bits["core"], stream, block],
            "y",
            w_send.at[stream],
            w_recv.at[stream],
        )
        piece.start()
        pieces.append(piece)
    first = half // 32 * 16 + 16
    spans = [(0, first), (first, half - first)]
    trades = [
        remote(
            x_ref.at[1 - me, pl.ds(at, size)],
            x2_ref.at[pl.ds(half + at, size)],
            "y",
            x_send.at[index],
            x_recv.at[index],
        )
        for index, (at, size) in enumerate(spans)
    ]
    for piece in pieces:
        piece.wait()
    gather.begin()
    trades[0].start()
    vec_copy.wait()
    mine, others = vec_ref[...], vec_other[...]
    vecs_ref[...] = jnp.where(
        me == 0,
        jnp.concatenate([mine, others], axis=1),
        jnp.concatenate([others, mine], axis=1),
    )
    for c in range(4):
        half_at = slice(c % 2 * (width // 2), (c % 2 + 1) * (width // 2))
        vecs_ref[12 + c : 13 + c, :] = jnp.concatenate(
            [vecs_ref[8 + c // 2 : 9 + c // 2, half_at], vecs_ref[10 + c // 2 : 11 + c // 2, half_at]],
            axis=1,
        )
    gather.advance_all(0)
    trades[1].start()

    def norm_rows(at, size):
        values = x2_ref[at : at + size, :].astype(jnp.float32)
        normed, _, _ = normalize(values, vecs_ref[0:1, :], vecs_ref[1:2, :])
        norm[at : at + size, :] = normed.astype(jnp.bfloat16)

    own_x.wait()
    leave_rows(x2_ref, x2_out, 0, half)
    norm_rows(0, half)
    leave_rows(norm, norm_out, 0, half)
    gather.advance_all(1)
    for index in range(4, 8):
        lower(index)
    gather.advance_all(2)
    for index in range(8, 12):
        lower(index)
    leave(late_ref, late_out)
    gather.advance_all(3)
    part = width // 2

    for source, at in ((w_ref, me * part), (other, (1 - me) * part)):
        for matrix in range(4):
            for index in range(12):
                flat = matrix * 12 + index
                block = source[flat // 24, flat // 8 % 3, flat % 8]
                rows = pl.ds(pl.multiple_of(at + index * 32, 32), 32)
                if matrix < 3:
                    wqkv_ref[rows, matrix * width : (matrix + 1) * width] = block
                else:
                    wout_ref[rows, :] = block

    leave(wqkv_ref, wqkv_out)
    leave(wout_ref, wout_out)

    def project(at, size):
        @pl.loop(0, 3)
        def _(matrix):
            cols = pl.ds(pl.multiple_of(matrix * width, 128), width)
            shift = jnp.where(matrix == 0, vecs_ref[2:3, :], vecs_ref[3:4, :])
            shift = jnp.where(matrix == 1, 0.0, shift)
            proj_ref[at : at + size, cols] = (
                lax.dot_general(
                    norm[at : at + size, :], wqkv_ref[:, cols], NN, preferred_element_type=jnp.float32
                )
                + shift
            ).astype(jnp.bfloat16)

        leave_rows(proj_ref, proj_out, at, size)

    project(0, half)
    for trade, (at, size) in zip(trades, spans):
        trade.wait()
        leave_rows(x2_ref, x2_out, half + at, size)
        norm_rows(half + at, size)
        leave_rows(norm, norm_out, half + at, size)
        project(half + at, size)
    for copy in leaving:
        copy.wait()


def start_call(x_tokens, vector_own, w_qkv, w_out, w_up, w_down):
    _, half, width = x_tokens.shape
    low = jnp.bfloat16
    anywhere = pl.BlockSpec(memory_space=pl.ANY)
    vmem = pl.BlockSpec(memory_space=pltpu.VMEM)
    dma = pltpu.SemaphoreType.DMA
    return pl.pallas_call(
        start_kernel,
        in_specs=[anywhere, vmem] + [anywhere] * 4,
        out_specs=[anywhere] * 4 + [vmem] + [anywhere] * 2,
        out_shape=[
            jax.ShapeDtypeStruct((2 * half, width), low),
            jax.ShapeDtypeStruct((2 * half, 3 * width), low),
            jax.ShapeDtypeStruct((width, 3 * width), low),
            jax.ShapeDtypeStruct((width, width), low),
            jax.ShapeDtypeStruct((16, width), jnp.float32),
            jax.ShapeDtypeStruct((2 * half, width), low),
            jax.ShapeDtypeStruct((2, 3, 8, 64, width), low),
        ],
        scratch_shapes=[
            pltpu.VMEM((2 * half, width), low),
            pltpu.VMEM((2 * half, 3 * width), low),
            pltpu.VMEM((width, 3 * width), low),
            pltpu.VMEM((width, width), low),
            pltpu.VMEM((2 * half, width), low),
            pltpu.VMEM((2, 3, 8, 64, width), low),
            pltpu.VMEM((2, 3, 8, 32, width), low),
            pltpu.VMEM((2, 3, 8, 32, width), low),
            pltpu.VMEM((4, width // 2, width), jnp.float32),
            pltpu.VMEM(vector_own.shape, jnp.float32),
        ]
        + gather_sems(3)
        + [dma((3,)), dma((3,)), dma((2,)), dma((2,)), dma((2,)), dma, dma((12, 2)), dma((12,))],
        compiler_params=pltpu.CompilerParams(
            vmem_limit_bytes=KERNEL_VMEM, collective_id=1, has_side_effects=True
        ),
        name="start",
    )(x_tokens, vector_own, w_qkv, w_out, w_up, w_down)


def attend_gather_kernel(
    q_ref, k_ref, v_ref, w_ref, grad_ref, o_ref, r_ref, p_ref, other_ref, grad2_ref,
    score_a, score_b, g_send, g_recv, w_send, w_recv, t_send, t_recv,
):
    step = pl.program_id(0)
    last = pl.num_programs(0) - 1
    bits = own_bits()
    me = bits["y"]
    gather = Gather(other_ref, GATHER_ORDERS, g_send, g_recv)

    def piece(stream):
        block = block_of(GATHER_ORDERS[stream], bits)
        return remote(
            w_ref.at[bits["core"], stream, block],
            other_ref.at[bits["core"], stream, block],
            "y",
            w_send.at[stream],
            w_recv.at[stream],
        )

    trade = remote(grad_ref.at[1 - me], grad2_ref, "y", t_send, t_recv)

    @pl.when(step == 0)
    def _():
        meet_partners()
        for stream in range(3):
            piece(stream).start()

    @pl.when(step == 1)
    def _():
        for stream in range(3):
            piece(stream).wait()
        gather.begin()
        trade.start()

    for stage, at in enumerate(GATHER_STEPS):
        @pl.when(step == at)
        def _(stage=stage):
            gather.advance_all(stage)

    attend_kernel(q_ref, k_ref, v_ref, o_ref, r_ref, p_ref, score_a, score_b)

    @pl.when(step == last)
    def _():
        gather.advance_all(3)
        trade.wait()


GATHER_STEPS = (2, 3, 5)


def attend_call(projected, weights, out_grad, width):
    total = projected.shape[0]
    pairs = width // (2 * HD)
    half = out_grad.shape[1]
    anywhere = pl.BlockSpec(memory_space=pl.ANY)
    dma = pltpu.SemaphoreType.DMA

    def columns(start):
        return pl.BlockSpec((total, 2 * HD), lambda p: (0, start * pairs + p))

    return pl.pallas_call(
        attend_gather_kernel,
        grid=(pairs,),
        in_specs=[columns(0), columns(1), columns(2), anywhere, anywhere],
        out_specs=[
            columns(0),
            columns(0),
            pl.BlockSpec((2, total, total), lambda p: (p, 0, 0)),
            anywhere,
            anywhere,
        ],
        out_shape=[
            jax.ShapeDtypeStruct((total, width), jnp.bfloat16),
            jax.ShapeDtypeStruct((total, width), jnp.float32),
            jax.ShapeDtypeStruct((2 * pairs, total, total), jnp.bfloat16),
            jax.ShapeDtypeStruct(weights.shape, jnp.bfloat16),
            jax.ShapeDtypeStruct((half, width), jnp.bfloat16),
        ],
        scratch_shapes=[pltpu.VMEM((total // 2, total), jnp.float32)] * 2
        + gather_sems(3)
        + [dma((3,)), dma((3,)), dma, dma],
        compiler_params=pltpu.CompilerParams(
            vmem_limit_bytes=KERNEL_VMEM, collective_id=2, has_side_effects=True
        ),
        cost_estimate=pl.CostEstimate(
            flops=16 * pairs * total * total * 2 * HD,
            bytes_accessed=4 * pairs * total * total,
            transcendentals=2 * pairs * total * total,
        ),
        name="attend",
    )(projected, projected, projected, weights, out_grad)


BACK_FIRST = (4, 3, 2, 1)
BACK_STAGES = ((), (3,), (2, 3), (1, 2, 3), (0, 1, 2, 3), (0, 1, 2, 3), (0, 1))
BACK_MOVES = (
    (2, ((4, 0),)),
    (3, ((2, 2),)),
    (4, ((0, 4), (1, 3))),
    (5, ((2, 3), (3, 1), (4, 1), (5, 0))),
    (6, ((0, 5), (1, 4))),
    (7, ((0, 6), (2, 4), (4, 2), (3, 2))),
    (8, ((4, 3), (5, 1), (1, 5))),
    (9, ((2, 5), (1, 6), (3, 3), (5, 2), (6, 0))),
    (10, ((4, 4), (2, 6))),
    (11, ((4, 5),)),
)
BACK_LAST = ((4, 6), (3, 4), (5, 3), (6, 1))
TRADE_STEP = 3


def attend_back_sum_kernel(
    q_ref, k_ref, v_ref, g_ref, o_ref, r_ref, p_ref, partial_ref, y2_ref, norm_ref, out_ref,
    dq_ref, dk_ref, dv_ref, late_ref, first_ref, tokens_ref, third_ref, parts_out,
    ds, qt, gt, dkt, dvt, total, small, parts, turned, *rest,
):
    landing, rest = rest[:-7], rest[-7:]
    s_send, s_recv, s_local, t_send, t_recv, l_sem, o_sem = rest
    pair, head = pl.program_id(0), pl.program_id(1)
    step = pair * 2 + head
    last = pl.num_programs(0) * 2 - 1
    core = own_bits()["core"]
    half = tokens_ref.shape[0]
    streams, cores, held = [], {}, list(landing)
    for index, stages in enumerate(BACK_STAGES):
        buffers = {stage: held.pop(0) for stage in stages}
        sems = (s_send.at[index], s_recv.at[index], s_local.at[index])
        if index < 4:
            shared, sums = late_ref.at[core, index], total.at[index]
        else:
            shared, sums = first_ref.at[core, index - 4], small.at[index - 4]
            source = parts.at[1 if index == 4 else (index - 5) % 2]
            cores[index] = CoreSum(
                source, sums, buffers[0], s_send.at[index, 0], s_recv.at[index, 0]
            )
        streams.append(StreamSum(sums, buffers, shared, *sems))
    trade = remote(y2_ref.at[pl.ds(half, half)], tokens_ref, "y", t_send, t_recv)
    load = local_copy(partial_ref, total, l_sem.at[1])
    load_out = local_copy(out_ref, parts.at[1], l_sem.at[3])
    load_norm = local_copy(norm_ref, ds.at[:, pl.ds(0, norm_ref.shape[1])], l_sem.at[2])

    @pl.when(step == 0)
    def _():
        load.start()
        load_norm.start()
        load_out.start()
        meet_partners()
        load_out.wait()
        cores[4].start()
        load_norm.wait()
        turned[...] = ds[:, : norm_ref.shape[1]].T
        load.wait()
        for index, stage in enumerate(BACK_FIRST):
            streams[index].start(stage)

    for at, moves in BACK_MOVES:
        @pl.when(step == at)
        def _(at=at, moves=moves):
            for index, stage in moves:
                if stage == 0:
                    cores[index].finish()
                    streams[index].start(1)
                else:
                    streams[index].move(stage)
            if at == TRADE_STEP:
                trade.start()

    attend_back_kernel(
        q_ref, k_ref, v_ref, g_ref, o_ref, r_ref, p_ref, dq_ref, dk_ref, dv_ref, ds, qt, gt, dkt, dvt
    )

    @pl.when(head == 1)
    def _():
        sides = jnp.concatenate([dq_ref[...], dk_ref[...], dv_ref[...]], axis=1)
        values = lax.dot_general(
            turned[...], sides, NN, preferred_element_type=jnp.float32
        ).astype(jnp.bfloat16)
        slot, part = (pair // 2) % 2, pair % 2
        rows = parts.shape[4]
        for side in range(2):
            for block in range(8):
                at = side * 8 * rows + block * rows
                parts[slot, part, block, side] = values[at : at + rows, :]

    for index, at in ((5, 3), (6, 7)):
        @pl.when(step == at)
        def _(index=index):
            cores[index].start()

    @pl.when(step == last)
    def _():
        hand = local_copy(parts.at[0], parts_out, o_sem.at[0])
        hand.start()
        for index, stage in BACK_LAST:
            streams[index].finish(stage)
        third = local_copy(small.at[2], third_ref.at[0], o_sem.at[1])
        third.start()
        second = local_copy(small.at[1], third_ref.at[1], o_sem.at[2])
        second.start()
        trade.wait()
        hand.wait()
        second.wait()
        third.wait()


def attend_back_call(projected, upstream, attended, inverse, exponent, partial, y2, norm, out_parts):
    total, width = attended.shape
    pairs = width // (2 * HD)
    streams, _, _, rows, _ = partial.shape
    side = width // 2
    low = jnp.bfloat16
    anywhere = pl.BlockSpec(memory_space=pl.ANY)
    dma = pltpu.SemaphoreType.DMA

    def columns(start):
        return pl.BlockSpec((total, 2 * HD), lambda p, h: (0, start * pairs + p))

    landing = []
    for index, stages in enumerate(BACK_STAGES):
        landing += landing_shapes(stages, rows, width if index < 4 else side)
    return pl.pallas_call(
        attend_back_sum_kernel,
        grid=(pairs, 2),
        in_specs=[columns(0), columns(1), columns(2), columns(0), columns(0), columns(0)]
        + [pl.BlockSpec((None, total, total), lambda p, h: (p * 2 + h, 0, 0))]
        + [anywhere] * 4,
        out_specs=[columns(0)] * 3 + [anywhere] * 5,
        out_shape=[jax.ShapeDtypeStruct((total, width), low)] * 3
        + [
            jax.ShapeDtypeStruct((2, streams, 8, rows, width), low),
            jax.ShapeDtypeStruct((2, 4, 8, rows, side), low),
            jax.ShapeDtypeStruct((total // 2, width), low),
            jax.ShapeDtypeStruct((2, 8, 2, rows, side), low),
            jax.ShapeDtypeStruct((2, 8, 2, rows, side), low),
        ],
        scratch_shapes=[pltpu.VMEM((total, total), low)]
        + [pltpu.VMEM((2 * HD, total), low)] * 2
        + [pltpu.VMEM((2 * HD, total), jnp.float32)] * 2
        + [
            pltpu.VMEM(partial.shape, low),
            pltpu.VMEM((3, 8, 2, rows, side), low),
            pltpu.VMEM((2, 2, 8, 2, rows, side), low),
            pltpu.VMEM((width, total), low),
        ]
        + landing
        + sum_sems(len(BACK_STAGES))
        + [dma, dma, dma((4,)), dma((3,))],
        compiler_params=pltpu.CompilerParams(
            vmem_limit_bytes=KERNEL_VMEM, collective_id=3, has_side_effects=True
        ),
        cost_estimate=pl.CostEstimate(
            flops=32 * pairs * total * total * 2 * HD,
            bytes_accessed=4 * pairs * total * total,
            transcendentals=0,
        ),
        name="attend_back",
    )(
        projected, projected, projected, upstream, attended, inverse, exponent, partial, y2, norm,
        out_parts,
    )


LAST_FIRST = ((0, 5), (1, 4), (2, 2))
LAST_STAGES = ((), (), (2, 3), (0, 1, 2, 3))
LAST_MOVES = (
    ((3, 0),),
    ((1, 4), (2, 2), (0, 5)),
    ((3, 1), (2, 3), (1, 5)),
    ((3, 2), (0, 6)),
    ((2, 4), (1, 6)),
    ((3, 3),),
    ((2, 5),),
    ((3, 4),),
    ((2, 6), (3, 5)),
    ((3, 6),),
)


def finish_kernel(
    dq_in, dk_in, dv_in, x_in, w_in, resid_in, vec_ref, part_ref, late_in, first_in, small_in,
    parts_ref,
    xg_ref, vsum_ref, late_ref, first_ref,
    dq_ref, dk_ref, dv_ref, x_ref, w_ref, resid_ref, sent_rows, own_rows, coming, small, *rest,
):
    landing, rest = rest[:-10], rest[-10:]
    s_send, s_recv, s_local, t_send, t_recv, l_sem, v_land, v_send, v_recv, i_sem = rest
    bits = own_bits()
    me, core = bits["y"], bits["core"]
    rows, width = x_ref.shape
    half = rows // 2
    streams, held = [], list(landing)
    for index, stages in enumerate(LAST_STAGES):
        buffers = {stage: held.pop(0) for stage in stages}
        sems = (s_send.at[index], s_recv.at[index], s_local.at[index])
        shared = late_ref.at[core, 3] if index == 0 else first_ref.at[core, index]
        streams.append(
            StreamSum(None if index == 0 else small.at[index - 1], buffers, shared, *sems)
        )
    core_sum = CoreSum(
        parts_ref, small.at[2], streams[3].landing[0], s_send.at[3, 0], s_recv.at[3, 0]
    )
    entering = {}
    for part, at in ((1, half), (0, 0)):
        copies = []
        for k, (source, target) in enumerate(
            ((dq_in, dq_ref), (dk_in, dk_ref), (dv_in, dv_ref), (x_in, x_ref), (resid_in, resid_ref))
        ):
            span = pl.ds(at, half)
            copies.append(local_copy(source.at[span], target.at[span], i_sem.at[part, k]))
        if part == 1:
            copies.append(local_copy(w_in, w_ref, i_sem.at[1, 5]))
        for copy in copies:
            copy.start()
        entering[part] = copies
    loads = [local_copy(small_in.at[1 - i], small.at[i], l_sem.at[1 + i]) for i in range(2)]
    for load in loads:
        load.start()
    gain, shift = vec_ref[0:1, :], vec_ref[1:2, :]
    meet_partners()
    core_sum.start()
    for load in loads:
        load.wait()
    for index, stage in LAST_FIRST:
        streams[index].start(stage)

    def turn(at):
        for index, stage in LAST_MOVES[at]:
            if stage == 0:
                core_sum.finish()
                streams[index].start(1)
            else:
                streams[index].move(stage)

    step = half // 7

    def products(at):
        span = slice(at, at + half)
        for matrix, part in enumerate((dq_ref, dk_ref, dv_ref)):
            term = lax.dot_general(
                part[span, :],
                w_ref[:, matrix * width : (matrix + 1) * width],
                NT,
                preferred_element_type=jnp.float32,
            )
            if matrix == 0:
                coming[...] = term
            else:
                coming[...] += term

    def input_rows(at, target):
        @pl.loop(0, 7)
        def _(index):
            here = pl.ds(pl.multiple_of(index * step, 16), step)
            span = pl.ds(pl.multiple_of(at + index * step, 16), step)
            upstream = coming[here, :]
            _, normed, inverse = normalize(x_ref[span, :].astype(jnp.float32), gain, shift)
            target[here, :] = (
                resid_ref[span, :] + norm_back(upstream, gain, normed, inverse)
            ).astype(jnp.bfloat16)
            vsum_ref[0:1, :] += jnp.sum(upstream * normed, axis=0, keepdims=True)
            vsum_ref[1:2, :] += jnp.sum(upstream, axis=0, keepdims=True)

    vsum_ref[...] = part_ref[...]
    for copy in entering[1]:
        copy.wait()
    products(half)
    turn(0)
    input_rows(half, sent_rows)
    trade = remote(sent_rows, xg_ref.at[me], "y", t_send, t_recv)
    trade.start()
    turn(1)
    for copy in entering[0]:
        copy.wait()
    products(0)
    turn(2)
    input_rows(0, own_rows)
    own = local_copy(own_rows, xg_ref.at[me], l_sem.at[0])
    own.start()
    vsum_ref[2:3, :] = jnp.sum(dq_ref[...].astype(jnp.float32), axis=0, keepdims=True)
    vsum_ref[3:4, :] = jnp.sum(dv_ref[...].astype(jnp.float32), axis=0, keepdims=True)

    def vector_step(stage):
        name = ("core", "x", "a", "b", "y")[stage]
        return remote(vsum_ref, v_land.at[stage], name, v_send.at[stage], v_recv.at[stage])

    vector_step(0).start()
    for at in range(3, len(LAST_MOVES)):
        turn(at)
        if at < 8:
            vector_step(at - 3).wait()
            vsum_ref[...] += v_land[at - 3]
            if at < 7:
                vector_step(at - 2).start()
    trade.wait()
    own.wait()


def finish_call(grad_parts, x2, wqkv, grad_resid, vecs, part_sums, late, first, small, parts):
    total, width = x2.shape
    low = jnp.bfloat16
    anywhere = pl.BlockSpec(memory_space=pl.ANY)
    vmem = pl.BlockSpec(memory_space=pltpu.VMEM)
    dma = pltpu.SemaphoreType.DMA
    rows, side = small.shape[3], small.shape[4]
    landing = []
    for stages in LAST_STAGES:
        landing += landing_shapes(stages, rows, side)
    return pl.pallas_call(
        finish_kernel,
        in_specs=[anywhere] * 6 + [vmem] * 2 + [anywhere] * 3 + [vmem],
        out_specs=[anywhere, vmem, anywhere, anywhere],
        out_shape=[
            jax.ShapeDtypeStruct((2, total // 2, width), low),
            jax.ShapeDtypeStruct((16, width), jnp.float32),
            jax.ShapeDtypeStruct(late.shape, low),
            jax.ShapeDtypeStruct(first.shape, low),
        ],
        input_output_aliases={8: 2, 9: 3},
        scratch_shapes=[pltpu.VMEM((total, width), low)] * 4
        + [
            pltpu.VMEM((width, 3 * width), low),
            pltpu.VMEM((total, width), jnp.float32),
            pltpu.VMEM((total // 2, width), low),
            pltpu.VMEM((total // 2, width), low),
            pltpu.VMEM((total // 2, width), jnp.float32),
            pltpu.VMEM((3, 8, 2, rows, side), low),
        ]
        + landing
        + sum_sems(len(LAST_STAGES))
        + [dma, dma, dma((3,)), pltpu.VMEM((5, 16, width), jnp.float32), dma((5,)), dma((5,)), dma((2, 6))],
        compiler_params=pltpu.CompilerParams(
            vmem_limit_bytes=KERNEL_VMEM, collective_id=4, has_side_effects=True
        ),
        name="finish",
    )(*grad_parts, x2, wqkv, grad_resid, vecs, part_sums, late, first, small, parts)


def update_kernel(*refs):
    groups = [refs[3 * i : 3 * i + 3] for i in range(4)]
    late_ref, first_ref, y_in, y_got, xg_in = refs[12:17]
    outs = [refs[17 + 3 * i : 20 + 3 * i] for i in range(4)]
    y_out, xg_out = refs[29:31]
    wide, share, through, in_sem, out_sem, t_sem = refs[31:]
    me = lax.axis_index("ctx")
    side = wide.shape[2]
    width = 2 * side
    slots = wide.shape[0]
    ahead = slots // 2
    half = through.shape[1]
    passing = [
        (y_in.at[pl.ds(0, half)], through.at[0], y_out.at[me]),
        (y_got, through.at[1], y_out.at[1 - me]),
    ] + [(xg_in.at[part], through.at[2 + part], xg_out.at[part]) for part in range(2)]
    brought = [
        local_copy(source, held, t_sem.at[0, k]) for k, (source, held, _) in enumerate(passing)
    ]
    taken = [
        local_copy(held, target, t_sem.at[1, k]) for k, (_, held, target) in enumerate(passing)
    ]

    def columns(at, size, into):
        return lambda ref: ref.at[:, pl.ds(at, size)], into, size

    units = []
    for c in range(4):
        rows = lambda ref, c=c: ref.at[pl.ds(c * side, side)]
        units.append((3, [(rows, 0, width)], [(late_ref.at[0, c], 0, width)], False))
        halves = [columns((c + 4 * j) * side, side, j * side) for j in range(2)]
        units.append((2, halves, [(late_ref.at[1, c], 0, width)], False))
    for k in range(4):
        shares = [(first_ref.at[part, k], part * side, side) for part in range(2)]
        if k == 0:
            units.append((1, [columns(0, width, 0)], shares, False))
        else:
            third = width // 3
            thirds = [
                columns(m * width + (k - 1) * third, third, m * third) for m in range(3)
            ]
            units.append((0, thirds, shares, True))

    def loads(index):
        which, spans, shares, _ = units[index]
        slot = index % slots
        copies = []
        for k in range(3):
            for part, (view, into, size) in enumerate(spans):
                copies.append(
                    local_copy(
                        view(groups[which][k]),
                        wide.at[slot, k, :, pl.ds(into, size)],
                        in_sem.at[index, k * 3 + part],
                    )
                )
        for part, (source, into, size) in enumerate(shares):
            copies.append(
                local_copy(source, share.at[slot, :, :, pl.ds(into, size)], in_sem.at[index, 9 + part])
            )
        return copies

    def stores(index):
        which, spans, _, _ = units[index]
        slot = index % slots
        return [
            local_copy(
                wide.at[slot, k, :, pl.ds(into, size)],
                view(outs[which][k]),
                out_sem.at[index, k * 3 + part],
            )
            for k in range(3)
            for part, (view, into, size) in enumerate(spans)
        ]

    def compute(index):
        slot, pairs = index % slots, units[index][3]
        rows = share.shape[2]

        @pl.loop(0, 8)
        def _(block):
            gradient = share[slot, block].astype(jnp.float32)
            if pairs:
                piece = 2 * HD
                gradient = jnp.concatenate(
                    [
                        gradient[:, part * side + m * piece : part * side + (m + 1) * piece]
                        for m in range(3)
                        for part in range(2)
                    ],
                    axis=1,
                )
            span = pl.ds(pl.multiple_of(block * rows, 16), rows)
            weight, first, second = (wide[slot, k, span, :] for k in range(3))
            new = adam_update(weight, gradient, first, second, matrix_rate, matrix_decay)
            wide[slot, 0, span, :] = new[2]
            wide[slot, 1, span, :] = new[0]
            wide[slot, 2, span, :] = new[1]

    for index in range(ahead):
        for copy in loads(index):
            copy.start()
    for copy in brought:
        copy.start()
    for index in range(len(units)):
        if index + ahead < len(units):
            if index + ahead >= slots:
                for copy in stores(index + ahead - slots):
                    copy.wait()
            for copy in loads(index + ahead):
                copy.start()
        for copy in loads(index):
            copy.wait()
        compute(index)
        for copy in stores(index):
            copy.start()
        if index == 2:
            for copy in brought:
                copy.wait()
            for copy in taken:
                copy.start()
    for index in range(len(units) - slots, len(units)):
        for copy in stores(index):
            copy.wait()
    for copy in taken:
        copy.wait()


def update_call(groups, late, first, y_rows, y_got, x_grad):
    flat = [member for group in groups for member in group]
    anywhere = pl.BlockSpec(memory_space=pl.ANY)
    side, width = groups[1][0].shape
    dma = pltpu.SemaphoreType.DMA
    shapes = [jax.ShapeDtypeStruct(member.shape, member.dtype) for member in flat]
    *new, y_new, x_new = pl.pallas_call(
        update_kernel,
        in_specs=[anywhere] * 17,
        out_specs=[anywhere] * 14,
        out_shape=shapes
        + [jax.ShapeDtypeStruct(x_grad.shape, x_grad.dtype)] * 2,
        scratch_shapes=[
            pltpu.VMEM((6, 3, side, width), jnp.float32),
            pltpu.VMEM((6, 8, side // 8, width), jnp.bfloat16),
            pltpu.VMEM((4,) + y_got.shape, jnp.bfloat16),
            dma((12, 11)),
            dma((12, 9)),
            dma((2, 4)),
        ],
        compiler_params=pltpu.CompilerParams(vmem_limit_bytes=KERNEL_VMEM),
        name="update",
    )(*flat, late, first, y_rows, y_got, x_grad)
    return new, y_new, x_new


def middle_kernel(
    att_ref, x_ref, grad_ref, got_ref, vec_ref, wo_ref, mine_ref, other_ref,
    y_out, gr_out, ga_out, partial_ref, go_ref, sums_ref,
    y_ref, gr_ref, ga_ref, up_w, down_w, g_ref, mlp, upstream, acts, grads_pre, grads, total, *rest,
):
    landing, rest = rest[:-6], rest[-6:]
    s_send, s_recv, s_local, w_sem, x_sem, o_sem = rest
    bits = own_bits()
    me, core = bits["y"], bits["core"]
    rows, width = g_ref.shape
    half = rows // 2
    side = width // 2
    chunks = total.shape[0]
    piece = total.shape[3]
    resid, low_rows = gr_ref, ga_ref
    streams, cores, held = [], [], list(landing[2:])
    for index, stages in enumerate(MIDDLE_STAGES):
        buffers = {stage: held.pop(0) for stage in stages}
        sems = (s_send.at[index], s_recv.at[index], s_local.at[index])
        streams.append(StreamSum(total.at[index], buffers, None, *sems))
        cores.append(
            CoreSum(
                grads, total.at[index], landing[index % 2], s_send.at[index, 0], s_recv.at[index, 0]
            )
        )

    own_x = local_copy(x_ref, y_ref, x_sem.at[0])
    own_x.start()
    loads = [
        local_copy(grad_ref.at[me], g_ref.at[pl.ds(0, half)], x_sem.at[1]),
        local_copy(got_ref, g_ref.at[pl.ds(half, half)], x_sem.at[2]),
    ]
    for index, (source, at) in enumerate(((mine_ref, me), (other_ref, 1 - me))):
        for c in range(chunks):
            part = pl.ds(pl.multiple_of(c * width + at * side, 16), side)
            loads.append(
                local_copy(source.at[pl.ds(c * side, side)], down_w.at[part], w_sem.at[index, c])
            )
            part = pl.ds(pl.multiple_of(at * side, 16), side)
            loads.append(
                local_copy(
                    source.at[pl.ds((chunks + c) * side, side)],
                    up_w.at[part, pl.ds(c * width, width)],
                    w_sem.at[index, chunks + c],
                )
            )
    for load in loads:
        load.start()
    meet_partners()
    own_x.wait()
    gain = vec_ref[5:6, :]
    step = rows // 7

    resid[...] = lax.dot_general(att_ref[...], wo_ref[...], NN, preferred_element_type=jnp.float32)

    @pl.loop(0, 7)
    def _(index):
        span = pl.ds(pl.multiple_of(index * step, 16), step)
        resid[span, :] = y_ref[span, :].astype(jnp.float32) + (resid[span, :] + vec_ref[4:5, :])
        normed_two, _, _ = normalize(resid[span, :], gain, vec_ref[6:7, :])
        low_rows[span, :] = normed_two.astype(jnp.bfloat16)

    for load in loads:
        load.wait()
    sums_ref[...] = jnp.zeros_like(sums_ref)
    mlp[...] = jnp.zeros_like(mlp)
    upstream[...] = jnp.zeros_like(upstream)

    def column_sum(values):
        return jnp.sum(values, axis=0, keepdims=True)

    @pl.loop(0, chunks)
    def _(c):
        cols = pl.ds(pl.multiple_of(c * width, 128), width)
        shift = vec_ref[pl.ds(12 + c, 1), :]
        for part in range(2):
            span = slice(part * half, (part + 1) * half)
            pre = (
                lax.dot_general(
                    low_rows[span, :], up_w[:, cols], NN, preferred_element_type=jnp.float32
                )
                + shift
            )
            below = normal_cdf(pre)
            acts[span, :] = (pre * below).astype(jnp.bfloat16)
            density = jnp.exp(-0.5 * pre * pre) * 0.3989422804014327
            grad_act = lax.dot_general(
                g_ref[span, :], down_w[cols, :], NT, preferred_element_type=jnp.float32
            )
            grad_pre = (grad_act * (below + pre * density)).astype(jnp.bfloat16)
            grads_pre[span, :] = grad_pre
            sums_ref[pl.ds(12 + c, 1), :] += column_sum(grad_pre.astype(jnp.float32))
            mlp[span, :] += lax.dot_general(
                acts[span, :], down_w[cols, :], NN, preferred_element_type=jnp.float32
            )
            upstream[span, :] += lax.dot_general(
                grads_pre[span, :], up_w[:, cols], NT, preferred_element_type=jnp.float32
            )

        for chunk, moves in enumerate(MIDDLE_MOVES):
            @pl.when(c == chunk)
            def _(moves=moves):
                for index, stage in moves:
                    if stage == 0:
                        cores[index].finish()
                        streams[index].start(1)
                    else:
                        streams[index].move(stage)

        def put(which, values):
            for part in range(2):
                for block in range(8):
                    at = part * side + block * piece
                    grads[which, block, part] = values[at : at + piece, :].astype(jnp.bfloat16)

        put(0, lax.dot_general(acts[...], g_ref[...], TN, preferred_element_type=jnp.float32))
        put(
            1, lax.dot_general(low_rows[...], grads_pre[...], TN, preferred_element_type=jnp.float32)
        )
        for index in range(chunks):
            @pl.when(c == index)
            def _(index=index):
                cores[index].start()

    for c in range(chunks):
        at = slice(c % 2 * side, (c % 2 + 1) * side)
        sums_ref[8 + c // 2 : 9 + c // 2, at] = sums_ref[12 + c : 13 + c, :side]
        sums_ref[10 + c // 2 : 11 + c // 2, at] = sums_ref[12 + c : 13 + c, side:]

    @pl.loop(0, 7)
    def _(index):
        span = pl.ds(pl.multiple_of(index * step, 16), step)
        y_ref[span, :] = (resid[span, :] + mlp[span, :] + vec_ref[7:8, :]).astype(jnp.bfloat16)
        _, normed, inverse = normalize(resid[span, :], gain, vec_ref[6:7, :])
        coming = upstream[span, :]
        grads_out = g_ref[span, :].astype(jnp.float32)
        sums_ref[5:6, :] += column_sum(coming * normed)
        sums_ref[6:7, :] += column_sum(coming)
        sums_ref[7:8, :] += column_sum(grads_out)
        grad_resid = grads_out + norm_back(coming, gain, normed, inverse)
        gr_ref[span, :] = grad_resid
        acts[span, :] = grad_resid.astype(jnp.bfloat16)
        sums_ref[4:5, :] += column_sum(acts[span, :].astype(jnp.float32))

    leaving = []

    def leave(source, target):
        copy = local_copy(source, target, o_sem.at[len(leaving)])
        copy.start()
        leaving.append(copy)

    leave(y_ref, y_out)
    leave(gr_ref, gr_out)
    cores[3].finish()
    leave(total.at[3], partial_ref.at[3])
    streams[0].finish(3)
    leave(total.at[0], partial_ref.at[0])
    ga_ref[...] = lax.dot_general(
        acts[...], wo_ref[...], NT, preferred_element_type=jnp.float32
    ).astype(jnp.bfloat16)
    leave(ga_ref, ga_out)
    branch_grad = lax.dot_general(
        att_ref[...], acts[...], TN, preferred_element_type=jnp.float32
    ).astype(jnp.bfloat16)
    for part in range(2):
        for sides in range(2):
            for block in range(8):
                at = sides * side + block * piece
                go_ref[part, block, sides] = branch_grad[
                    at : at + piece, part * side : (part + 1) * side
                ]
    for index, stage in ((1, 2), (2, 1)):
        streams[index].finish(stage)
        leave(total.at[index], partial_ref.at[index])
    for copy in leaving:
        copy.wait()


MIDDLE_STAGES = ((1, 2, 3), (1, 2), (1,), ())
MIDDLE_MOVES = ((), ((0, 0),), ((0, 1), (1, 0)), ((0, 2), (1, 1), (2, 0)))


def middle_call(attended, x_rows, out_grad, grad_got, vecs, out_low, mine, other):
    rows, width = x_rows.shape
    hidden = mine.shape[0]
    low = jnp.bfloat16
    anywhere = pl.BlockSpec(memory_space=pl.ANY)
    vmem = pl.BlockSpec(memory_space=pltpu.VMEM)
    dma = pltpu.SemaphoreType.DMA
    chunks = len(MIDDLE_STAGES)
    piece = hidden // (2 * chunks * 8)
    landing = landing_shapes((0, 0), piece, width)
    for stages in MIDDLE_STAGES:
        landing += landing_shapes(stages, piece, width)
    return pl.pallas_call(
        middle_kernel,
        in_specs=[vmem, anywhere, anywhere, anywhere, vmem, vmem, anywhere, anywhere],
        out_specs=[anywhere] * 4 + [vmem] * 2,
        out_shape=[
            jax.ShapeDtypeStruct((rows, width), low),
            jax.ShapeDtypeStruct((rows, width), jnp.float32),
            jax.ShapeDtypeStruct((rows, width), low),
            jax.ShapeDtypeStruct((chunks, 8, 2, piece, width), low),
            jax.ShapeDtypeStruct((2, 8, 2, piece, width // 2), low),
            jax.ShapeDtypeStruct((16, width), jnp.float32),
        ],
        scratch_shapes=[
            pltpu.VMEM((rows, width), low),
            pltpu.VMEM((rows, width), jnp.float32),
            pltpu.VMEM((rows, width), low),
            pltpu.VMEM((width, hidden), low),
            pltpu.VMEM((hidden, width), low),
            pltpu.VMEM((rows, width), low),
            pltpu.VMEM((rows, width), jnp.float32),
            pltpu.VMEM((rows, width), jnp.float32),
            pltpu.VMEM((rows, hidden // chunks), low),
            pltpu.VMEM((rows, hidden // chunks), low),
            pltpu.VMEM((2, 8, 2, piece, width), low),
            pltpu.VMEM((chunks, 8, 2, piece, width), low),
        ]
        + landing
        + sum_sems(chunks)
        + [dma((2, 2 * chunks)), dma((3,)), dma((7,))],
        compiler_params=pltpu.CompilerParams(
            vmem_limit_bytes=KERNEL_VMEM, collective_id=5, has_side_effects=True
        ),
        name="middle",
    )(attended, x_rows, out_grad, grad_got, vecs, out_low, mine, other)


def per_device_clips(
    x_tokens,
    out_grad,
    w_qkv,
    w_out,
    w_up,
    w_down,
    vectors,
    qkv_mean,
    qkv_square,
    out_mean,
    out_square,
    up_mean,
    up_square,
    down_mean,
    down_square,
    vectors_mean,
    vectors_square,
):
    me = lax.axis_index("ctx")
    width = x_tokens.shape[2]
    side = width // 2
    vector_own = jnp.pad(
        vectors.astype(jnp.bfloat16).astype(jnp.float32), ((0, 4), (0, 0))
    )
    x_low, projected, qkv_low, out_low, vector_rows, norm_rows, late_weights = start_call(
        x_tokens, vector_own, w_qkv, w_out, w_up, w_down
    )
    attended_low, inverse_total, exponent, late_other, grad_got = attend_call(
        projected, late_weights, out_grad, width
    )
    y_rows, grad_resid, grad_attended, partial, grad_out, part_sums = middle_call(
        attended_low,
        x_low,
        out_grad,
        grad_got,
        vector_rows,
        out_low,
        late_weights.reshape(-1, width),
        late_other.reshape(-1, width),
    )
    *grad_parts, late, first, y_got, small, last_parts = attend_back_call(
        projected,
        grad_attended,
        attended_low,
        inverse_total,
        exponent,
        partial,
        y_rows,
        norm_rows,
        grad_out,
    )
    x_grad, summed_vectors, late_shared, first_shared = finish_call(
        grad_parts,
        x_low,
        qkv_low,
        grad_resid,
        vector_rows,
        part_sums,
        late,
        first,
        small,
        last_parts,
    )

    vector_share = lax.dynamic_slice_in_dim(summed_vectors[:12], me * side, side, axis=1)

    weights, y_tokens, x_grad = update_call(
        (
            (w_qkv, qkv_mean, qkv_square),
            (w_out, out_mean, out_square),
            (w_up, up_mean, up_square),
            (w_down, down_mean, down_square),
        ),
        late_shared,
        first_shared,
        y_rows,
        y_got,
        x_grad,
    )
    qkv_new, out_new, up_new, down_new = (
        (weights[3 * i + 1], weights[3 * i + 2], weights[3 * i]) for i in range(4)
    )
    vectors_new = adam_update(
        vectors, vector_share, vectors_mean, vectors_square, vector_rate, 0.0
    )
    return (y_tokens, x_grad) + qkv_new + out_new + up_new + down_new + vectors_new


def per_device(x_tokens, *others):
    clips = x_tokens.shape[0]
    if lax.axis_size("ctx") == 2 and lax.axis_size("dp") == 16 and clips == 2:
        return per_device_clips(x_tokens, *others)
    return per_device_split(x_tokens, *others)


def solution(mesh):
    return jax.shard_map(
        per_device,
        mesh=mesh,
        in_specs=(
            P("dp", "ctx", None),
            P("dp", "ctx", None),
            P("ctx", None),
            P("ctx", None),
            P("ctx", None),
            P("ctx", None),
            P(None, "ctx"),
            P("ctx", None),
            P("ctx", None),
            P("ctx", None),
            P("ctx", None),
            P("ctx", None),
            P("ctx", None),
            P("ctx", None),
            P("ctx", None),
            P(None, "ctx"),
            P(None, "ctx"),
        ),
        out_specs=(
            P("dp", "ctx", None),
            P("dp", "ctx", None),
            P("ctx", None),
            P("ctx", None),
            P("ctx", None),
            P("ctx", None),
            P("ctx", None),
            P("ctx", None),
            P("ctx", None),
            P("ctx", None),
            P("ctx", None),
            P("ctx", None),
            P("ctx", None),
            P("ctx", None),
            P(None, "ctx"),
            P(None, "ctx"),
            P(None, "ctx"),
        ),
        check_vma=False,
    )
```

```python
import functools

import jax
import jax.numpy as jnp
from jax import lax
from jax.experimental import pallas as pl
from jax.experimental.pallas import tpu as pltpu
from jax.sharding import PartitionSpec as P

HD = 64
STEP = 10


norm_epsilon = 1e-06
adam_epsilon = 1e-08
matrix_rate = 0.04
matrix_decay = 0.05
vector_rate = 0.2


def normalize(values, norm_gain, norm_shift):
    row_mean = jnp.mean(values, axis=-1, keepdims=True)
    centred = values - row_mean
    row_var = jnp.mean(centred * centred, axis=-1, keepdims=True)
    inverse = lax.rsqrt(row_var + norm_epsilon)
    normed = centred * inverse
    return (normed * norm_gain + norm_shift, normed, inverse)


def norm_back(upstream, norm_gain, normed, inverse):
    scaled = upstream * norm_gain
    first_mean = jnp.mean(scaled, axis=-1, keepdims=True)
    second_mean = jnp.mean(scaled * normed, axis=-1, keepdims=True)
    return inverse * (scaled - first_mean - normed * second_mean)


def normal_cdf(values):
    return 0.5 * (1.0 + lax.erf(values * 0.7071067811865476))


def attend(operands):
    query_block, key_block, value_block = operands
    scores = (
        jnp.einsum("qhd,khd->hqk", query_block, key_block, preferred_element_type=jnp.float32)
        * 0.125
    )
    peak_score = jnp.max(scores, axis=-1, keepdims=True)
    exponent = jnp.exp(scores - peak_score)
    totals = jnp.sum(exponent, axis=-1, keepdims=True)
    probs_low = (exponent / totals).astype(jnp.bfloat16)
    attended = jnp.einsum(
        "hqk,khd->qhd", probs_low, value_block, preferred_element_type=jnp.float32
    )
    return (attended, peak_score + jnp.log(totals))


def attend_back(operands):
    query_block, key_block, value_block, log_total, grad_block = operands
    scores = (
        jnp.einsum("qhd,khd->hqk", query_block, key_block, preferred_element_type=jnp.float32)
        * 0.125
    )
    probs = jnp.exp(scores - log_total)
    grad_probs = jnp.einsum(
        "qhd,khd->hqk", grad_block, value_block, preferred_element_type=jnp.float32
    )
    delta = jnp.sum(probs * grad_probs, axis=-1, keepdims=True)
    grad_scores = (probs * (grad_probs - delta)).astype(jnp.bfloat16)
    grad_query = (
        jnp.einsum("hqk,khd->qhd", grad_scores, key_block, preferred_element_type=jnp.float32)
        * 0.125
    )
    grad_key = (
        jnp.einsum("hqk,qhd->khd", grad_scores, query_block, preferred_element_type=jnp.float32)
        * 0.125
    )
    grad_value = jnp.einsum(
        "hqk,qhd->khd", probs.astype(jnp.bfloat16), grad_block, preferred_element_type=jnp.float32
    )
    return (grad_query, grad_key, grad_value)


def adam_update(weight, gradient, first_old, second_old, step_rate, decay_rate):
    first_new = 0.5 * first_old + 0.5 * gradient
    second_new = 0.5 * second_old + 0.5 * gradient * gradient
    correction = 1.0 - 0.5**STEP
    update = (
        first_new / correction / (jnp.sqrt(second_new / correction) + adam_epsilon)
        + decay_rate * weight
    )
    return (first_new, second_new, weight - step_rate * update)


def per_device_split(
    x_tokens,
    out_grad,
    w_qkv,
    w_out,
    w_up,
    w_down,
    vectors,
    qkv_mean,
    qkv_square,
    out_mean,
    out_square,
    up_mean,
    up_square,
    down_mean,
    down_square,
    vectors_mean,
    vectors_square,
):
    masters = (w_qkv, w_out, w_up, w_down, vectors)
    lowered = tuple((member.astype(jnp.bfloat16) for member in masters))
    qkv_low, out_low, up_low, down_low, vector_low = (
        lax.all_gather(lowered[0], "ctx", axis=0, tiled=True),
        lax.all_gather(lowered[1], "ctx", axis=0, tiled=True),
        lax.all_gather(lowered[2], "ctx", axis=0, tiled=True),
        lax.all_gather(lowered[3], "ctx", axis=0, tiled=True),
        lax.all_gather(lowered[4], "ctx", axis=1, tiled=True),
    )
    vector_rows = vector_low.astype(jnp.float32)
    clip_count, row_count, model_width = x_tokens.shape
    head_count = model_width // HD
    token_total = clip_count * row_count
    flat_rows = x_tokens.reshape(token_total, model_width).astype(jnp.float32)
    norm_one, normed_one, inverse_one = normalize(flat_rows, vector_rows[0], vector_rows[1])
    norm_one_low = norm_one.astype(jnp.bfloat16)
    qkv_shift = jnp.concatenate([vector_rows[2], jnp.zeros_like(vector_rows[2]), vector_rows[3]])
    projected = (
        jnp.dot(norm_one_low, qkv_low, preferred_element_type=jnp.float32) + qkv_shift
    ).astype(jnp.bfloat16)
    query_rows = projected[:, :model_width].reshape(clip_count, row_count, head_count, HD)
    key_local = projected[:, model_width : 2 * model_width].reshape(
        clip_count, row_count, head_count, HD
    )
    value_local = projected[:, 2 * model_width :].reshape(clip_count, row_count, head_count, HD)
    key_rows, value_rows = (
        lax.all_gather(key_local, "ctx", axis=1, tiled=True),
        lax.all_gather(value_local, "ctx", axis=1, tiled=True),
    )
    attended, log_total = lax.map(attend, (query_rows, key_rows, value_rows))
    attended_low = attended.reshape(token_total, model_width).astype(jnp.bfloat16)
    branch = jnp.dot(attended_low, out_low, preferred_element_type=jnp.float32) + vector_rows[4]
    resid = flat_rows + branch
    norm_two, normed_two, inverse_two = normalize(resid, vector_rows[5], vector_rows[6])
    norm_two_low = norm_two.astype(jnp.bfloat16)
    pre_act = jnp.dot(norm_two_low, up_low, preferred_element_type=jnp.float32) + vector_rows[
        8:
    ].reshape(-1)
    act_low = (pre_act * normal_cdf(pre_act)).astype(jnp.bfloat16)
    mlp_out = jnp.dot(act_low, down_low, preferred_element_type=jnp.float32) + vector_rows[7]
    y_tokens = (resid + mlp_out).astype(jnp.bfloat16).reshape(clip_count, row_count, model_width)
    grad_output = out_grad.reshape(token_total, model_width)
    grad_float = grad_output.astype(jnp.float32)
    grad_down = jnp.einsum("tf,td->fd", act_low, grad_output, preferred_element_type=jnp.float32)
    down_shift = jnp.sum(grad_float, axis=0)
    grad_act = jnp.dot(grad_output, down_low.T, preferred_element_type=jnp.float32)
    density = jnp.exp(-0.5 * pre_act * pre_act) * 0.3989422804014327
    grad_pre = (grad_act * (normal_cdf(pre_act) + pre_act * density)).astype(jnp.bfloat16)
    grad_up = jnp.einsum("td,tf->df", norm_two_low, grad_pre, preferred_element_type=jnp.float32)
    up_shift = jnp.sum(grad_pre.astype(jnp.float32), axis=0)
    grad_norm_two = jnp.dot(grad_pre, up_low.T, preferred_element_type=jnp.float32)
    gain_two_grad = jnp.sum(grad_norm_two * normed_two, axis=0)
    shift_two_grad = jnp.sum(grad_norm_two, axis=0)
    grad_resid = grad_float + norm_back(grad_norm_two, vector_rows[5], normed_two, inverse_two)
    grad_branch = grad_resid.astype(jnp.bfloat16)
    grad_out = jnp.einsum(
        "td,te->de", attended_low, grad_branch, preferred_element_type=jnp.float32
    )
    out_shift = jnp.sum(grad_branch.astype(jnp.float32), axis=0)
    grad_attended = jnp.dot(grad_branch, out_low.T, preferred_element_type=jnp.float32).astype(
        jnp.bfloat16
    )
    grad_attended = grad_attended.reshape(clip_count, row_count, head_count, HD)
    grad_query, key_terms, value_terms = lax.map(
        attend_back, (query_rows, key_rows, value_rows, log_total, grad_attended)
    )
    grad_key, grad_value = (
        lax.psum_scatter(
            key_terms.astype(jnp.bfloat16), "ctx", scatter_dimension=1, tiled=True
        ).astype(jnp.float32),
        lax.psum_scatter(
            value_terms.astype(jnp.bfloat16), "ctx", scatter_dimension=1, tiled=True
        ).astype(jnp.float32),
    )
    grad_projected = jnp.concatenate(
        [
            grad_query.reshape(token_total, model_width),
            grad_key.reshape(token_total, model_width),
            grad_value.reshape(token_total, model_width),
        ],
        axis=1,
    ).astype(jnp.bfloat16)
    grad_qkv = jnp.einsum(
        "td,te->de", norm_one_low, grad_projected, preferred_element_type=jnp.float32
    )
    projected_sums = jnp.sum(grad_projected.astype(jnp.float32), axis=0)
    grad_norm_one = jnp.dot(grad_projected, qkv_low.T, preferred_element_type=jnp.float32)
    gain_one_grad = jnp.sum(grad_norm_one * normed_one, axis=0)
    shift_one_grad = jnp.sum(grad_norm_one, axis=0)
    x_grad = (
        grad_resid + norm_back(grad_norm_one, vector_rows[0], normed_one, inverse_one)
    ).astype(jnp.bfloat16)
    x_grad = x_grad.reshape(clip_count, row_count, model_width)
    first_rows = jnp.stack(
        [
            gain_one_grad,
            shift_one_grad,
            projected_sums[:model_width],
            projected_sums[2 * model_width :],
            out_shift,
            gain_two_grad,
            shift_two_grad,
            down_shift,
        ]
    )
    grad_vectors = jnp.concatenate([first_rows, up_shift.reshape(-1, model_width)], axis=0)
    group_size = lax.axis_size("ctx")
    vector_count = grad_vectors.shape[0]
    flat_vectors = (
        grad_vectors.reshape(vector_count, group_size, -1)
        .transpose(1, 0, 2)
        .reshape(group_size, -1)
    )
    shaped = (grad_qkv, grad_out, grad_up, grad_down, flat_vectors)
    spread = (
        lax.psum_scatter(
            shaped[0].astype(jnp.bfloat16), "dp", scatter_dimension=1, tiled=True
        ).astype(jnp.float32),
        lax.psum_scatter(
            shaped[1].astype(jnp.bfloat16), "dp", scatter_dimension=1, tiled=True
        ).astype(jnp.float32),
        lax.psum_scatter(
            shaped[2].astype(jnp.bfloat16), "dp", scatter_dimension=1, tiled=True
        ).astype(jnp.float32),
        lax.psum_scatter(
            shaped[3].astype(jnp.bfloat16), "dp", scatter_dimension=1, tiled=True
        ).astype(jnp.float32),
        lax.psum_scatter(
            shaped[4].astype(jnp.bfloat16), "dp", scatter_dimension=1, tiled=True
        ).astype(jnp.float32),
    )
    owned = (
        lax.psum_scatter(
            spread[0].astype(jnp.bfloat16), "ctx", scatter_dimension=0, tiled=True
        ).astype(jnp.float32),
        lax.psum_scatter(
            spread[1].astype(jnp.bfloat16), "ctx", scatter_dimension=0, tiled=True
        ).astype(jnp.float32),
        lax.psum_scatter(
            spread[2].astype(jnp.bfloat16), "ctx", scatter_dimension=0, tiled=True
        ).astype(jnp.float32),
        lax.psum_scatter(
            spread[3].astype(jnp.bfloat16), "ctx", scatter_dimension=0, tiled=True
        ).astype(jnp.float32),
        lax.psum_scatter(
            spread[4].astype(jnp.bfloat16), "ctx", scatter_dimension=0, tiled=True
        ).astype(jnp.float32),
    )
    collected = (
        lax.all_gather(owned[0].astype(jnp.bfloat16), "dp", axis=1, tiled=True).astype(jnp.float32),
        lax.all_gather(owned[1].astype(jnp.bfloat16), "dp", axis=1, tiled=True).astype(jnp.float32),
        lax.all_gather(owned[2].astype(jnp.bfloat16), "dp", axis=1, tiled=True).astype(jnp.float32),
        lax.all_gather(owned[3].astype(jnp.bfloat16), "dp", axis=1, tiled=True).astype(jnp.float32),
        lax.all_gather(owned[4].astype(jnp.bfloat16), "dp", axis=1, tiled=True).astype(jnp.float32),
    )
    shares = (
        collected[0],
        collected[1],
        collected[2],
        collected[3],
        collected[4].reshape(vector_count, -1),
    )
    qkv_moment, qkv_second, qkv_master = adam_update(
        w_qkv, shares[0], qkv_mean, qkv_square, matrix_rate, matrix_decay
    )
    out_moment, out_second, out_master = adam_update(
        w_out, shares[1], out_mean, out_square, matrix_rate, matrix_decay
    )
    up_moment, up_second, up_master = adam_update(
        w_up, shares[2], up_mean, up_square, matrix_rate, matrix_decay
    )
    down_moment, down_second, down_master = adam_update(
        w_down, shares[3], down_mean, down_square, matrix_rate, matrix_decay
    )
    vectors_moment, vectors_second, vectors_master = adam_update(
        vectors, shares[4], vectors_mean, vectors_square, vector_rate, 0.0
    )
    return (
        y_tokens,
        x_grad,
        qkv_moment,
        qkv_second,
        qkv_master,
        out_moment,
        out_second,
        out_master,
        up_moment,
        up_second,
        up_master,
        down_moment,
        down_second,
        down_master,
        vectors_moment,
        vectors_second,
        vectors_master,
    )


LOG2E = 1.4426950408889634
NT = (((1,), (1,)), ((), ()))
NN = (((1,), (0,)), ((), ()))
TN = (((0,), (0,)), ((), ()))
KERNEL_VMEM = 62 * 2**20


def attend_kernel(q_ref, k_ref, v_ref, o_ref, r_ref, p_ref, score_a, score_b, peak_a, peak_b):
    rows = score_a.shape[0]
    total = k_ref.shape[0]
    lane = lax.broadcasted_iota(jnp.int32, (1, 2 * HD), 1)
    held, peaks = (score_a, score_b), (peak_a, peak_b)
    parts = total // rows
    items = [(head, part) for head in range(2) for part in range(parts)]
    middle = total // 256 * 2 // 3 * 256
    upper = rows // 32 * 16 + 16

    def score(index, first, last):
        head, part = items[index]
        keys = jnp.where((lane // HD) == head, k_ref[...], 0).astype(jnp.bfloat16)[first:last]
        values = lax.dot_general(
            q_ref[part * rows : (part + 1) * rows, :], keys, NT, preferred_element_type=jnp.float32
        )
        held[index % 2][:, first:last] = values
        return jnp.max(values, axis=1, keepdims=True)

    def keep_peak(index, first, second):
        peaks[index % 2][...] = jnp.broadcast_to(jnp.maximum(first, second), (rows, 128))

    def soften(index, first, last):
        head, part = items[index]
        values = held[index % 2][first:last, :] - peaks[index % 2][first:last, 0:1]
        p_ref[head, part * rows + first : part * rows + last, :] = jnp.exp2(
            values * (0.125 * LOG2E)
        ).astype(jnp.bfloat16)

    def weigh(index):
        head, part = items[index]
        span = slice(part * rows, (part + 1) * rows)
        kept = jnp.where((lane // HD) == head, v_ref[...], 0).astype(jnp.bfloat16)
        table = jnp.concatenate([kept, jnp.ones((total, 2 * HD), jnp.bfloat16)], axis=1)
        out = lax.dot_general(p_ref[head, span, :], table, NN, preferred_element_type=jnp.float32)
        inverse = 1.0 / out[:, 2 * HD :]
        mixed = (out[:, : 2 * HD] * inverse).astype(jnp.bfloat16)
        if head == 0:
            o_ref[span, :] = mixed
            r_ref[span, :] = inverse
        else:
            o_ref[span, :] = jnp.where(lane < HD, o_ref[span, :], mixed)
            r_ref[span, :] = jnp.where(lane < HD, r_ref[span, :], inverse)

    keep_peak(0, score(0, 0, middle), score(0, middle, total))
    for index in range(len(items)):
        more = index + 1 < len(items)
        if more:
            first = score(index + 1, 0, middle)
        soften(index, 0, upper)
        if more:
            keep_peak(index + 1, first, score(index + 1, middle, total))
        soften(index, upper, rows)
        weigh(index)


def attend_back_kernel(
    q_ref, k_ref, v_ref, g_ref, o_ref, r_ref, p_ref, dq_ref, dk_ref, dv_ref, ds, qt, gt, dkt, dvt
):
    head = pl.program_id(1)
    total = k_ref.shape[0]
    half = total // 2
    lane = lax.broadcasted_iota(jnp.int32, (1, 2 * HD), 1)
    keep = (lane // HD) == head
    scaled = g_ref[...].astype(jnp.float32) * r_ref[...]

    @pl.when(head == 0)
    def _():
        qt[...] = q_ref[...].T
        gt[...] = scaled.astype(jnp.bfloat16).T

    delta = jnp.sum(jnp.where(keep, scaled * o_ref[...].astype(jnp.float32), 0.0), axis=1, keepdims=True)
    values = jnp.where(keep, v_ref[...], 0).astype(jnp.bfloat16)
    grad_probs = lax.dot_general(
        scaled.astype(jnp.bfloat16), values, NT, preferred_element_type=jnp.float32
    )
    ds[...] = (p_ref[...].astype(jnp.float32) * (grad_probs - delta)).astype(jnp.bfloat16)
    span = pl.ds(pl.multiple_of(head * HD, HD), HD)
    dvt[span, :] = lax.dot_general(gt[span, :], p_ref[...], NN, preferred_element_type=jnp.float32)
    dkt[span, :] = 0.125 * lax.dot_general(
        qt[span, :], ds[...], NN, preferred_element_type=jnp.float32
    )
    keys = jnp.where(keep, k_ref[...], 0).astype(jnp.bfloat16)
    for part in range(2):
        rows = slice(part * half, (part + 1) * half)
        term = 0.125 * lax.dot_general(ds[rows, :], keys, NN, preferred_element_type=jnp.float32)
        dq_ref[rows, :] = jnp.where(keep, term.astype(jnp.bfloat16), dq_ref[rows, :])

    @pl.when(head == 1)
    def _():
        dk_ref[...] = dkt[...].T.astype(jnp.bfloat16)
        dv_ref[...] = dvt[...].T.astype(jnp.bfloat16)


MESH = pl.DeviceIdType.MESH
GATHER_ORDERS = ("xab", "bxa", "abx")


def own_bits():
    place = lax.axis_index("dp")
    z = place // 4
    return {
        "z": z,
        "core": place % 2,
        "x": (place // 2) % 2,
        "a": (z % 2 + z // 2) % 2,
        "b": z // 2,
        "y": lax.axis_index("ctx"),
    }


def partner(name):
    place, group = lax.axis_index("dp"), lax.axis_index("ctx")
    z = place // 4
    if name == "core":
        return (place + 1 - 2 * (place % 2), group)
    if name == "x":
        return (place + 2 - 4 * ((place // 2) % 2), group)
    if name == "a":
        return (place + 4 - 8 * (z % 2), group)
    if name == "b":
        return (place + 4 * (3 - 2 * z), group)
    if name in ("z1", "z2", "z3"):
        return (place + 4 * ((z + int(name[1])) % 4 - z), group)
    return (place, 1 - group)


def meet_partners():
    barrier = pltpu.get_barrier_semaphore()
    names = ("core", "x", "y", "z1", "z2", "z3")
    for name in names:
        pl.semaphore_signal(barrier, inc=1, device_id=partner(name), device_id_type=MESH)
    pl.semaphore_wait(barrier, len(names))


def remote(source, target, name, send_sem, recv_sem):
    return pltpu.make_async_remote_copy(
        src_ref=source,
        dst_ref=target,
        send_sem=send_sem,
        recv_sem=recv_sem,
        device_id=partner(name),
        device_id_type=MESH,
    )


def local_copy(source, target, sem):
    return pltpu.make_async_copy(source, target, sem)


def block_of(order, bits):
    first, second, third = (bits[name] for name in order if name != "y")
    return first * 4 + second * 2 + third


class Gather:
    stages = 4

    def __init__(self, buffer, orders, send, recv):
        self.buffer, self.orders, self.send, self.recv = buffer, orders, send, recv

    def copy(self, stage, stream):
        bits = own_bits()
        order = self.orders[stream].replace("y", "")
        block = block_of(order, bits)
        size = (1, 2, 4, 8)[stage]
        name = "core" if stage == 3 else order[2 - stage]
        region = self.buffer.at[bits["core"], stream, pl.ds(block // size * size, size)]
        return remote(region, region, name, self.send.at[stage, stream], self.recv.at[stage, stream])

    def start(self, stage, stream):
        self.copy(stage, stream).start()

    def advance(self, stage, stream):
        self.copy(stage, stream).wait()
        if stage + 1 < self.stages:
            self.copy(stage + 1, stream).start()

    def begin(self):
        for stream in range(len(self.orders)):
            self.start(0, stream)

    def advance_all(self, stage):
        for stream in range(len(self.orders)):
            self.advance(stage, stream)


class StreamSum:
    def __init__(self, total, landing, shared, send, recv, local):
        self.total, self.landing, self.shared = total, landing, shared
        self.send, self.recv, self.local = send, recv, local

    def copies(self, stage):
        bits = own_bits()
        x, y, z = bits["x"], bits["y"], bits["z"]

        def make(source, target, name, at):
            return remote(source, target, name, self.send.at[at], self.recv.at[at])

        if stage == 1:
            return [make(self.total.at[:, 1 - y], self.landing[1], "y", 1)]
        if stage == 2:
            return [make(self.total.at[pl.ds((1 - x) * 4, 4), y], self.landing[2], "x", 2)]
        if stage == 3:
            return [
                make(
                    self.total.at[x * 4 + (z + d) % 4, y],
                    self.landing[3].at[d - 1],
                    "z" + str(d),
                    2 + d,
                )
                for d in (1, 2, 3)
            ]
        if stage == 4:
            return [
                make(
                    self.total.at[x * 4 + z, y],
                    self.shared.at[x * 4 + z],
                    "z" + str(d),
                    5 + d,
                )
                for d in (1, 2, 3)
            ]
        if stage == 5:
            region = self.shared.at[pl.ds(x * 4, 4)]
            return [make(region, region, "x", 9)]
        return [make(self.shared, self.shared, "core", 10)]

    def own_copy(self):
        bits = own_bits()
        block = bits["x"] * 4 + bits["z"]
        return local_copy(self.total.at[block, bits["y"]], self.shared.at[block], self.local)

    def start(self, stage):
        for copy in self.copies(stage):
            copy.start()
        if stage == 4:
            self.own_copy().start()

    def finish(self, stage):
        for copy in self.copies(stage):
            copy.wait()
        if stage == 4:
            self.own_copy().wait()
        if stage > 3:
            return
        bits = own_bits()
        x, y, z = bits["x"], bits["y"], bits["z"]
        start, size = ((0, 8), (x * 4, 4), (x * 4 + z, 1))[stage - 1]
        landed = self.landing[stage]

        @pl.loop(0, size)
        def _(block):
            here = self.total[start + block, y].astype(jnp.float32)
            if stage == 3:
                for d in range(3):
                    here = here + landed[d].astype(jnp.float32)
            else:
                here = here + landed[block].astype(jnp.float32)
            self.total[start + block, y] = here.astype(jnp.bfloat16)

    def move(self, stage):
        self.finish(stage)
        if stage < 6:
            self.start(stage + 1)


class CoreSum:
    def __init__(self, parts, total, landed, send, recv, local=None):
        self.parts, self.total, self.landed = parts, total, landed
        self.send, self.recv, self.local = send, recv, local

    def copy(self):
        away = 1 - own_bits()["core"]
        return remote(self.parts.at[away], self.landed, "core", self.send, self.recv)

    def start(self):
        self.copy().start()

    def finish(self):
        self.copy().wait()
        core = own_bits()["core"]

        @pl.loop(0, 8)
        def _(block):
            self.total[block] = (
                self.parts[core, block].astype(jnp.float32) + self.landed[block].astype(jnp.float32)
            ).astype(jnp.bfloat16)


def landing_shapes(stages, rows, columns):
    leads = {0: (8, 2), 1: (8,), 2: (4,), 3: (3,)}
    return [pltpu.VMEM(leads[stage] + (rows, columns), jnp.bfloat16) for stage in stages]


def sum_sems(streams):
    dma = pltpu.SemaphoreType.DMA
    return [dma((streams, 11)), dma((streams, 11)), dma((streams,))]


def gather_sems(streams):
    return [pltpu.SemaphoreType.DMA((4, streams)), pltpu.SemaphoreType.DMA((4, streams))]


def start_kernel(
    x_ref, vec_ref, wqkv_in, wout_in, wup_in, wdown_in,
    x2_out, proj_out, wqkv_out, wout_out, vecs_ref, norm_out, late_out, late_other,
    x2_ref, proj_ref, wqkv_ref, wout_ref, norm, late_ref, w_ref, other, wide, vec_other, g_send, g_recv, w_send, w_recv, x_send, x_recv, v_sem, l_sem, f_sem, o_sem,
    p_send, p_recv,
):
    bits = own_bits()
    me = bits["y"]
    half, width = x_ref.shape[1], x_ref.shape[2]
    gather = Gather(other, GATHER_ORDERS, g_send, g_recv)
    side = width // 2
    leaving = []

    def leave(source, target):
        copy = local_copy(source, target, o_sem.at[len(leaving)])
        copy.start()
        leaving.append(copy)

    def leave_rows(source, target, at, size):
        leave(source.at[pl.ds(at, size)], target.at[pl.ds(at, size)])

    pieces_in = [[(wqkv_in.at[:, pl.ds(i * width, width)], 0, width)] for i in range(3)]
    pieces_in.append([(wout_in, 0, width)])
    pieces_in += [[(wdown_in.at[pl.ds(i * side, side)], 0, width)] for i in range(4)]
    pieces_in += [
        [(wup_in.at[:, pl.ds((i + 4 * j) * side, side)], j * side, side) for j in range(2)]
        for i in range(4)
    ]

    def fetch(index):
        slot = index % 4
        return [
            local_copy(source, wide.at[slot, :, pl.ds(at, size)], f_sem.at[index, k])
            for k, (source, at, size) in enumerate(pieces_in[index])
        ]

    def lower(index):
        for copy in fetch(index):
            copy.wait()
        rows = 32 if index < 4 else 64
        target = w_ref if index < 4 else late_ref
        count = side // rows
        for block in range(count):
            flat = index % 4 * count + block if index < 4 else (index - 4) * count + block
            target[flat // 24, flat // 8 % 3, flat % 8] = wide[
                index % 4, block * rows : (block + 1) * rows, :
            ].astype(jnp.bfloat16)
        if index + 4 < len(pieces_in):
            for copy in fetch(index + 4):
                copy.start()

    for index in range(4):
        for copy in fetch(index):
            copy.start()
    meet_partners()
    vec_copy = remote(vec_ref, vec_other, "y", v_sem.at[0], v_sem.at[1])
    vec_copy.start()
    own_x = local_copy(x_ref.at[me], x2_ref.at[pl.ds(0, half)], l_sem)
    own_x.start()
    for index in range(4):
        lower(index)
    pieces = []
    for stream in range(3):
        block = block_of(GATHER_ORDERS[stream], bits)
        piece = remote(
            w_ref.at[bits["core"], stream, block],
            other.at[bits["core"], stream, block],
            "y",
            w_send.at[stream],
            w_recv.at[stream],
        )
        piece.start()
        pieces.append(piece)
    first = half // 32 * 16 + 16
    spans = [(0, first), (first, half - first)]
    trades = [
        remote(
            x_ref.at[1 - me, pl.ds(at, size)],
            x2_ref.at[pl.ds(half + at, size)],
            "y",
            x_send.at[index],
            x_recv.at[index],
        )
        for index, (at, size) in enumerate(spans)
    ]
    for piece in pieces:
        piece.wait()
    gather.begin()
    trades[0].start()
    vec_copy.wait()
    mine, others = vec_ref[...], vec_other[...]
    vecs_ref[...] = jnp.where(
        me == 0,
        jnp.concatenate([mine, others], axis=1),
        jnp.concatenate([others, mine], axis=1),
    )
    for c in range(4):
        half_at = slice(c % 2 * (width // 2), (c % 2 + 1) * (width // 2))
        vecs_ref[12 + c : 13 + c, :] = jnp.concatenate(
            [vecs_ref[8 + c // 2 : 9 + c // 2, half_at], vecs_ref[10 + c // 2 : 11 + c // 2, half_at]],
            axis=1,
        )
    gather.advance_all(0)
    trades[1].start()

    def norm_rows(at, size):
        values = x2_ref[at : at + size, :].astype(jnp.float32)
        normed, _, _ = normalize(values, vecs_ref[0:1, :], vecs_ref[1:2, :])
        norm[at : at + size, :] = normed.astype(jnp.bfloat16)

    own_x.wait()
    leave_rows(x2_ref, x2_out, 0, half)
    norm_rows(0, half)
    leave_rows(norm, norm_out, 0, half)
    gather.advance_all(1)
    for index in range(4, 8):
        lower(index)
    gather.advance_all(2)
    for index in range(8, 12):
        lower(index)
    leave(late_ref, late_out)
    gather.advance_all(3)
    part = width // 2

    for source, at in ((w_ref, me * part), (other, (1 - me) * part)):
        for matrix in range(4):
            for index in range(12):
                flat = matrix * 12 + index
                block = source[flat // 24, flat // 8 % 3, flat % 8]
                rows = pl.ds(pl.multiple_of(at + index * 32, 32), 32)
                if matrix < 3:
                    wqkv_ref[rows, matrix * width : (matrix + 1) * width] = block
                else:
                    wout_ref[rows, :] = block

    leave(wqkv_ref, wqkv_out)
    leave(wout_ref, wout_out)

    def project(at, size):
        @pl.loop(0, 3)
        def _(matrix):
            cols = pl.ds(pl.multiple_of(matrix * width, 128), width)
            shift = jnp.where(matrix == 0, vecs_ref[2:3, :], vecs_ref[3:4, :])
            shift = jnp.where(matrix == 1, 0.0, shift)
            proj_ref[at : at + size, cols] = (
                lax.dot_general(
                    norm[at : at + size, :], wqkv_ref[:, cols], NN, preferred_element_type=jnp.float32
                )
                + shift
            ).astype(jnp.bfloat16)

        leave_rows(proj_ref, proj_out, at, size)

    late_pieces = [
        remote(
            late_ref.at[bits["core"], stream, block_of(order, bits)],
            late_other.at[bits["core"], stream, block_of(order, bits)],
            "y",
            p_send.at[stream],
            p_recv.at[stream],
        )
        for stream, order in enumerate(GATHER_ORDERS)
    ]
    project(0, half)
    for index, (trade, (at, size)) in enumerate(zip(trades, spans)):
        trade.wait()
        if index == 1:
            for piece in late_pieces:
                piece.start()
        leave_rows(x2_ref, x2_out, half + at, size)
        norm_rows(half + at, size)
        leave_rows(norm, norm_out, half + at, size)
        project(half + at, size)
    for copy in leaving + late_pieces:
        copy.wait()


def start_call(x_tokens, vector_own, w_qkv, w_out, w_up, w_down):
    _, half, width = x_tokens.shape
    low = jnp.bfloat16
    anywhere = pl.BlockSpec(memory_space=pl.ANY)
    vmem = pl.BlockSpec(memory_space=pltpu.VMEM)
    dma = pltpu.SemaphoreType.DMA
    return pl.pallas_call(
        start_kernel,
        in_specs=[anywhere, vmem] + [anywhere] * 4,
        out_specs=[anywhere] * 4 + [vmem] + [anywhere] * 3,
        out_shape=[
            jax.ShapeDtypeStruct((2 * half, width), low),
            jax.ShapeDtypeStruct((2 * half, 3 * width), low),
            jax.ShapeDtypeStruct((width, 3 * width), low),
            jax.ShapeDtypeStruct((width, width), low),
            jax.ShapeDtypeStruct((16, width), jnp.float32),
            jax.ShapeDtypeStruct((2 * half, width), low),
            jax.ShapeDtypeStruct((2, 3, 8, 64, width), low),
            jax.ShapeDtypeStruct((2, 3, 8, 64, width), low),
        ],
        scratch_shapes=[
            pltpu.VMEM((2 * half, width), low),
            pltpu.VMEM((2 * half, 3 * width), low),
            pltpu.VMEM((width, 3 * width), low),
            pltpu.VMEM((width, width), low),
            pltpu.VMEM((2 * half, width), low),
            pltpu.VMEM((2, 3, 8, 64, width), low),
            pltpu.VMEM((2, 3, 8, 32, width), low),
            pltpu.VMEM((2, 3, 8, 32, width), low),
            pltpu.VMEM((4, width // 2, width), jnp.float32),
            pltpu.VMEM(vector_own.shape, jnp.float32),
        ]
        + gather_sems(3)
        + [dma((3,)), dma((3,)), dma((2,)), dma((2,)), dma((2,)), dma, dma((12, 2)), dma((12,)), dma((3,)), dma((3,))],
        compiler_params=pltpu.CompilerParams(
            vmem_limit_bytes=KERNEL_VMEM, collective_id=1, has_side_effects=True
        ),
        name="start",
    )(x_tokens, vector_own, w_qkv, w_out, w_up, w_down)


def attend_gather_kernel(
    q_ref, k_ref, v_ref, grad_ref, other_in, o_ref, r_ref, p_ref, other_ref, got_ref,
    score_a, score_b, peak_a, peak_b, g_send, g_recv, t_send, t_recv,
):
    step = pl.program_id(0)
    last = pl.num_programs(0) - 1
    me = own_bits()["y"]
    gather = Gather(other_ref, GATHER_ORDERS, g_send, g_recv)
    trade = remote(grad_ref.at[1 - me], got_ref, "y", t_send, t_recv)

    @pl.when(step == 0)
    def _():
        meet_partners()
        gather.begin()
        trade.start()

    for stage, at in enumerate(GATHER_STEPS):
        @pl.when(step == at)
        def _(stage=stage):
            gather.advance_all(stage)

    attend_kernel(
        q_ref, k_ref, v_ref, o_ref, r_ref, p_ref, score_a, score_b, peak_a, peak_b
    )

    @pl.when(step == last)
    def _():
        gather.advance_all(3)
        trade.wait()


GATHER_STEPS = (1, 3, 5)


def attend_call(projected, out_grad, late_other, width):
    total = projected.shape[0]
    pairs = width // (2 * HD)
    half = out_grad.shape[1]
    anywhere = pl.BlockSpec(memory_space=pl.ANY)
    dma = pltpu.SemaphoreType.DMA

    def columns(start):
        return pl.BlockSpec((total, 2 * HD), lambda p: (0, start * pairs + p))

    return pl.pallas_call(
        attend_gather_kernel,
        grid=(pairs,),
        in_specs=[columns(0), columns(1), columns(2), anywhere, anywhere],
        out_specs=[
            columns(0),
            columns(0),
            pl.BlockSpec((2, total, total), lambda p: (p, 0, 0)),
            anywhere,
            anywhere,
        ],
        out_shape=[
            jax.ShapeDtypeStruct((total, width), jnp.bfloat16),
            jax.ShapeDtypeStruct((total, width), jnp.float32),
            jax.ShapeDtypeStruct((2 * pairs, total, total), jnp.bfloat16),
            jax.ShapeDtypeStruct(late_other.shape, jnp.bfloat16),
            jax.ShapeDtypeStruct((half, width), jnp.bfloat16),
        ],
        scratch_shapes=[pltpu.VMEM((total // 2, total), jnp.float32)] * 2
        + [pltpu.VMEM((total // 2, 128), jnp.float32)] * 2
        + gather_sems(3)
        + [dma, dma],
        input_output_aliases={4: 3},
        compiler_params=pltpu.CompilerParams(
            vmem_limit_bytes=KERNEL_VMEM, collective_id=2, has_side_effects=True
        ),
        cost_estimate=pl.CostEstimate(
            flops=16 * pairs * total * total * 2 * HD,
            bytes_accessed=4 * pairs * total * total,
            transcendentals=2 * pairs * total * total,
        ),
        name="attend",
    )(projected, projected, projected, out_grad, late_other)


BACK_FIRST = (4, 3, 2, 1)
BACK_STAGES = ((), (3,), (2, 3), (1, 2, 3), (0, 1, 2, 3), (0, 1, 2, 3), (0, 1))
BACK_MOVES = (
    (2, ((4, 0),)),
    (3, ((2, 2),)),
    (4, ((0, 4), (1, 3))),
    (5, ((2, 3), (3, 1), (4, 1), (5, 0))),
    (6, ((0, 5), (1, 4))),
    (7, ((0, 6), (2, 4), (4, 2), (3, 2))),
    (8, ((4, 3), (5, 1), (1, 5))),
    (9, ((2, 5), (1, 6), (3, 3), (5, 2), (6, 0))),
    (10, ((4, 4), (2, 6))),
    (11, ((4, 5),)),
)
BACK_LAST = ((4, 6), (3, 4), (5, 3), (6, 1))
TRADE_STEP = 3


def attend_back_sum_kernel(
    q_ref, k_ref, v_ref, g_ref, o_ref, r_ref, p_ref, partial_ref, y2_ref, norm_ref, out_ref,
    dq_ref, dk_ref, dv_ref, late_ref, first_ref, tokens_ref, third_ref, parts_out,
    ds, qt, gt, dkt, dvt, total, small, parts, turned, *rest,
):
    landing, rest = rest[:-7], rest[-7:]
    s_send, s_recv, s_local, t_send, t_recv, l_sem, o_sem = rest
    pair, head = pl.program_id(0), pl.program_id(1)
    step = pair * 2 + head
    last = pl.num_programs(0) * 2 - 1
    core = own_bits()["core"]
    half = tokens_ref.shape[0]
    streams, cores, held = [], {}, list(landing)
    for index, stages in enumerate(BACK_STAGES):
        buffers = {stage: held.pop(0) for stage in stages}
        sems = (s_send.at[index], s_recv.at[index], s_local.at[index])
        if index < 4:
            shared, sums = late_ref.at[core, index], total.at[index]
        else:
            shared, sums = first_ref.at[core, index - 4], small.at[index - 4]
            source = parts.at[1 if index == 4 else (index - 5) % 2]
            cores[index] = CoreSum(
                source, sums, buffers[0], s_send.at[index, 0], s_recv.at[index, 0]
            )
        streams.append(StreamSum(sums, buffers, shared, *sems))
    trade = remote(y2_ref.at[pl.ds(half, half)], tokens_ref, "y", t_send, t_recv)
    load = local_copy(partial_ref, total, l_sem.at[1])
    load_out = local_copy(out_ref, parts.at[1], l_sem.at[3])
    load_norm = local_copy(norm_ref, ds.at[:, pl.ds(0, norm_ref.shape[1])], l_sem.at[2])

    @pl.when(step == 0)
    def _():
        load.start()
        load_norm.start()
        load_out.start()
        meet_partners()
        load_out.wait()
        cores[4].start()
        load_norm.wait()
        turned[...] = ds[:, : norm_ref.shape[1]].T
        load.wait()
        for index, stage in enumerate(BACK_FIRST):
            streams[index].start(stage)

    for at, moves in BACK_MOVES:
        @pl.when(step == at)
        def _(at=at, moves=moves):
            for index, stage in moves:
                if stage == 0:
                    cores[index].finish()
                    streams[index].start(1)
                else:
                    streams[index].move(stage)
            if at == TRADE_STEP:
                trade.start()

    attend_back_kernel(
        q_ref, k_ref, v_ref, g_ref, o_ref, r_ref, p_ref, dq_ref, dk_ref, dv_ref, ds, qt, gt, dkt, dvt
    )

    @pl.when(head == 1)
    def _():
        sides = jnp.concatenate([dq_ref[...], dk_ref[...], dv_ref[...]], axis=1)
        values = lax.dot_general(
            turned[...], sides, NN, preferred_element_type=jnp.float32
        ).astype(jnp.bfloat16)
        slot, part = (pair // 2) % 2, pair % 2
        rows = parts.shape[4]
        for side in range(2):
            for block in range(8):
                at = side * 8 * rows + block * rows
                parts[slot, part, block, side] = values[at : at + rows, :]

    for index, at in ((5, 3), (6, 7)):
        @pl.when(step == at)
        def _(index=index):
            cores[index].start()

    @pl.when(step == last)
    def _():
        hand = local_copy(parts.at[0], parts_out, o_sem.at[0])
        hand.start()
        for index, stage in BACK_LAST:
            streams[index].finish(stage)
        third = local_copy(small.at[2], third_ref.at[0], o_sem.at[1])
        third.start()
        second = local_copy(small.at[1], third_ref.at[1], o_sem.at[2])
        second.start()
        trade.wait()
        hand.wait()
        second.wait()
        third.wait()


def attend_back_call(projected, upstream, attended, inverse, exponent, partial, y2, norm, out_parts):
    total, width = attended.shape
    pairs = width // (2 * HD)
    streams, _, _, rows, _ = partial.shape
    side = width // 2
    low = jnp.bfloat16
    anywhere = pl.BlockSpec(memory_space=pl.ANY)
    dma = pltpu.SemaphoreType.DMA

    def columns(start):
        return pl.BlockSpec((total, 2 * HD), lambda p, h: (0, start * pairs + p))

    landing = []
    for index, stages in enumerate(BACK_STAGES):
        landing += landing_shapes(stages, rows, width if index < 4 else side)
    return pl.pallas_call(
        attend_back_sum_kernel,
        grid=(pairs, 2),
        in_specs=[columns(0), columns(1), columns(2), columns(0), columns(0), columns(0)]
        + [pl.BlockSpec((None, total, total), lambda p, h: (p * 2 + h, 0, 0))]
        + [anywhere] * 4,
        out_specs=[columns(0)] * 3 + [anywhere] * 5,
        out_shape=[jax.ShapeDtypeStruct((total, width), low)] * 3
        + [
            jax.ShapeDtypeStruct((2, streams, 8, rows, width), low),
            jax.ShapeDtypeStruct((2, 4, 8, rows, side), low),
            jax.ShapeDtypeStruct((total // 2, width), low),
            jax.ShapeDtypeStruct((2, 8, 2, rows, side), low),
            jax.ShapeDtypeStruct((2, 8, 2, rows, side), low),
        ],
        scratch_shapes=[pltpu.VMEM((total, total), low)]
        + [pltpu.VMEM((2 * HD, total), low)] * 2
        + [pltpu.VMEM((2 * HD, total), jnp.float32)] * 2
        + [
            pltpu.VMEM(partial.shape, low),
            pltpu.VMEM((3, 8, 2, rows, side), low),
            pltpu.VMEM((2, 2, 8, 2, rows, side), low),
            pltpu.VMEM((width, total), low),
        ]
        + landing
        + sum_sems(len(BACK_STAGES))
        + [dma, dma, dma((4,)), dma((3,))],
        compiler_params=pltpu.CompilerParams(
            vmem_limit_bytes=KERNEL_VMEM, collective_id=3, has_side_effects=True
        ),
        cost_estimate=pl.CostEstimate(
            flops=32 * pairs * total * total * 2 * HD,
            bytes_accessed=4 * pairs * total * total,
            transcendentals=0,
        ),
        name="attend_back",
    )(
        projected, projected, projected, upstream, attended, inverse, exponent, partial, y2, norm,
        out_parts,
    )


LAST_FIRST = ((0, 5), (1, 4), (2, 2))
LAST_STAGES = ((), (), (2, 3), (0, 1, 2, 3))
LAST_MOVES = (
    ((3, 0),),
    ((3, 1), (1, 4), (2, 2), (0, 5)),
    ((3, 2), (2, 3), (1, 5)),
    ((3, 3), (0, 6)),
    ((2, 4), (1, 6)),
    ((3, 4),),
    ((2, 5),),
    ((3, 5),),
    ((2, 6),),
    ((3, 6),),
)


def finish_kernel(
    dq_in, dk_in, dv_in, x_in, w_in, resid_in, vec_ref, part_ref, late_in, first_in, small_in,
    parts_ref,
    xg_ref, vsum_ref, late_ref, first_ref,
    dq_ref, dk_ref, dv_ref, x_ref, w_ref, resid_ref, sent_rows, own_rows, coming, small, *rest,
):
    landing, rest = rest[:-10], rest[-10:]
    s_send, s_recv, s_local, t_send, t_recv, l_sem, v_land, v_send, v_recv, i_sem = rest
    bits = own_bits()
    me, core = bits["y"], bits["core"]
    rows, width = x_ref.shape
    half = rows // 2
    streams, held = [], list(landing)
    for index, stages in enumerate(LAST_STAGES):
        buffers = {stage: held.pop(0) for stage in stages}
        sems = (s_send.at[index], s_recv.at[index], s_local.at[index])
        shared = late_ref.at[core, 3] if index == 0 else first_ref.at[core, index]
        streams.append(
            StreamSum(None if index == 0 else small.at[index - 1], buffers, shared, *sems)
        )
    core_sum = CoreSum(
        parts_ref, small.at[2], streams[3].landing[0], s_send.at[3, 0], s_recv.at[3, 0]
    )
    entering = {}
    for part, at in ((1, half), (0, 0)):
        copies = []
        for k, (source, target) in enumerate(
            ((dq_in, dq_ref), (dk_in, dk_ref), (dv_in, dv_ref), (x_in, x_ref), (resid_in, resid_ref))
        ):
            span = pl.ds(at, half)
            copies.append(local_copy(source.at[span], target.at[span], i_sem.at[part, k]))
        if part == 1:
            copies.append(local_copy(w_in, w_ref, i_sem.at[1, 5]))
        for copy in copies:
            copy.start()
        entering[part] = copies
    loads = [local_copy(small_in.at[1 - i], small.at[i], l_sem.at[1 + i]) for i in range(2)]
    for load in loads:
        load.start()
    gain, shift = vec_ref[0:1, :], vec_ref[1:2, :]
    meet_partners()
    core_sum.start()
    for load in loads:
        load.wait()
    for index, stage in LAST_FIRST:
        streams[index].start(stage)

    def turn(at):
        for index, stage in LAST_MOVES[at]:
            if stage == 0:
                core_sum.finish()
                streams[index].start(1)
            else:
                streams[index].move(stage)

    step = half // 7

    def products(at):
        span = slice(at, at + half)
        for matrix, part in enumerate((dq_ref, dk_ref, dv_ref)):
            term = lax.dot_general(
                part[span, :],
                w_ref[:, matrix * width : (matrix + 1) * width],
                NT,
                preferred_element_type=jnp.float32,
            )
            if matrix == 0:
                coming[...] = term
            else:
                coming[...] += term

    def input_rows(at, target):
        @pl.loop(0, 7)
        def _(index):
            here = pl.ds(pl.multiple_of(index * step, 16), step)
            span = pl.ds(pl.multiple_of(at + index * step, 16), step)
            upstream = coming[here, :]
            _, normed, inverse = normalize(x_ref[span, :].astype(jnp.float32), gain, shift)
            target[here, :] = (
                resid_ref[span, :] + norm_back(upstream, gain, normed, inverse)
            ).astype(jnp.bfloat16)
            vsum_ref[0:1, :] += jnp.sum(upstream * normed, axis=0, keepdims=True)
            vsum_ref[1:2, :] += jnp.sum(upstream, axis=0, keepdims=True)

    vsum_ref[...] = part_ref[...]
    turn(0)
    for copy in entering[1]:
        copy.wait()
    products(half)
    input_rows(half, sent_rows)
    trade = remote(sent_rows, xg_ref.at[me], "y", t_send, t_recv)
    trade.start()
    turn(1)
    for copy in entering[0]:
        copy.wait()
    products(0)
    turn(2)
    input_rows(0, own_rows)
    own = local_copy(own_rows, xg_ref.at[me], l_sem.at[0])
    own.start()
    vsum_ref[2:3, :] = jnp.sum(dq_ref[...].astype(jnp.float32), axis=0, keepdims=True)
    vsum_ref[3:4, :] = jnp.sum(dv_ref[...].astype(jnp.float32), axis=0, keepdims=True)

    def vector_step(stage):
        name = ("core", "x", "a", "b", "y")[stage]
        return remote(vsum_ref, v_land.at[stage], name, v_send.at[stage], v_recv.at[stage])

    vector_step(0).start()
    for at in range(3, len(LAST_MOVES)):
        turn(at)
        if at < 8:
            vector_step(at - 3).wait()
            vsum_ref[...] += v_land[at - 3]
            if at < 7:
                vector_step(at - 2).start()
    trade.wait()
    own.wait()


def finish_call(grad_parts, x2, wqkv, grad_resid, vecs, part_sums, late, first, small, parts):
    total, width = x2.shape
    low = jnp.bfloat16
    anywhere = pl.BlockSpec(memory_space=pl.ANY)
    vmem = pl.BlockSpec(memory_space=pltpu.VMEM)
    dma = pltpu.SemaphoreType.DMA
    rows, side = small.shape[3], small.shape[4]
    landing = []
    for stages in LAST_STAGES:
        landing += landing_shapes(stages, rows, side)
    return pl.pallas_call(
        finish_kernel,
        in_specs=[anywhere] * 6 + [vmem] * 2 + [anywhere] * 3 + [vmem],
        out_specs=[anywhere, vmem, anywhere, anywhere],
        out_shape=[
            jax.ShapeDtypeStruct((2, total // 2, width), low),
            jax.ShapeDtypeStruct((16, width), jnp.float32),
            jax.ShapeDtypeStruct(late.shape, low),
            jax.ShapeDtypeStruct(first.shape, low),
        ],
        input_output_aliases={8: 2, 9: 3},
        scratch_shapes=[pltpu.VMEM((total, width), low)] * 4
        + [
            pltpu.VMEM((width, 3 * width), low),
            pltpu.VMEM((total, width), jnp.float32),
            pltpu.VMEM((total // 2, width), low),
            pltpu.VMEM((total // 2, width), low),
            pltpu.VMEM((total // 2, width), jnp.float32),
            pltpu.VMEM((3, 8, 2, rows, side), low),
        ]
        + landing
        + sum_sems(len(LAST_STAGES))
        + [dma, dma, dma((3,)), pltpu.VMEM((5, 16, width), jnp.float32), dma((5,)), dma((5,)), dma((2, 6))],
        compiler_params=pltpu.CompilerParams(
            vmem_limit_bytes=KERNEL_VMEM, collective_id=4, has_side_effects=True
        ),
        name="finish",
    )(*grad_parts, x2, wqkv, grad_resid, vecs, part_sums, late, first, small, parts)


def update_kernel(*refs):
    groups = [refs[3 * i : 3 * i + 3] for i in range(4)]
    late_ref, first_ref, y_in, y_got, xg_in = refs[12:17]
    outs = [refs[17 + 3 * i : 20 + 3 * i] for i in range(4)]
    y_out, xg_out = refs[29:31]
    wide, share, through, in_sem, out_sem, t_sem = refs[31:]
    me = lax.axis_index("ctx")
    side = wide.shape[2]
    width = 2 * side
    slots = wide.shape[0]
    ahead = slots // 2
    half = through.shape[1]
    passing = [
        (y_in.at[pl.ds(0, half)], through.at[0], y_out.at[me]),
        (y_got, through.at[1], y_out.at[1 - me]),
    ] + [(xg_in.at[part], through.at[2 + part], xg_out.at[part]) for part in range(2)]
    brought = [
        local_copy(source, held, t_sem.at[0, k]) for k, (source, held, _) in enumerate(passing)
    ]
    taken = [
        local_copy(held, target, t_sem.at[1, k]) for k, (_, held, target) in enumerate(passing)
    ]

    def columns(at, size, into):
        return lambda ref: ref.at[:, pl.ds(at, size)], into, size

    units = []
    for c in range(4):
        rows = lambda ref, c=c: ref.at[pl.ds(c * side, side)]
        units.append((3, [(rows, 0, width)], [(late_ref.at[0, c], 0, width)], False))
        halves = [columns((c + 4 * j) * side, side, j * side) for j in range(2)]
        units.append((2, halves, [(late_ref.at[1, c], 0, width)], False))
    for k in range(4):
        shares = [(first_ref.at[part, k], part * side, side) for part in range(2)]
        if k == 0:
            units.append((1, [columns(0, width, 0)], shares, False))
        else:
            third = width // 3
            thirds = [
                columns(m * width + (k - 1) * third, third, m * third) for m in range(3)
            ]
            units.append((0, thirds, shares, True))

    def loads(index):
        which, spans, shares, _ = units[index]
        slot = index % slots
        copies = []
        for k in range(3):
            for part, (view, into, size) in enumerate(spans):
                copies.append(
                    local_copy(
                        view(groups[which][k]),
                        wide.at[slot, k, :, pl.ds(into, size)],
                        in_sem.at[index, k * 3 + part],
                    )
                )
        for part, (source, into, size) in enumerate(shares):
            copies.append(
                local_copy(source, share.at[slot, :, :, pl.ds(into, size)], in_sem.at[index, 9 + part])
            )
        return copies

    def stores(index):
        which, spans, _, _ = units[index]
        slot = index % slots
        return [
            local_copy(
                wide.at[slot, k, :, pl.ds(into, size)],
                view(outs[which][k]),
                out_sem.at[index, k * 3 + part],
            )
            for k in range(3)
            for part, (view, into, size) in enumerate(spans)
        ]

    def compute(index):
        slot, pairs = index % slots, units[index][3]
        rows = share.shape[2]

        @pl.loop(0, 8)
        def _(block):
            gradient = share[slot, block].astype(jnp.float32)
            if pairs:
                piece = 2 * HD
                gradient = jnp.concatenate(
                    [
                        gradient[:, part * side + m * piece : part * side + (m + 1) * piece]
                        for m in range(3)
                        for part in range(2)
                    ],
                    axis=1,
                )
            span = pl.ds(pl.multiple_of(block * rows, 16), rows)
            weight, first, second = (wide[slot, k, span, :] for k in range(3))
            new = adam_update(weight, gradient, first, second, matrix_rate, matrix_decay)
            wide[slot, 0, span, :] = new[2]
            wide[slot, 1, span, :] = new[0]
            wide[slot, 2, span, :] = new[1]

    for index in range(ahead):
        for copy in loads(index):
            copy.start()
    for copy in brought:
        copy.start()
    for index in range(len(units)):
        if index + ahead < len(units):
            if index + ahead >= slots:
                for copy in stores(index + ahead - slots):
                    copy.wait()
            for copy in loads(index + ahead):
                copy.start()
        for copy in loads(index):
            copy.wait()
        compute(index)
        for copy in stores(index):
            copy.start()
        if index == 2:
            for copy in brought:
                copy.wait()
            for copy in taken:
                copy.start()
    for index in range(len(units) - slots, len(units)):
        for copy in stores(index):
            copy.wait()
    for copy in taken:
        copy.wait()


def update_call(groups, late, first, y_rows, y_got, x_grad):
    flat = [member for group in groups for member in group]
    anywhere = pl.BlockSpec(memory_space=pl.ANY)
    side, width = groups[1][0].shape
    dma = pltpu.SemaphoreType.DMA
    shapes = [jax.ShapeDtypeStruct(member.shape, member.dtype) for member in flat]
    *new, y_new, x_new = pl.pallas_call(
        update_kernel,
        in_specs=[anywhere] * 17,
        out_specs=[anywhere] * 14,
        out_shape=shapes
        + [jax.ShapeDtypeStruct(x_grad.shape, x_grad.dtype)] * 2,
        scratch_shapes=[
            pltpu.VMEM((6, 3, side, width), jnp.float32),
            pltpu.VMEM((6, 8, side // 8, width), jnp.bfloat16),
            pltpu.VMEM((4,) + y_got.shape, jnp.bfloat16),
            dma((12, 11)),
            dma((12, 9)),
            dma((2, 4)),
        ],
        compiler_params=pltpu.CompilerParams(vmem_limit_bytes=KERNEL_VMEM),
        name="update",
    )(*flat, late, first, y_rows, y_got, x_grad)
    return new, y_new, x_new


def middle_kernel(
    att_ref, x_ref, grad_ref, got_ref, vec_ref, wo_ref, mine_ref, other_ref,
    y_out, gr_out, ga_out, partial_ref, go_ref, sums_ref,
    y_ref, gr_ref, ga_ref, up_w, down_w, g_ref, mlp, upstream, acts, grads_pre, grads, total, *rest,
):
    landing, rest = rest[:-6], rest[-6:]
    s_send, s_recv, s_local, w_sem, x_sem, o_sem = rest
    bits = own_bits()
    me, core = bits["y"], bits["core"]
    rows, width = g_ref.shape
    half = rows // 2
    side = width // 2
    chunks = total.shape[0]
    piece = total.shape[3]
    resid, low_rows = gr_ref, ga_ref
    streams, cores, held = [], [], list(landing[2:])
    for index, stages in enumerate(MIDDLE_STAGES):
        buffers = {stage: held.pop(0) for stage in stages}
        sems = (s_send.at[index], s_recv.at[index], s_local.at[index])
        streams.append(StreamSum(total.at[index], buffers, None, *sems))
        cores.append(
            CoreSum(
                grads, total.at[index], landing[index % 2], s_send.at[index, 0], s_recv.at[index, 0]
            )
        )

    own_x = local_copy(x_ref, y_ref, x_sem.at[0])
    own_x.start()
    loads = [
        local_copy(grad_ref.at[me], g_ref.at[pl.ds(0, half)], x_sem.at[1]),
        local_copy(got_ref, g_ref.at[pl.ds(half, half)], x_sem.at[2]),
    ]
    for index, (source, at) in enumerate(((mine_ref, me), (other_ref, 1 - me))):
        for c in range(chunks):
            part = pl.ds(pl.multiple_of(c * width + at * side, 16), side)
            loads.append(
                local_copy(source.at[pl.ds(c * side, side)], down_w.at[part], w_sem.at[index, c])
            )
            part = pl.ds(pl.multiple_of(at * side, 16), side)
            loads.append(
                local_copy(
                    source.at[pl.ds((chunks + c) * side, side)],
                    up_w.at[part, pl.ds(c * width, width)],
                    w_sem.at[index, chunks + c],
                )
            )
    for load in loads:
        load.start()
    meet_partners()
    own_x.wait()
    gain = vec_ref[5:6, :]
    step = rows // 7

    resid[...] = lax.dot_general(att_ref[...], wo_ref[...], NN, preferred_element_type=jnp.float32)

    @pl.loop(0, 7)
    def _(index):
        span = pl.ds(pl.multiple_of(index * step, 16), step)
        resid[span, :] = y_ref[span, :].astype(jnp.float32) + (resid[span, :] + vec_ref[4:5, :])
        normed_two, _, _ = normalize(resid[span, :], gain, vec_ref[6:7, :])
        low_rows[span, :] = normed_two.astype(jnp.bfloat16)

    for load in loads:
        load.wait()
    sums_ref[...] = jnp.zeros_like(sums_ref)
    mlp[...] = jnp.zeros_like(mlp)
    upstream[...] = jnp.zeros_like(upstream)

    def column_sum(values):
        return jnp.sum(values, axis=0, keepdims=True)

    @pl.loop(0, chunks)
    def _(c):
        cols = pl.ds(pl.multiple_of(c * width, 128), width)
        shift = vec_ref[pl.ds(12 + c, 1), :]
        for part in range(2):
            span = slice(part * half, (part + 1) * half)
            pre = (
                lax.dot_general(
                    low_rows[span, :], up_w[:, cols], NN, preferred_element_type=jnp.float32
                )
                + shift
            )
            below = normal_cdf(pre)
            acts[span, :] = (pre * below).astype(jnp.bfloat16)
            density = jnp.exp(-0.5 * pre * pre) * 0.3989422804014327
            grad_act = lax.dot_general(
                g_ref[span, :], down_w[cols, :], NT, preferred_element_type=jnp.float32
            )
            grad_pre = (grad_act * (below + pre * density)).astype(jnp.bfloat16)
            grads_pre[span, :] = grad_pre
            sums_ref[pl.ds(12 + c, 1), :] += column_sum(grad_pre.astype(jnp.float32))
            mlp[span, :] += lax.dot_general(
                acts[span, :], down_w[cols, :], NN, preferred_element_type=jnp.float32
            )
            upstream[span, :] += lax.dot_general(
                grads_pre[span, :], up_w[:, cols], NT, preferred_element_type=jnp.float32
            )

        for chunk, moves in enumerate(MIDDLE_MOVES):
            @pl.when(c == chunk)
            def _(moves=moves):
                for index, stage in moves:
                    if stage == 0:
                        cores[index].finish()
                        streams[index].start(1)
                    else:
                        streams[index].move(stage)

        def put(which, values):
            for part in range(2):
                for block in range(8):
                    at = part * side + block * piece
                    grads[which, block, part] = values[at : at + piece, :].astype(jnp.bfloat16)

        put(0, lax.dot_general(acts[...], g_ref[...], TN, preferred_element_type=jnp.float32))
        put(
            1, lax.dot_general(low_rows[...], grads_pre[...], TN, preferred_element_type=jnp.float32)
        )
        for index in range(chunks):
            @pl.when(c == index)
            def _(index=index):
                cores[index].start()

    for c in range(chunks):
        at = slice(c % 2 * side, (c % 2 + 1) * side)
        sums_ref[8 + c // 2 : 9 + c // 2, at] = sums_ref[12 + c : 13 + c, :side]
        sums_ref[10 + c // 2 : 11 + c // 2, at] = sums_ref[12 + c : 13 + c, side:]

    @pl.loop(0, 7)
    def _(index):
        span = pl.ds(pl.multiple_of(index * step, 16), step)
        y_ref[span, :] = (resid[span, :] + mlp[span, :] + vec_ref[7:8, :]).astype(jnp.bfloat16)
        _, normed, inverse = normalize(resid[span, :], gain, vec_ref[6:7, :])
        coming = upstream[span, :]
        grads_out = g_ref[span, :].astype(jnp.float32)
        sums_ref[5:6, :] += column_sum(coming * normed)
        sums_ref[6:7, :] += column_sum(coming)
        sums_ref[7:8, :] += column_sum(grads_out)
        grad_resid = grads_out + norm_back(coming, gain, normed, inverse)
        gr_ref[span, :] = grad_resid
        acts[span, :] = grad_resid.astype(jnp.bfloat16)
        sums_ref[4:5, :] += column_sum(acts[span, :].astype(jnp.float32))

    leaving = []

    def leave(source, target):
        copy = local_copy(source, target, o_sem.at[len(leaving)])
        copy.start()
        leaving.append(copy)

    leave(y_ref, y_out)
    leave(gr_ref, gr_out)
    cores[3].finish()
    leave(total.at[3], partial_ref.at[3])
    streams[0].finish(3)
    leave(total.at[0], partial_ref.at[0])
    ga_ref[...] = lax.dot_general(
        acts[...], wo_ref[...], NT, preferred_element_type=jnp.float32
    ).astype(jnp.bfloat16)
    leave(ga_ref, ga_out)
    branch_grad = lax.dot_general(
        att_ref[...], acts[...], TN, preferred_element_type=jnp.float32
    ).astype(jnp.bfloat16)
    for part in range(2):
        for sides in range(2):
            for block in range(8):
                at = sides * side + block * piece
                go_ref[part, block, sides] = branch_grad[
                    at : at + piece, part * side : (part + 1) * side
                ]
    for index, stage in ((1, 2), (2, 1)):
        streams[index].finish(stage)
        leave(total.at[index], partial_ref.at[index])
    for copy in leaving:
        copy.wait()


MIDDLE_STAGES = ((1, 2, 3), (1, 2), (1,), ())
MIDDLE_MOVES = ((), ((0, 0),), ((0, 1), (1, 0)), ((0, 2), (1, 1), (2, 0)))


def middle_call(attended, x_rows, out_grad, grad_got, vecs, out_low, mine, other):
    rows, width = x_rows.shape
    hidden = mine.shape[0]
    low = jnp.bfloat16
    anywhere = pl.BlockSpec(memory_space=pl.ANY)
    vmem = pl.BlockSpec(memory_space=pltpu.VMEM)
    dma = pltpu.SemaphoreType.DMA
    chunks = len(MIDDLE_STAGES)
    piece = hidden // (2 * chunks * 8)
    landing = landing_shapes((0, 0), piece, width)
    for stages in MIDDLE_STAGES:
        landing += landing_shapes(stages, piece, width)
    return pl.pallas_call(
        middle_kernel,
        in_specs=[vmem, anywhere, anywhere, anywhere, vmem, vmem, anywhere, anywhere],
        out_specs=[anywhere] * 4 + [vmem] * 2,
        out_shape=[
            jax.ShapeDtypeStruct((rows, width), low),
            jax.ShapeDtypeStruct((rows, width), jnp.float32),
            jax.ShapeDtypeStruct((rows, width), low),
            jax.ShapeDtypeStruct((chunks, 8, 2, piece, width), low),
            jax.ShapeDtypeStruct((2, 8, 2, piece, width // 2), low),
            jax.ShapeDtypeStruct((16, width), jnp.float32),
        ],
        scratch_shapes=[
            pltpu.VMEM((rows, width), low),
            pltpu.VMEM((rows, width), jnp.float32),
            pltpu.VMEM((rows, width), low),
            pltpu.VMEM((width, hidden), low),
            pltpu.VMEM((hidden, width), low),
            pltpu.VMEM((rows, width), low),
            pltpu.VMEM((rows, width), jnp.float32),
            pltpu.VMEM((rows, width), jnp.float32),
            pltpu.VMEM((rows, hidden // chunks), low),
            pltpu.VMEM((rows, hidden // chunks), low),
            pltpu.VMEM((2, 8, 2, piece, width), low),
            pltpu.VMEM((chunks, 8, 2, piece, width), low),
        ]
        + landing
        + sum_sems(chunks)
        + [dma((2, 2 * chunks)), dma((3,)), dma((7,))],
        compiler_params=pltpu.CompilerParams(
            vmem_limit_bytes=KERNEL_VMEM, collective_id=5, has_side_effects=True
        ),
        name="middle",
    )(attended, x_rows, out_grad, grad_got, vecs, out_low, mine, other)


def per_device_clips(
    x_tokens,
    out_grad,
    w_qkv,
    w_out,
    w_up,
    w_down,
    vectors,
    qkv_mean,
    qkv_square,
    out_mean,
    out_square,
    up_mean,
    up_square,
    down_mean,
    down_square,
    vectors_mean,
    vectors_square,
):
    me = lax.axis_index("ctx")
    width = x_tokens.shape[2]
    side = width // 2
    vector_own = jnp.pad(
        vectors.astype(jnp.bfloat16).astype(jnp.float32), ((0, 4), (0, 0))
    )
    (
        x_low,
        projected,
        qkv_low,
        out_low,
        vector_rows,
        norm_rows,
        late_weights,
        late_pieces,
    ) = start_call(x_tokens, vector_own, w_qkv, w_out, w_up, w_down)
    attended_low, inverse_total, exponent, late_other, grad_got = attend_call(
        projected, out_grad, late_pieces, width
    )
    y_rows, grad_resid, grad_attended, partial, grad_out, part_sums = middle_call(
        attended_low,
        x_low,
        out_grad,
        grad_got,
        vector_rows,
        out_low,
        late_weights.reshape(-1, width),
        late_other.reshape(-1, width),
    )
    *grad_parts, late, first, y_got, small, last_parts = attend_back_call(
        projected,
        grad_attended,
        attended_low,
        inverse_total,
        exponent,
        partial,
        y_rows,
        norm_rows,
        grad_out,
    )
    x_grad, summed_vectors, late_shared, first_shared = finish_call(
        grad_parts,
        x_low,
        qkv_low,
        grad_resid,
        vector_rows,
        part_sums,
        late,
        first,
        small,
        last_parts,
    )

    vector_share = lax.dynamic_slice_in_dim(summed_vectors[:12], me * side, side, axis=1)

    weights, y_tokens, x_grad = update_call(
        (
            (w_qkv, qkv_mean, qkv_square),
            (w_out, out_mean, out_square),
            (w_up, up_mean, up_square),
            (w_down, down_mean, down_square),
        ),
        late_shared,
        first_shared,
        y_rows,
        y_got,
        x_grad,
    )
    qkv_new, out_new, up_new, down_new = (
        (weights[3 * i + 1], weights[3 * i + 2], weights[3 * i]) for i in range(4)
    )
    vectors_new = adam_update(
        vectors, vector_share, vectors_mean, vectors_square, vector_rate, 0.0
    )
    return (y_tokens, x_grad) + qkv_new + out_new + up_new + down_new + vectors_new


def per_device(x_tokens, *others):
    clips = x_tokens.shape[0]
    if lax.axis_size("ctx") == 2 and lax.axis_size("dp") == 16 and clips == 2:
        return per_device_clips(x_tokens, *others)
    return per_device_split(x_tokens, *others)


def solution(mesh):
    return jax.shard_map(
        per_device,
        mesh=mesh,
        in_specs=(
            P("dp", "ctx", None),
            P("dp", "ctx", None),
            P("ctx", None),
            P("ctx", None),
            P("ctx", None),
            P("ctx", None),
            P(None, "ctx"),
            P("ctx", None),
            P("ctx", None),
            P("ctx", None),
            P("ctx", None),
            P("ctx", None),
            P("ctx", None),
            P("ctx", None),
            P("ctx", None),
            P(None, "ctx"),
            P(None, "ctx"),
        ),
        out_specs=(
            P("dp", "ctx", None),
            P("dp", "ctx", None),
            P("ctx", None),
            P("ctx", None),
            P("ctx", None),
            P("ctx", None),
            P("ctx", None),
            P("ctx", None),
            P("ctx", None),
            P("ctx", None),
            P("ctx", None),
            P("ctx", None),
            P("ctx", None),
            P("ctx", None),
            P(None, "ctx"),
            P(None, "ctx"),
            P(None, "ctx"),
        ),
        check_vma=False,
    )
```

```python
import functools

import jax
import jax.numpy as jnp
from jax import lax
from jax.experimental import pallas as pl
from jax.experimental.pallas import tpu as pltpu
from jax.sharding import PartitionSpec as P

HD = 64
STEP = 10


norm_epsilon = 1e-06
adam_epsilon = 1e-08
matrix_rate = 0.04
matrix_decay = 0.05
vector_rate = 0.2


def normalize(values, norm_gain, norm_shift):
    row_mean = jnp.mean(values, axis=-1, keepdims=True)
    centred = values - row_mean
    row_var = jnp.mean(centred * centred, axis=-1, keepdims=True)
    inverse = lax.rsqrt(row_var + norm_epsilon)
    normed = centred * inverse
    return (normed * norm_gain + norm_shift, normed, inverse)


def norm_back(upstream, norm_gain, normed, inverse):
    scaled = upstream * norm_gain
    first_mean = jnp.mean(scaled, axis=-1, keepdims=True)
    second_mean = jnp.mean(scaled * normed, axis=-1, keepdims=True)
    return inverse * (scaled - first_mean - normed * second_mean)


def normal_cdf(values):
    return 0.5 * (1.0 + lax.erf(values * 0.7071067811865476))


def attend(operands):
    query_block, key_block, value_block = operands
    scores = (
        jnp.einsum("qhd,khd->hqk", query_block, key_block, preferred_element_type=jnp.float32)
        * 0.125
    )
    peak_score = jnp.max(scores, axis=-1, keepdims=True)
    exponent = jnp.exp(scores - peak_score)
    totals = jnp.sum(exponent, axis=-1, keepdims=True)
    probs_low = (exponent / totals).astype(jnp.bfloat16)
    attended = jnp.einsum(
        "hqk,khd->qhd", probs_low, value_block, preferred_element_type=jnp.float32
    )
    return (attended, peak_score + jnp.log(totals))


def attend_back(operands):
    query_block, key_block, value_block, log_total, grad_block = operands
    scores = (
        jnp.einsum("qhd,khd->hqk", query_block, key_block, preferred_element_type=jnp.float32)
        * 0.125
    )
    probs = jnp.exp(scores - log_total)
    grad_probs = jnp.einsum(
        "qhd,khd->hqk", grad_block, value_block, preferred_element_type=jnp.float32
    )
    delta = jnp.sum(probs * grad_probs, axis=-1, keepdims=True)
    grad_scores = (probs * (grad_probs - delta)).astype(jnp.bfloat16)
    grad_query = (
        jnp.einsum("hqk,khd->qhd", grad_scores, key_block, preferred_element_type=jnp.float32)
        * 0.125
    )
    grad_key = (
        jnp.einsum("hqk,qhd->khd", grad_scores, query_block, preferred_element_type=jnp.float32)
        * 0.125
    )
    grad_value = jnp.einsum(
        "hqk,qhd->khd", probs.astype(jnp.bfloat16), grad_block, preferred_element_type=jnp.float32
    )
    return (grad_query, grad_key, grad_value)


def adam_update(weight, gradient, first_old, second_old, step_rate, decay_rate):
    first_new = 0.5 * first_old + 0.5 * gradient
    second_new = 0.5 * second_old + 0.5 * gradient * gradient
    correction = 1.0 - 0.5**STEP
    update = (
        first_new / correction / (jnp.sqrt(second_new / correction) + adam_epsilon)
        + decay_rate * weight
    )
    return (first_new, second_new, weight - step_rate * update)


def per_device_split(
    x_tokens,
    out_grad,
    w_qkv,
    w_out,
    w_up,
    w_down,
    vectors,
    qkv_mean,
    qkv_square,
    out_mean,
    out_square,
    up_mean,
    up_square,
    down_mean,
    down_square,
    vectors_mean,
    vectors_square,
):
    masters = (w_qkv, w_out, w_up, w_down, vectors)
    lowered = tuple((member.astype(jnp.bfloat16) for member in masters))
    qkv_low, out_low, up_low, down_low, vector_low = (
        lax.all_gather(lowered[0], "ctx", axis=0, tiled=True),
        lax.all_gather(lowered[1], "ctx", axis=0, tiled=True),
        lax.all_gather(lowered[2], "ctx", axis=0, tiled=True),
        lax.all_gather(lowered[3], "ctx", axis=0, tiled=True),
        lax.all_gather(lowered[4], "ctx", axis=1, tiled=True),
    )
    vector_rows = vector_low.astype(jnp.float32)
    clip_count, row_count, model_width = x_tokens.shape
    head_count = model_width // HD
    token_total = clip_count * row_count
    flat_rows = x_tokens.reshape(token_total, model_width).astype(jnp.float32)
    norm_one, normed_one, inverse_one = normalize(flat_rows, vector_rows[0], vector_rows[1])
    norm_one_low = norm_one.astype(jnp.bfloat16)
    qkv_shift = jnp.concatenate([vector_rows[2], jnp.zeros_like(vector_rows[2]), vector_rows[3]])
    projected = (
        jnp.dot(norm_one_low, qkv_low, preferred_element_type=jnp.float32) + qkv_shift
    ).astype(jnp.bfloat16)
    query_rows = projected[:, :model_width].reshape(clip_count, row_count, head_count, HD)
    key_local = projected[:, model_width : 2 * model_width].reshape(
        clip_count, row_count, head_count, HD
    )
    value_local = projected[:, 2 * model_width :].reshape(clip_count, row_count, head_count, HD)
    key_rows, value_rows = (
        lax.all_gather(key_local, "ctx", axis=1, tiled=True),
        lax.all_gather(value_local, "ctx", axis=1, tiled=True),
    )
    attended, log_total = lax.map(attend, (query_rows, key_rows, value_rows))
    attended_low = attended.reshape(token_total, model_width).astype(jnp.bfloat16)
    branch = jnp.dot(attended_low, out_low, preferred_element_type=jnp.float32) + vector_rows[4]
    resid = flat_rows + branch
    norm_two, normed_two, inverse_two = normalize(resid, vector_rows[5], vector_rows[6])
    norm_two_low = norm_two.astype(jnp.bfloat16)
    pre_act = jnp.dot(norm_two_low, up_low, preferred_element_type=jnp.float32) + vector_rows[
        8:
    ].reshape(-1)
    act_low = (pre_act * normal_cdf(pre_act)).astype(jnp.bfloat16)
    mlp_out = jnp.dot(act_low, down_low, preferred_element_type=jnp.float32) + vector_rows[7]
    y_tokens = (resid + mlp_out).astype(jnp.bfloat16).reshape(clip_count, row_count, model_width)
    grad_output = out_grad.reshape(token_total, model_width)
    grad_float = grad_output.astype(jnp.float32)
    grad_down = jnp.einsum("tf,td->fd", act_low, grad_output, preferred_element_type=jnp.float32)
    down_shift = jnp.sum(grad_float, axis=0)
    grad_act = jnp.dot(grad_output, down_low.T, preferred_element_type=jnp.float32)
    density = jnp.exp(-0.5 * pre_act * pre_act) * 0.3989422804014327
    grad_pre = (grad_act * (normal_cdf(pre_act) + pre_act * density)).astype(jnp.bfloat16)
    grad_up = jnp.einsum("td,tf->df", norm_two_low, grad_pre, preferred_element_type=jnp.float32)
    up_shift = jnp.sum(grad_pre.astype(jnp.float32), axis=0)
    grad_norm_two = jnp.dot(grad_pre, up_low.T, preferred_element_type=jnp.float32)
    gain_two_grad = jnp.sum(grad_norm_two * normed_two, axis=0)
    shift_two_grad = jnp.sum(grad_norm_two, axis=0)
    grad_resid = grad_float + norm_back(grad_norm_two, vector_rows[5], normed_two, inverse_two)
    grad_branch = grad_resid.astype(jnp.bfloat16)
    grad_out = jnp.einsum(
        "td,te->de", attended_low, grad_branch, preferred_element_type=jnp.float32
    )
    out_shift = jnp.sum(grad_branch.astype(jnp.float32), axis=0)
    grad_attended = jnp.dot(grad_branch, out_low.T, preferred_element_type=jnp.float32).astype(
        jnp.bfloat16
    )
    grad_attended = grad_attended.reshape(clip_count, row_count, head_count, HD)
    grad_query, key_terms, value_terms = lax.map(
        attend_back, (query_rows, key_rows, value_rows, log_total, grad_attended)
    )
    grad_key, grad_value = (
        lax.psum_scatter(
            key_terms.astype(jnp.bfloat16), "ctx", scatter_dimension=1, tiled=True
        ).astype(jnp.float32),
        lax.psum_scatter(
            value_terms.astype(jnp.bfloat16), "ctx", scatter_dimension=1, tiled=True
        ).astype(jnp.float32),
    )
    grad_projected = jnp.concatenate(
        [
            grad_query.reshape(token_total, model_width),
            grad_key.reshape(token_total, model_width),
            grad_value.reshape(token_total, model_width),
        ],
        axis=1,
    ).astype(jnp.bfloat16)
    grad_qkv = jnp.einsum(
        "td,te->de", norm_one_low, grad_projected, preferred_element_type=jnp.float32
    )
    projected_sums = jnp.sum(grad_projected.astype(jnp.float32), axis=0)
    grad_norm_one = jnp.dot(grad_projected, qkv_low.T, preferred_element_type=jnp.float32)
    gain_one_grad = jnp.sum(grad_norm_one * normed_one, axis=0)
    shift_one_grad = jnp.sum(grad_norm_one, axis=0)
    x_grad = (
        grad_resid + norm_back(grad_norm_one, vector_rows[0], normed_one, inverse_one)
    ).astype(jnp.bfloat16)
    x_grad = x_grad.reshape(clip_count, row_count, model_width)
    first_rows = jnp.stack(
        [
            gain_one_grad,
            shift_one_grad,
            projected_sums[:model_width],
            projected_sums[2 * model_width :],
            out_shift,
            gain_two_grad,
            shift_two_grad,
            down_shift,
        ]
    )
    grad_vectors = jnp.concatenate([first_rows, up_shift.reshape(-1, model_width)], axis=0)
    group_size = lax.axis_size("ctx")
    vector_count = grad_vectors.shape[0]
    flat_vectors = (
        grad_vectors.reshape(vector_count, group_size, -1)
        .transpose(1, 0, 2)
        .reshape(group_size, -1)
    )
    shaped = (grad_qkv, grad_out, grad_up, grad_down, flat_vectors)
    spread = (
        lax.psum_scatter(
            shaped[0].astype(jnp.bfloat16), "dp", scatter_dimension=1, tiled=True
        ).astype(jnp.float32),
        lax.psum_scatter(
            shaped[1].astype(jnp.bfloat16), "dp", scatter_dimension=1, tiled=True
        ).astype(jnp.float32),
        lax.psum_scatter(
            shaped[2].astype(jnp.bfloat16), "dp", scatter_dimension=1, tiled=True
        ).astype(jnp.float32),
        lax.psum_scatter(
            shaped[3].astype(jnp.bfloat16), "dp", scatter_dimension=1, tiled=True
        ).astype(jnp.float32),
        lax.psum_scatter(
            shaped[4].astype(jnp.bfloat16), "dp", scatter_dimension=1, tiled=True
        ).astype(jnp.float32),
    )
    owned = (
        lax.psum_scatter(
            spread[0].astype(jnp.bfloat16), "ctx", scatter_dimension=0, tiled=True
        ).astype(jnp.float32),
        lax.psum_scatter(
            spread[1].astype(jnp.bfloat16), "ctx", scatter_dimension=0, tiled=True
        ).astype(jnp.float32),
        lax.psum_scatter(
            spread[2].astype(jnp.bfloat16), "ctx", scatter_dimension=0, tiled=True
        ).astype(jnp.float32),
        lax.psum_scatter(
            spread[3].astype(jnp.bfloat16), "ctx", scatter_dimension=0, tiled=True
        ).astype(jnp.float32),
        lax.psum_scatter(
            spread[4].astype(jnp.bfloat16), "ctx", scatter_dimension=0, tiled=True
        ).astype(jnp.float32),
    )
    collected = (
        lax.all_gather(owned[0].astype(jnp.bfloat16), "dp", axis=1, tiled=True).astype(jnp.float32),
        lax.all_gather(owned[1].astype(jnp.bfloat16), "dp", axis=1, tiled=True).astype(jnp.float32),
        lax.all_gather(owned[2].astype(jnp.bfloat16), "dp", axis=1, tiled=True).astype(jnp.float32),
        lax.all_gather(owned[3].astype(jnp.bfloat16), "dp", axis=1, tiled=True).astype(jnp.float32),
        lax.all_gather(owned[4].astype(jnp.bfloat16), "dp", axis=1, tiled=True).astype(jnp.float32),
    )
    shares = (
        collected[0],
        collected[1],
        collected[2],
        collected[3],
        collected[4].reshape(vector_count, -1),
    )
    qkv_moment, qkv_second, qkv_master = adam_update(
        w_qkv, shares[0], qkv_mean, qkv_square, matrix_rate, matrix_decay
    )
    out_moment, out_second, out_master = adam_update(
        w_out, shares[1], out_mean, out_square, matrix_rate, matrix_decay
    )
    up_moment, up_second, up_master = adam_update(
        w_up, shares[2], up_mean, up_square, matrix_rate, matrix_decay
    )
    down_moment, down_second, down_master = adam_update(
        w_down, shares[3], down_mean, down_square, matrix_rate, matrix_decay
    )
    vectors_moment, vectors_second, vectors_master = adam_update(
        vectors, shares[4], vectors_mean, vectors_square, vector_rate, 0.0
    )
    return (
        y_tokens,
        x_grad,
        qkv_moment,
        qkv_second,
        qkv_master,
        out_moment,
        out_second,
        out_master,
        up_moment,
        up_second,
        up_master,
        down_moment,
        down_second,
        down_master,
        vectors_moment,
        vectors_second,
        vectors_master,
    )


LOG2E = 1.4426950408889634
NT = (((1,), (1,)), ((), ()))
NN = (((1,), (0,)), ((), ()))
TN = (((0,), (0,)), ((), ()))
KERNEL_VMEM = 62 * 2**20


def attend_kernel(q_ref, k_ref, v_ref, o_ref, r_ref, p_ref, score_a, score_b, peak_a, peak_b):
    rows = score_a.shape[0]
    total = k_ref.shape[0]
    lane = lax.broadcasted_iota(jnp.int32, (1, 2 * HD), 1)
    held, peaks = (score_a, score_b), (peak_a, peak_b)
    parts = total // rows
    items = [(head, part) for head in range(2) for part in range(parts)]
    middle = total // 256 * 2 // 3 * 256
    upper = rows // 32 * 16 + 16

    def score(index, first, last):
        head, part = items[index]
        keys = jnp.where((lane // HD) == head, k_ref[...], 0).astype(jnp.bfloat16)[first:last]
        values = lax.dot_general(
            q_ref[part * rows : (part + 1) * rows, :], keys, NT, preferred_element_type=jnp.float32
        )
        held[index % 2][:, first:last] = values
        return jnp.max(values, axis=1, keepdims=True)

    def keep_peak(index, first, second):
        peaks[index % 2][...] = jnp.broadcast_to(jnp.maximum(first, second), (rows, 128))

    def soften(index, first, last):
        head, part = items[index]
        values = held[index % 2][first:last, :] - peaks[index % 2][first:last, 0:1]
        p_ref[head, part * rows + first : part * rows + last, :] = jnp.exp2(
            values * (0.125 * LOG2E)
        ).astype(jnp.bfloat16)

    def weigh(index):
        head, part = items[index]
        span = slice(part * rows, (part + 1) * rows)
        kept = jnp.where((lane // HD) == head, v_ref[...], 0).astype(jnp.bfloat16)
        table = jnp.concatenate([kept, jnp.ones((total, 2 * HD), jnp.bfloat16)], axis=1)
        out = lax.dot_general(p_ref[head, span, :], table, NN, preferred_element_type=jnp.float32)
        inverse = 1.0 / out[:, 2 * HD :]
        mixed = (out[:, : 2 * HD] * inverse).astype(jnp.bfloat16)
        if head == 0:
            o_ref[span, :] = mixed
            r_ref[span, :] = inverse
        else:
            o_ref[span, :] = jnp.where(lane < HD, o_ref[span, :], mixed)
            r_ref[span, :] = jnp.where(lane < HD, r_ref[span, :], inverse)

    keep_peak(0, score(0, 0, middle), score(0, middle, total))
    for index in range(len(items)):
        more = index + 1 < len(items)
        if more:
            first = score(index + 1, 0, middle)
        soften(index, 0, upper)
        if more:
            keep_peak(index + 1, first, score(index + 1, middle, total))
        soften(index, upper, rows)
        weigh(index)


def attend_back_kernel(
    q_ref, k_ref, v_ref, g_ref, o_ref, r_ref, p_ref, dq_ref, dk_ref, dv_ref, ds, qt, gt, dkt, dvt
):
    head = pl.program_id(1)
    total = k_ref.shape[0]
    half = total // 2
    lane = lax.broadcasted_iota(jnp.int32, (1, 2 * HD), 1)
    keep = (lane // HD) == head
    scaled = g_ref[...].astype(jnp.float32) * r_ref[...]

    @pl.when(head == 0)
    def _():
        qt[...] = q_ref[...].T
        gt[...] = scaled.astype(jnp.bfloat16).T

    delta = jnp.sum(jnp.where(keep, scaled * o_ref[...].astype(jnp.float32), 0.0), axis=1, keepdims=True)
    values = jnp.where(keep, v_ref[...], 0).astype(jnp.bfloat16)
    grad_probs = lax.dot_general(
        scaled.astype(jnp.bfloat16), values, NT, preferred_element_type=jnp.float32
    )
    ds[...] = (p_ref[...].astype(jnp.float32) * (grad_probs - delta)).astype(jnp.bfloat16)
    span = pl.ds(pl.multiple_of(head * HD, HD), HD)
    dvt[span, :] = lax.dot_general(gt[span, :], p_ref[...], NN, preferred_element_type=jnp.float32)
    dkt[span, :] = 0.125 * lax.dot_general(
        qt[span, :], ds[...], NN, preferred_element_type=jnp.float32
    )
    keys = jnp.where(keep, k_ref[...], 0).astype(jnp.bfloat16)
    for part in range(2):
        rows = slice(part * half, (part + 1) * half)
        term = 0.125 * lax.dot_general(ds[rows, :], keys, NN, preferred_element_type=jnp.float32)
        dq_ref[rows, :] = jnp.where(keep, term.astype(jnp.bfloat16), dq_ref[rows, :])

    @pl.when(head == 1)
    def _():
        dk_ref[...] = dkt[...].T.astype(jnp.bfloat16)
        dv_ref[...] = dvt[...].T.astype(jnp.bfloat16)


MESH = pl.DeviceIdType.MESH
GATHER_ORDERS = ("xab", "bxa", "abx")


def own_bits():
    place = lax.axis_index("dp")
    z = place // 4
    return {
        "z": z,
        "core": place % 2,
        "x": (place // 2) % 2,
        "a": (z % 2 + z // 2) % 2,
        "b": z // 2,
        "y": lax.axis_index("ctx"),
    }


def partner(name):
    place, group = lax.axis_index("dp"), lax.axis_index("ctx")
    z = place // 4
    if name == "core":
        return (place + 1 - 2 * (place % 2), group)
    if name == "x":
        return (place + 2 - 4 * ((place // 2) % 2), group)
    if name == "a":
        return (place + 4 - 8 * (z % 2), group)
    if name == "b":
        return (place + 4 * (3 - 2 * z), group)
    if name in ("z1", "z2", "z3"):
        return (place + 4 * ((z + int(name[1])) % 4 - z), group)
    return (place, 1 - group)


def meet_partners():
    barrier = pltpu.get_barrier_semaphore()
    names = ("core", "x", "y", "z1", "z2", "z3")
    for name in names:
        pl.semaphore_signal(barrier, inc=1, device_id=partner(name), device_id_type=MESH)
    pl.semaphore_wait(barrier, len(names))


def remote(source, target, name, send_sem, recv_sem):
    return pltpu.make_async_remote_copy(
        src_ref=source,
        dst_ref=target,
        send_sem=send_sem,
        recv_sem=recv_sem,
        device_id=partner(name),
        device_id_type=MESH,
    )


def local_copy(source, target, sem):
    return pltpu.make_async_copy(source, target, sem)


def block_of(order, bits):
    first, second, third = (bits[name] for name in order if name != "y")
    return first * 4 + second * 2 + third


class Gather:
    stages = 4

    def __init__(self, buffer, orders, send, recv):
        self.buffer, self.orders, self.send, self.recv = buffer, orders, send, recv

    def copy(self, stage, stream):
        bits = own_bits()
        order = self.orders[stream].replace("y", "")
        block = block_of(order, bits)
        size = (1, 2, 4, 8)[stage]
        name = "core" if stage == 3 else order[2 - stage]
        region = self.buffer.at[bits["core"], stream, pl.ds(block // size * size, size)]
        return remote(region, region, name, self.send.at[stage, stream], self.recv.at[stage, stream])

    def start(self, stage, stream):
        self.copy(stage, stream).start()

    def advance(self, stage, stream):
        self.copy(stage, stream).wait()
        if stage + 1 < self.stages:
            self.copy(stage + 1, stream).start()

    def begin(self):
        for stream in range(len(self.orders)):
            self.start(0, stream)

    def advance_all(self, stage):
        for stream in range(len(self.orders)):
            self.advance(stage, stream)


class StreamSum:
    def __init__(self, total, landing, shared, send, recv, local):
        self.total, self.landing, self.shared = total, landing, shared
        self.send, self.recv, self.local = send, recv, local

    def copies(self, stage):
        bits = own_bits()
        x, y, z = bits["x"], bits["y"], bits["z"]

        def make(source, target, name, at):
            return remote(source, target, name, self.send.at[at], self.recv.at[at])

        if stage == 1:
            return [make(self.total.at[:, 1 - y], self.landing[1], "y", 1)]
        if stage == 2:
            return [make(self.total.at[pl.ds((1 - x) * 4, 4), y], self.landing[2], "x", 2)]
        if stage == 3:
            return [
                make(
                    self.total.at[x * 4 + (z + d) % 4, y],
                    self.landing[3].at[d - 1],
                    "z" + str(d),
                    2 + d,
                )
                for d in (1, 2, 3)
            ]
        if stage == 4:
            return [
                make(
                    self.total.at[x * 4 + z, y],
                    self.shared.at[x * 4 + z],
                    "z" + str(d),
                    5 + d,
                )
                for d in (1, 2, 3)
            ]
        if stage == 5:
            region = self.shared.at[pl.ds(x * 4, 4)]
            return [make(region, region, "x", 9)]
        return [make(self.shared, self.shared, "core", 10)]

    def own_copy(self):
        bits = own_bits()
        block = bits["x"] * 4 + bits["z"]
        return local_copy(self.total.at[block, bits["y"]], self.shared.at[block], self.local)

    def start(self, stage):
        for copy in self.copies(stage):
            copy.start()
        if stage == 4:
            self.own_copy().start()

    def finish(self, stage):
        for copy in self.copies(stage):
            copy.wait()
        if stage == 4:
            self.own_copy().wait()
        if stage > 3:
            return
        bits = own_bits()
        x, y, z = bits["x"], bits["y"], bits["z"]
        start, size = ((0, 8), (x * 4, 4), (x * 4 + z, 1))[stage - 1]
        landed = self.landing[stage]

        @pl.loop(0, size)
        def _(block):
            here = self.total[start + block, y].astype(jnp.float32)
            if stage == 3:
                for d in range(3):
                    here = here + landed[d].astype(jnp.float32)
            else:
                here = here + landed[block].astype(jnp.float32)
            self.total[start + block, y] = here.astype(jnp.bfloat16)

    def move(self, stage):
        self.finish(stage)
        if stage < 6:
            self.start(stage + 1)


class CoreSum:
    def __init__(self, parts, total, landed, send, recv, local=None):
        self.parts, self.total, self.landed = parts, total, landed
        self.send, self.recv, self.local = send, recv, local

    def copy(self):
        away = 1 - own_bits()["core"]
        return remote(self.parts.at[away], self.landed, "core", self.send, self.recv)

    def start(self):
        self.copy().start()

    def finish(self):
        self.copy().wait()
        core = own_bits()["core"]

        @pl.loop(0, 8)
        def _(block):
            self.total[block] = (
                self.parts[core, block].astype(jnp.float32) + self.landed[block].astype(jnp.float32)
            ).astype(jnp.bfloat16)


def landing_shapes(stages, rows, columns):
    leads = {0: (8, 2), 1: (8,), 2: (4,), 3: (3,)}
    return [pltpu.VMEM(leads[stage] + (rows, columns), jnp.bfloat16) for stage in stages]


def sum_sems(streams):
    dma = pltpu.SemaphoreType.DMA
    return [dma((streams, 11)), dma((streams, 11)), dma((streams,))]


def gather_sems(streams):
    return [pltpu.SemaphoreType.DMA((4, streams)), pltpu.SemaphoreType.DMA((4, streams))]


def start_kernel(
    x_ref, vec_ref, wqkv_in, wout_in, wup_in, wdown_in,
    x2_out, proj_out, wqkv_out, wout_out, vecs_ref, norm_out, late_out,
    x2_ref, proj_ref, wqkv_ref, wout_ref, norm, late_ref, w_ref, other, wide, vec_other, g_send, g_recv, w_send, w_recv, x_send, x_recv, v_sem, l_sem, f_sem, o_sem,
):
    bits = own_bits()
    me = bits["y"]
    half, width = x_ref.shape[1], x_ref.shape[2]
    gather = Gather(other, GATHER_ORDERS, g_send, g_recv)
    side = width // 2
    leaving = []

    def leave(source, target):
        copy = local_copy(source, target, o_sem.at[len(leaving)])
        copy.start()
        leaving.append(copy)

    def leave_rows(source, target, at, size):
        leave(source.at[pl.ds(at, size)], target.at[pl.ds(at, size)])

    pieces_in = [[(wqkv_in.at[:, pl.ds(i * width, width)], 0, width)] for i in range(3)]
    pieces_in.append([(wout_in, 0, width)])
    pieces_in += [[(wdown_in.at[pl.ds(i * side, side)], 0, width)] for i in range(4)]
    pieces_in += [
        [(wup_in.at[:, pl.ds((i + 4 * j) * side, side)], j * side, side) for j in range(2)]
        for i in range(4)
    ]

    def fetch(index):
        slot = index % 4
        return [
            local_copy(source, wide.at[slot, :, pl.ds(at, size)], f_sem.at[index, k])
            for k, (source, at, size) in enumerate(pieces_in[index])
        ]

    def lower(index):
        for copy in fetch(index):
            copy.wait()
        rows = 32 if index < 4 else 64
        target = w_ref if index < 4 else late_ref
        count = side // rows
        for block in range(count):
            flat = index % 4 * count + block if index < 4 else (index - 4) * count + block
            target[flat // 24, flat // 8 % 3, flat % 8] = wide[
                index % 4, block * rows : (block + 1) * rows, :
            ].astype(jnp.bfloat16)
        if index + 4 < len(pieces_in):
            for copy in fetch(index + 4):
                copy.start()

    for index in range(4):
        for copy in fetch(index):
            copy.start()
    meet_partners()
    vec_copy = remote(vec_ref, vec_other, "y", v_sem.at[0], v_sem.at[1])
    vec_copy.start()
    own_x = local_copy(x_ref.at[me], x2_ref.at[pl.ds(0, half)], l_sem)
    own_x.start()
    for index in range(4):
        lower(index)
    pieces = []
    for stream in range(3):
        block = block_of(GATHER_ORDERS[stream], bits)
        piece = remote(
            w_ref.at[bits["core"], stream, block],
            other.at[bits["core"], stream, block],
            "y",
            w_send.at[stream],
            w_recv.at[stream],
        )
        piece.start()
        pieces.append(piece)
    first = half // 32 * 16 + 16
    second = (half - first) // 48 * 32
    spans = [(0, first), (first, second), (first + second, half - first - second)]
    trades = [
        remote(
            x_ref.at[1 - me, pl.ds(at, size)],
            x2_ref.at[pl.ds(half + at, size)],
            "y",
            x_send.at[index],
            x_recv.at[index],
        )
        for index, (at, size) in enumerate(spans)
    ]
    for piece in pieces:
        piece.wait()
    gather.begin()
    trades[0].start()
    vec_copy.wait()
    mine, others = vec_ref[...], vec_other[...]
    vecs_ref[...] = jnp.where(
        me == 0,
        jnp.concatenate([mine, others], axis=1),
        jnp.concatenate([others, mine], axis=1),
    )
    for c in range(4):
        half_at = slice(c % 2 * (width // 2), (c % 2 + 1) * (width // 2))
        vecs_ref[12 + c : 13 + c, :] = jnp.concatenate(
            [vecs_ref[8 + c // 2 : 9 + c // 2, half_at], vecs_ref[10 + c // 2 : 11 + c // 2, half_at]],
            axis=1,
        )
    gather.advance_all(0)
    for trade in trades[1:]:
        trade.start()

    def norm_rows(at, size):
        values = x2_ref[at : at + size, :].astype(jnp.float32)
        normed, _, _ = normalize(values, vecs_ref[0:1, :], vecs_ref[1:2, :])
        norm[at : at + size, :] = normed.astype(jnp.bfloat16)

    own_x.wait()
    leave_rows(x2_ref, x2_out, 0, half)
    norm_rows(0, half)
    leave_rows(norm, norm_out, 0, half)
    gather.advance_all(1)
    for index in range(4, 8):
        lower(index)
    gather.advance_all(2)
    for index in range(8, 12):
        lower(index)
    leave(late_ref, late_out)
    gather.advance_all(3)
    part = width // 2

    for source, at in ((w_ref, me * part), (other, (1 - me) * part)):
        for matrix in range(4):
            for index in range(12):
                flat = matrix * 12 + index
                block = source[flat // 24, flat // 8 % 3, flat % 8]
                rows = pl.ds(pl.multiple_of(at + index * 32, 32), 32)
                if matrix < 3:
                    wqkv_ref[rows, matrix * width : (matrix + 1) * width] = block
                else:
                    wout_ref[rows, :] = block

    leave(wqkv_ref, wqkv_out)
    leave(wout_ref, wout_out)

    def project(at, size):
        @pl.loop(0, 3)
        def _(matrix):
            cols = pl.ds(pl.multiple_of(matrix * width, 128), width)
            shift = jnp.where(matrix == 0, vecs_ref[2:3, :], vecs_ref[3:4, :])
            shift = jnp.where(matrix == 1, 0.0, shift)
            proj_ref[at : at + size, cols] = (
                lax.dot_general(
                    norm[at : at + size, :], wqkv_ref[:, cols], NN, preferred_element_type=jnp.float32
                )
                + shift
            ).astype(jnp.bfloat16)

        leave_rows(proj_ref, proj_out, at, size)

    project(0, half)
    for trade, (at, size) in zip(trades, spans):
        trade.wait()
        leave_rows(x2_ref, x2_out, half + at, size)
        norm_rows(half + at, size)
        leave_rows(norm, norm_out, half + at, size)
        project(half + at, size)
    for copy in leaving:
        copy.wait()


def start_call(x_tokens, vector_own, w_qkv, w_out, w_up, w_down):
    _, half, width = x_tokens.shape
    low = jnp.bfloat16
    anywhere = pl.BlockSpec(memory_space=pl.ANY)
    vmem = pl.BlockSpec(memory_space=pltpu.VMEM)
    dma = pltpu.SemaphoreType.DMA
    return pl.pallas_call(
        start_kernel,
        in_specs=[anywhere, vmem] + [anywhere] * 4,
        out_specs=[anywhere] * 4 + [vmem] + [anywhere] * 2,
        out_shape=[
            jax.ShapeDtypeStruct((2 * half, width), low),
            jax.ShapeDtypeStruct((2 * half, 3 * width), low),
            jax.ShapeDtypeStruct((width, 3 * width), low),
            jax.ShapeDtypeStruct((width, width), low),
            jax.ShapeDtypeStruct((16, width), jnp.float32),
            jax.ShapeDtypeStruct((2 * half, width), low),
            jax.ShapeDtypeStruct((2, 3, 8, 64, width), low),
        ],
        scratch_shapes=[
            pltpu.VMEM((2 * half, width), low),
            pltpu.VMEM((2 * half, 3 * width), low),
            pltpu.VMEM((width, 3 * width), low),
            pltpu.VMEM((width, width), low),
            pltpu.VMEM((2 * half, width), low),
            pltpu.VMEM((2, 3, 8, 64, width), low),
            pltpu.VMEM((2, 3, 8, 32, width), low),
            pltpu.VMEM((2, 3, 8, 32, width), low),
            pltpu.VMEM((4, width // 2, width), jnp.float32),
            pltpu.VMEM(vector_own.shape, jnp.float32),
        ]
        + gather_sems(3)
        + [dma((3,)), dma((3,)), dma((3,)), dma((3,)), dma((2,)), dma, dma((12, 2)), dma((16,))],
        compiler_params=pltpu.CompilerParams(
            vmem_limit_bytes=KERNEL_VMEM, collective_id=1, has_side_effects=True
        ),
        name="start",
    )(x_tokens, vector_own, w_qkv, w_out, w_up, w_down)


def attend_gather_kernel(
    q_ref, k_ref, v_ref, grad_ref, w_ref, o_ref, r_ref, p_ref, other_ref, got_ref,
    score_a, score_b, peak_a, peak_b, g_send, g_recv, t_send, t_recv, w_send, w_recv,
):
    step = pl.program_id(0)
    last = pl.num_programs(0) - 1
    me = own_bits()["y"]
    gather = Gather(other_ref, GATHER_ORDERS, g_send, g_recv)
    trade = remote(grad_ref.at[1 - me], got_ref, "y", t_send, t_recv)
    bits = own_bits()
    pieces = [
        remote(
            w_ref.at[bits["core"], stream, block_of(order, bits)],
            other_ref.at[bits["core"], stream, block_of(order, bits)],
            "y",
            w_send.at[stream],
            w_recv.at[stream],
        )
        for stream, order in enumerate(GATHER_ORDERS)
    ]

    @pl.when(step == 0)
    def _():
        meet_partners()
        for piece in pieces:
            piece.start()

    @pl.when(step == 1)
    def _():
        for piece in pieces:
            piece.wait()
        gather.begin()
        trade.start()

    for stage, at in enumerate(GATHER_STEPS):
        @pl.when(step == at)
        def _(stage=stage):
            gather.advance_all(stage)

    attend_kernel(
        q_ref, k_ref, v_ref, o_ref, r_ref, p_ref, score_a, score_b, peak_a, peak_b
    )

    @pl.when(step == last)
    def _():
        gather.advance_all(3)
        trade.wait()


GATHER_STEPS = (2, 3, 5)


def attend_call(projected, out_grad, weights, width):
    total = projected.shape[0]
    pairs = width // (2 * HD)
    half = out_grad.shape[1]
    anywhere = pl.BlockSpec(memory_space=pl.ANY)
    dma = pltpu.SemaphoreType.DMA

    def columns(start):
        return pl.BlockSpec((total, 2 * HD), lambda p: (0, start * pairs + p))

    return pl.pallas_call(
        attend_gather_kernel,
        grid=(pairs,),
        in_specs=[columns(0), columns(1), columns(2), anywhere, anywhere],
        out_specs=[
            columns(0),
            columns(0),
            pl.BlockSpec((2, total, total), lambda p: (p, 0, 0)),
            anywhere,
            anywhere,
        ],
        out_shape=[
            jax.ShapeDtypeStruct((total, width), jnp.bfloat16),
            jax.ShapeDtypeStruct((total, width), jnp.float32),
            jax.ShapeDtypeStruct((2 * pairs, total, total), jnp.bfloat16),
            jax.ShapeDtypeStruct(weights.shape, jnp.bfloat16),
            jax.ShapeDtypeStruct((half, width), jnp.bfloat16),
        ],
        scratch_shapes=[pltpu.VMEM((total // 2, total), jnp.float32)] * 2
        + [pltpu.VMEM((total // 2, 128), jnp.float32)] * 2
        + gather_sems(3)
        + [dma, dma, dma((3,)), dma((3,))],
        compiler_params=pltpu.CompilerParams(
            vmem_limit_bytes=KERNEL_VMEM, collective_id=2, has_side_effects=True
        ),
        cost_estimate=pl.CostEstimate(
            flops=16 * pairs * total * total * 2 * HD,
            bytes_accessed=4 * pairs * total * total,
            transcendentals=2 * pairs * total * total,
        ),
        name="attend",
    )(projected, projected, projected, out_grad, weights)


BACK_FIRST = (4, 3, 2, 1)
BACK_STAGES = ((), (3,), (2, 3), (1, 2, 3), (0, 1, 2, 3), (0, 1, 2, 3), (0, 1))
BACK_MOVES = (
    (2, ((4, 0),)),
    (3, ((2, 2),)),
    (4, ((0, 4), (1, 3))),
    (5, ((2, 3), (3, 1), (4, 1), (5, 0))),
    (6, ((0, 5), (1, 4))),
    (7, ((0, 6), (2, 4), (4, 2), (3, 2))),
    (8, ((4, 3), (5, 1), (1, 5))),
    (9, ((2, 5), (1, 6), (3, 3), (5, 2), (6, 0))),
    (10, ((4, 4), (2, 6))),
    (11, ((4, 5),)),
)
BACK_LAST = ((4, 6), (3, 4), (5, 3), (6, 1))
TRADE_STEP = 3


def attend_back_sum_kernel(
    q_ref, k_ref, v_ref, g_ref, o_ref, r_ref, p_ref, partial_ref, y2_ref, norm_ref, out_ref,
    dq_ref, dk_ref, dv_ref, late_ref, first_ref, tokens_ref, third_ref, parts_out,
    ds, qt, gt, dkt, dvt, total, small, parts, turned, *rest,
):
    landing, rest = rest[:-7], rest[-7:]
    s_send, s_recv, s_local, t_send, t_recv, l_sem, o_sem = rest
    pair, head = pl.program_id(0), pl.program_id(1)
    step = pair * 2 + head
    last = pl.num_programs(0) * 2 - 1
    core = own_bits()["core"]
    half = tokens_ref.shape[0]
    streams, cores, held = [], {}, list(landing)
    for index, stages in enumerate(BACK_STAGES):
        buffers = {stage: held.pop(0) for stage in stages}
        sems = (s_send.at[index], s_recv.at[index], s_local.at[index])
        if index < 4:
            shared, sums = late_ref.at[core, index], total.at[index]
        else:
            shared, sums = first_ref.at[core, index - 4], small.at[index - 4]
            source = parts.at[1 if index == 4 else (index - 5) % 2]
            cores[index] = CoreSum(
                source, sums, buffers[0], s_send.at[index, 0], s_recv.at[index, 0]
            )
        streams.append(StreamSum(sums, buffers, shared, *sems))
    trade = remote(y2_ref.at[pl.ds(half, half)], tokens_ref, "y", t_send, t_recv)
    load = local_copy(partial_ref, total, l_sem.at[1])
    load_out = local_copy(out_ref, parts.at[1], l_sem.at[3])
    load_norm = local_copy(norm_ref, ds.at[:, pl.ds(0, norm_ref.shape[1])], l_sem.at[2])

    @pl.when(step == 0)
    def _():
        load.start()
        load_norm.start()
        load_out.start()
        meet_partners()
        load_out.wait()
        cores[4].start()
        load_norm.wait()
        turned[...] = ds[:, : norm_ref.shape[1]].T
        load.wait()
        for index, stage in enumerate(BACK_FIRST):
            streams[index].start(stage)

    for at, moves in BACK_MOVES:
        @pl.when(step == at)
        def _(at=at, moves=moves):
            for index, stage in moves:
                if stage == 0:
                    cores[index].finish()
                    streams[index].start(1)
                else:
                    streams[index].move(stage)
            if at == TRADE_STEP:
                trade.start()

    attend_back_kernel(
        q_ref, k_ref, v_ref, g_ref, o_ref, r_ref, p_ref, dq_ref, dk_ref, dv_ref, ds, qt, gt, dkt, dvt
    )

    @pl.when(head == 1)
    def _():
        sides = jnp.concatenate([dq_ref[...], dk_ref[...], dv_ref[...]], axis=1)
        values = lax.dot_general(
            turned[...], sides, NN, preferred_element_type=jnp.float32
        ).astype(jnp.bfloat16)
        slot, part = (pair // 2) % 2, pair % 2
        rows = parts.shape[4]
        for side in range(2):
            for block in range(8):
                at = side * 8 * rows + block * rows
                parts[slot, part, block, side] = values[at : at + rows, :]

    for index, at in ((5, 3), (6, 7)):
        @pl.when(step == at)
        def _(index=index):
            cores[index].start()

    @pl.when(step == last)
    def _():
        hand = local_copy(parts.at[0], parts_out, o_sem.at[0])
        hand.start()
        for index, stage in BACK_LAST:
            streams[index].finish(stage)
        third = local_copy(small.at[2], third_ref.at[0], o_sem.at[1])
        third.start()
        second = local_copy(small.at[1], third_ref.at[1], o_sem.at[2])
        second.start()
        trade.wait()
        hand.wait()
        second.wait()
        third.wait()


def attend_back_call(projected, upstream, attended, inverse, exponent, partial, y2, norm, out_parts):
    total, width = attended.shape
    pairs = width // (2 * HD)
    streams, _, _, rows, _ = partial.shape
    side = width // 2
    low = jnp.bfloat16
    anywhere = pl.BlockSpec(memory_space=pl.ANY)
    dma = pltpu.SemaphoreType.DMA

    def columns(start):
        return pl.BlockSpec((total, 2 * HD), lambda p, h: (0, start * pairs + p))

    landing = []
    for index, stages in enumerate(BACK_STAGES):
        landing += landing_shapes(stages, rows, width if index < 4 else side)
    return pl.pallas_call(
        attend_back_sum_kernel,
        grid=(pairs, 2),
        in_specs=[columns(0), columns(1), columns(2), columns(0), columns(0), columns(0)]
        + [pl.BlockSpec((None, total, total), lambda p, h: (p * 2 + h, 0, 0))]
        + [anywhere] * 4,
        out_specs=[columns(0)] * 3 + [anywhere] * 5,
        out_shape=[jax.ShapeDtypeStruct((total, width), low)] * 3
        + [
            jax.ShapeDtypeStruct((2, streams, 8, rows, width), low),
            jax.ShapeDtypeStruct((2, 4, 8, rows, side), low),
            jax.ShapeDtypeStruct((total // 2, width), low),
            jax.ShapeDtypeStruct((2, 8, 2, rows, side), low),
            jax.ShapeDtypeStruct((2, 8, 2, rows, side), low),
        ],
        scratch_shapes=[pltpu.VMEM((total, total), low)]
        + [pltpu.VMEM((2 * HD, total), low)] * 2
        + [pltpu.VMEM((2 * HD, total), jnp.float32)] * 2
        + [
            pltpu.VMEM(partial.shape, low),
            pltpu.VMEM((3, 8, 2, rows, side), low),
            pltpu.VMEM((2, 2, 8, 2, rows, side), low),
            pltpu.VMEM((width, total), low),
        ]
        + landing
        + sum_sems(len(BACK_STAGES))
        + [dma, dma, dma((4,)), dma((3,))],
        compiler_params=pltpu.CompilerParams(
            vmem_limit_bytes=KERNEL_VMEM, collective_id=3, has_side_effects=True
        ),
        cost_estimate=pl.CostEstimate(
            flops=32 * pairs * total * total * 2 * HD,
            bytes_accessed=4 * pairs * total * total,
            transcendentals=0,
        ),
        name="attend_back",
    )(
        projected, projected, projected, upstream, attended, inverse, exponent, partial, y2, norm,
        out_parts,
    )


LAST_FIRST = ((0, 5), (1, 4), (2, 2))
LAST_STAGES = ((), (), (2, 3), (0, 1, 2, 3))
LAST_MOVES = (
    ((3, 0),),
    ((3, 1), (1, 4), (2, 2), (0, 5)),
    ((3, 2), (2, 3), (1, 5)),
    ((3, 3), (0, 6)),
    ((2, 4), (1, 6)),
    ((3, 4),),
    ((2, 5),),
    ((3, 5),),
    ((2, 6),),
    ((3, 6),),
)


def finish_kernel(
    dq_in, dk_in, dv_in, x_in, w_in, resid_in, vec_ref, part_ref, late_in, first_in, small_in,
    parts_ref,
    xg_ref, vsum_ref, late_ref, first_ref,
    dq_ref, dk_ref, dv_ref, x_ref, w_ref, resid_ref, sent_rows, own_rows, coming, small, *rest,
):
    landing, rest = rest[:-10], rest[-10:]
    s_send, s_recv, s_local, t_send, t_recv, l_sem, v_land, v_send, v_recv, i_sem = rest
    bits = own_bits()
    me, core = bits["y"], bits["core"]
    rows, width = x_ref.shape
    half = rows // 2
    streams, held = [], list(landing)
    for index, stages in enumerate(LAST_STAGES):
        buffers = {stage: held.pop(0) for stage in stages}
        sems = (s_send.at[index], s_recv.at[index], s_local.at[index])
        shared = late_ref.at[core, 3] if index == 0 else first_ref.at[core, index]
        streams.append(
            StreamSum(None if index == 0 else small.at[index - 1], buffers, shared, *sems)
        )
    core_sum = CoreSum(
        parts_ref, small.at[2], streams[3].landing[0], s_send.at[3, 0], s_recv.at[3, 0]
    )
    entering = {}
    for part, at in ((1, half), (0, 0)):
        copies = []
        for k, (source, target) in enumerate(
            ((dq_in, dq_ref), (dk_in, dk_ref), (dv_in, dv_ref), (x_in, x_ref), (resid_in, resid_ref))
        ):
            span = pl.ds(at, half)
            copies.append(local_copy(source.at[span], target.at[span], i_sem.at[part, k]))
        if part == 1:
            copies.append(local_copy(w_in, w_ref, i_sem.at[1, 5]))
        for copy in copies:
            copy.start()
        entering[part] = copies
    loads = [local_copy(small_in.at[1 - i], small.at[i], l_sem.at[1 + i]) for i in range(2)]
    for load in loads:
        load.start()
    gain, shift = vec_ref[0:1, :], vec_ref[1:2, :]
    meet_partners()
    core_sum.start()
    for load in loads:
        load.wait()
    for index, stage in LAST_FIRST:
        streams[index].start(stage)

    def turn(at):
        for index, stage in LAST_MOVES[at]:
            if stage == 0:
                core_sum.finish()
                streams[index].start(1)
            else:
                streams[index].move(stage)

    step = half // 7

    def products(at):
        span = slice(at, at + half)
        for matrix, part in enumerate((dq_ref, dk_ref, dv_ref)):
            term = lax.dot_general(
                part[span, :],
                w_ref[:, matrix * width : (matrix + 1) * width],
                NT,
                preferred_element_type=jnp.float32,
            )
            if matrix == 0:
                coming[...] = term
            else:
                coming[...] += term

    def input_rows(at, target):
        @pl.loop(0, 7)
        def _(index):
            here = pl.ds(pl.multiple_of(index * step, 16), step)
            span = pl.ds(pl.multiple_of(at + index * step, 16), step)
            upstream = coming[here, :]
            _, normed, inverse = normalize(x_ref[span, :].astype(jnp.float32), gain, shift)
            target[here, :] = (
                resid_ref[span, :] + norm_back(upstream, gain, normed, inverse)
            ).astype(jnp.bfloat16)
            vsum_ref[0:1, :] += jnp.sum(upstream * normed, axis=0, keepdims=True)
            vsum_ref[1:2, :] += jnp.sum(upstream, axis=0, keepdims=True)

    vsum_ref[...] = part_ref[...]
    turn(0)
    for copy in entering[1]:
        copy.wait()
    products(half)
    input_rows(half, sent_rows)
    trade = remote(sent_rows, xg_ref.at[me], "y", t_send, t_recv)
    trade.start()
    turn(1)
    for copy in entering[0]:
        copy.wait()
    products(0)
    turn(2)
    input_rows(0, own_rows)
    own = local_copy(own_rows, xg_ref.at[me], l_sem.at[0])
    own.start()
    vsum_ref[2:3, :] = jnp.sum(dq_ref[...].astype(jnp.float32), axis=0, keepdims=True)
    vsum_ref[3:4, :] = jnp.sum(dv_ref[...].astype(jnp.float32), axis=0, keepdims=True)

    def vector_step(stage):
        name = ("core", "x", "a", "b", "y")[stage]
        return remote(vsum_ref, v_land.at[stage], name, v_send.at[stage], v_recv.at[stage])

    vector_step(0).start()
    for at in range(3, len(LAST_MOVES)):
        turn(at)
        if at < 8:
            vector_step(at - 3).wait()
            vsum_ref[...] += v_land[at - 3]
            if at < 7:
                vector_step(at - 2).start()
    trade.wait()
    own.wait()


def finish_call(grad_parts, x2, wqkv, grad_resid, vecs, part_sums, late, first, small, parts):
    total, width = x2.shape
    low = jnp.bfloat16
    anywhere = pl.BlockSpec(memory_space=pl.ANY)
    vmem = pl.BlockSpec(memory_space=pltpu.VMEM)
    dma = pltpu.SemaphoreType.DMA
    rows, side = small.shape[3], small.shape[4]
    landing = []
    for stages in LAST_STAGES:
        landing += landing_shapes(stages, rows, side)
    return pl.pallas_call(
        finish_kernel,
        in_specs=[anywhere] * 6 + [vmem] * 2 + [anywhere] * 3 + [vmem],
        out_specs=[anywhere, vmem, anywhere, anywhere],
        out_shape=[
            jax.ShapeDtypeStruct((2, total // 2, width), low),
            jax.ShapeDtypeStruct((16, width), jnp.float32),
            jax.ShapeDtypeStruct(late.shape, low),
            jax.ShapeDtypeStruct(first.shape, low),
        ],
        input_output_aliases={8: 2, 9: 3},
        scratch_shapes=[pltpu.VMEM((total, width), low)] * 4
        + [
            pltpu.VMEM((width, 3 * width), low),
            pltpu.VMEM((total, width), jnp.float32),
            pltpu.VMEM((total // 2, width), low),
            pltpu.VMEM((total // 2, width), low),
            pltpu.VMEM((total // 2, width), jnp.float32),
            pltpu.VMEM((3, 8, 2, rows, side), low),
        ]
        + landing
        + sum_sems(len(LAST_STAGES))
        + [dma, dma, dma((3,)), pltpu.VMEM((5, 16, width), jnp.float32), dma((5,)), dma((5,)), dma((2, 6))],
        compiler_params=pltpu.CompilerParams(
            vmem_limit_bytes=KERNEL_VMEM, collective_id=4, has_side_effects=True
        ),
        name="finish",
    )(*grad_parts, x2, wqkv, grad_resid, vecs, part_sums, late, first, small, parts)


def update_kernel(*refs):
    groups = [refs[3 * i : 3 * i + 3] for i in range(4)]
    late_ref, first_ref, y_in, y_got, xg_in = refs[12:17]
    outs = [refs[17 + 3 * i : 20 + 3 * i] for i in range(4)]
    y_out, xg_out = refs[29:31]
    wide, share, through, in_sem, out_sem, t_sem = refs[31:]
    me = lax.axis_index("ctx")
    side = wide.shape[2]
    width = 2 * side
    slots = wide.shape[0]
    ahead = slots // 2
    half = through.shape[1]
    passing = [
        (y_in.at[pl.ds(0, half)], through.at[0], y_out.at[me]),
        (y_got, through.at[1], y_out.at[1 - me]),
    ] + [(xg_in.at[part], through.at[2 + part], xg_out.at[part]) for part in range(2)]
    brought = [
        local_copy(source, held, t_sem.at[0, k]) for k, (source, held, _) in enumerate(passing)
    ]
    taken = [
        local_copy(held, target, t_sem.at[1, k]) for k, (_, held, target) in enumerate(passing)
    ]

    def columns(at, size, into):
        return lambda ref: ref.at[:, pl.ds(at, size)], into, size

    units = []
    for c in range(4):
        rows = lambda ref, c=c: ref.at[pl.ds(c * side, side)]
        units.append((3, [(rows, 0, width)], [(late_ref.at[0, c], 0, width)], False))
        halves = [columns((c + 4 * j) * side, side, j * side) for j in range(2)]
        units.append((2, halves, [(late_ref.at[1, c], 0, width)], False))
    for k in range(4):
        shares = [(first_ref.at[part, k], part * side, side) for part in range(2)]
        if k == 0:
            units.append((1, [columns(0, width, 0)], shares, False))
        else:
            third = width // 3
            thirds = [
                columns(m * width + (k - 1) * third, third, m * third) for m in range(3)
            ]
            units.append((0, thirds, shares, True))

    def loads(index):
        which, spans, shares, _ = units[index]
        slot = index % slots
        copies = []
        for k in range(3):
            for part, (view, into, size) in enumerate(spans):
                copies.append(
                    local_copy(
                        view(groups[which][k]),
                        wide.at[slot, k, :, pl.ds(into, size)],
                        in_sem.at[index, k * 3 + part],
                    )
                )
        for part, (source, into, size) in enumerate(shares):
            copies.append(
                local_copy(source, share.at[slot, :, :, pl.ds(into, size)], in_sem.at[index, 9 + part])
            )
        return copies

    def stores(index):
        which, spans, _, _ = units[index]
        slot = index % slots
        return [
            local_copy(
                wide.at[slot, k, :, pl.ds(into, size)],
                view(outs[which][k]),
                out_sem.at[index, k * 3 + part],
            )
            for k in range(3)
            for part, (view, into, size) in enumerate(spans)
        ]

    def compute(index):
        slot, pairs = index % slots, units[index][3]
        rows = share.shape[2]

        @pl.loop(0, 8)
        def _(block):
            gradient = share[slot, block].astype(jnp.float32)
            if pairs:
                piece = 2 * HD
                gradient = jnp.concatenate(
                    [
                        gradient[:, part * side + m * piece : part * side + (m + 1) * piece]
                        for m in range(3)
                        for part in range(2)
                    ],
                    axis=1,
                )
            span = pl.ds(pl.multiple_of(block * rows, 16), rows)
            weight, first, second = (wide[slot, k, span, :] for k in range(3))
            new = adam_update(weight, gradient, first, second, matrix_rate, matrix_decay)
            wide[slot, 0, span, :] = new[2]
            wide[slot, 1, span, :] = new[0]
            wide[slot, 2, span, :] = new[1]

    for index in range(ahead):
        for copy in loads(index):
            copy.start()
    for copy in brought:
        copy.start()
    for index in range(len(units)):
        if index + ahead < len(units):
            if index + ahead >= slots:
                for copy in stores(index + ahead - slots):
                    copy.wait()
            for copy in loads(index + ahead):
                copy.start()
        for copy in loads(index):
            copy.wait()
        compute(index)
        for copy in stores(index):
            copy.start()
        if index == 2:
            for copy in brought:
                copy.wait()
            for copy in taken:
                copy.start()
    for index in range(len(units) - slots, len(units)):
        for copy in stores(index):
            copy.wait()
    for copy in taken:
        copy.wait()


def update_call(groups, late, first, y_rows, y_got, x_grad):
    flat = [member for group in groups for member in group]
    anywhere = pl.BlockSpec(memory_space=pl.ANY)
    side, width = groups[1][0].shape
    dma = pltpu.SemaphoreType.DMA
    shapes = [jax.ShapeDtypeStruct(member.shape, member.dtype) for member in flat]
    *new, y_new, x_new = pl.pallas_call(
        update_kernel,
        in_specs=[anywhere] * 17,
        out_specs=[anywhere] * 14,
        out_shape=shapes
        + [jax.ShapeDtypeStruct(x_grad.shape, x_grad.dtype)] * 2,
        scratch_shapes=[
            pltpu.VMEM((6, 3, side, width), jnp.float32),
            pltpu.VMEM((6, 8, side // 8, width), jnp.bfloat16),
            pltpu.VMEM((4,) + y_got.shape, jnp.bfloat16),
            dma((12, 11)),
            dma((12, 9)),
            dma((2, 4)),
        ],
        compiler_params=pltpu.CompilerParams(vmem_limit_bytes=KERNEL_VMEM),
        name="update",
    )(*flat, late, first, y_rows, y_got, x_grad)
    return new, y_new, x_new


def middle_kernel(
    att_ref, x_ref, grad_ref, got_ref, vec_ref, wo_ref, mine_ref, other_ref,
    y_out, gr_out, ga_out, partial_ref, go_ref, sums_ref,
    y_ref, gr_ref, ga_ref, up_w, down_w, g_ref, mlp, upstream, acts, grads_pre, grads, total, *rest,
):
    landing, rest = rest[:-6], rest[-6:]
    s_send, s_recv, s_local, w_sem, x_sem, o_sem = rest
    bits = own_bits()
    me, core = bits["y"], bits["core"]
    rows, width = g_ref.shape
    half = rows // 2
    side = width // 2
    chunks = total.shape[0]
    piece = total.shape[3]
    resid, low_rows = gr_ref, ga_ref
    streams, cores, held = [], [], list(landing[2:])
    for index, stages in enumerate(MIDDLE_STAGES):
        buffers = {stage: held.pop(0) for stage in stages}
        sems = (s_send.at[index], s_recv.at[index], s_local.at[index])
        streams.append(StreamSum(total.at[index], buffers, None, *sems))
        cores.append(
            CoreSum(
                grads, total.at[index], landing[index % 2], s_send.at[index, 0], s_recv.at[index, 0]
            )
        )

    own_x = local_copy(x_ref, y_ref, x_sem.at[0])
    own_x.start()
    loads = [
        local_copy(grad_ref.at[me], g_ref.at[pl.ds(0, half)], x_sem.at[1]),
        local_copy(got_ref, g_ref.at[pl.ds(half, half)], x_sem.at[2]),
    ]
    for index, (source, at) in enumerate(((mine_ref, me), (other_ref, 1 - me))):
        for c in range(chunks):
            part = pl.ds(pl.multiple_of(c * width + at * side, 16), side)
            loads.append(
                local_copy(source.at[pl.ds(c * side, side)], down_w.at[part], w_sem.at[index, c])
            )
            part = pl.ds(pl.multiple_of(at * side, 16), side)
            loads.append(
                local_copy(
                    source.at[pl.ds((chunks + c) * side, side)],
                    up_w.at[part, pl.ds(c * width, width)],
                    w_sem.at[index, chunks + c],
                )
            )
    for load in loads:
        load.start()
    meet_partners()
    own_x.wait()
    gain = vec_ref[5:6, :]
    step = rows // 7

    resid[...] = lax.dot_general(att_ref[...], wo_ref[...], NN, preferred_element_type=jnp.float32)

    @pl.loop(0, 7)
    def _(index):
        span = pl.ds(pl.multiple_of(index * step, 16), step)
        resid[span, :] = y_ref[span, :].astype(jnp.float32) + (resid[span, :] + vec_ref[4:5, :])
        normed_two, _, _ = normalize(resid[span, :], gain, vec_ref[6:7, :])
        low_rows[span, :] = normed_two.astype(jnp.bfloat16)

    for load in loads:
        load.wait()
    sums_ref[...] = jnp.zeros_like(sums_ref)
    mlp[...] = jnp.zeros_like(mlp)
    upstream[...] = jnp.zeros_like(upstream)

    def column_sum(values):
        return jnp.sum(values, axis=0, keepdims=True)

    @pl.loop(0, chunks)
    def _(c):
        cols = pl.ds(pl.multiple_of(c * width, 128), width)
        shift = vec_ref[pl.ds(12 + c, 1), :]
        for part in range(2):
            span = slice(part * half, (part + 1) * half)
            pre = (
                lax.dot_general(
                    low_rows[span, :], up_w[:, cols], NN, preferred_element_type=jnp.float32
                )
                + shift
            )
            below = normal_cdf(pre)
            acts[span, :] = (pre * below).astype(jnp.bfloat16)
            density = jnp.exp(-0.5 * pre * pre) * 0.3989422804014327
            grad_act = lax.dot_general(
                g_ref[span, :], down_w[cols, :], NT, preferred_element_type=jnp.float32
            )
            grad_pre = (grad_act * (below + pre * density)).astype(jnp.bfloat16)
            grads_pre[span, :] = grad_pre
            sums_ref[pl.ds(12 + c, 1), :] += column_sum(grad_pre.astype(jnp.float32))
            mlp[span, :] += lax.dot_general(
                acts[span, :], down_w[cols, :], NN, preferred_element_type=jnp.float32
            )
            upstream[span, :] += lax.dot_general(
                grads_pre[span, :], up_w[:, cols], NT, preferred_element_type=jnp.float32
            )

        for chunk, moves in enumerate(MIDDLE_MOVES):
            @pl.when(c == chunk)
            def _(moves=moves):
                for index, stage in moves:
                    if stage == 0:
                        cores[index].finish()
                        streams[index].start(1)
                    else:
                        streams[index].move(stage)

        def put(which, values):
            for part in range(2):
                for block in range(8):
                    at = part * side + block * piece
                    grads[which, block, part] = values[at : at + piece, :].astype(jnp.bfloat16)

        put(0, lax.dot_general(acts[...], g_ref[...], TN, preferred_element_type=jnp.float32))
        put(
            1, lax.dot_general(low_rows[...], grads_pre[...], TN, preferred_element_type=jnp.float32)
        )
        for index in range(chunks):
            @pl.when(c == index)
            def _(index=index):
                cores[index].start()

    for c in range(chunks):
        at = slice(c % 2 * side, (c % 2 + 1) * side)
        sums_ref[8 + c // 2 : 9 + c // 2, at] = sums_ref[12 + c : 13 + c, :side]
        sums_ref[10 + c // 2 : 11 + c // 2, at] = sums_ref[12 + c : 13 + c, side:]

    @pl.loop(0, 7)
    def _(index):
        span = pl.ds(pl.multiple_of(index * step, 16), step)
        y_ref[span, :] = (resid[span, :] + mlp[span, :] + vec_ref[7:8, :]).astype(jnp.bfloat16)
        _, normed, inverse = normalize(resid[span, :], gain, vec_ref[6:7, :])
        coming = upstream[span, :]
        grads_out = g_ref[span, :].astype(jnp.float32)
        sums_ref[5:6, :] += column_sum(coming * normed)
        sums_ref[6:7, :] += column_sum(coming)
        sums_ref[7:8, :] += column_sum(grads_out)
        grad_resid = grads_out + norm_back(coming, gain, normed, inverse)
        gr_ref[span, :] = grad_resid
        acts[span, :] = grad_resid.astype(jnp.bfloat16)
        sums_ref[4:5, :] += column_sum(acts[span, :].astype(jnp.float32))

    leaving = []

    def leave(source, target):
        copy = local_copy(source, target, o_sem.at[len(leaving)])
        copy.start()
        leaving.append(copy)

    leave(y_ref, y_out)
    leave(gr_ref, gr_out)
    cores[3].finish()
    leave(total.at[3], partial_ref.at[3])
    streams[0].finish(3)
    leave(total.at[0], partial_ref.at[0])
    ga_ref[...] = lax.dot_general(
        acts[...], wo_ref[...], NT, preferred_element_type=jnp.float32
    ).astype(jnp.bfloat16)
    leave(ga_ref, ga_out)
    branch_grad = lax.dot_general(
        att_ref[...], acts[...], TN, preferred_element_type=jnp.float32
    ).astype(jnp.bfloat16)
    for part in range(2):
        for sides in range(2):
            for block in range(8):
                at = sides * side + block * piece
                go_ref[part, block, sides] = branch_grad[
                    at : at + piece, part * side : (part + 1) * side
                ]
    for index, stage in ((1, 2), (2, 1)):
        streams[index].finish(stage)
        leave(total.at[index], partial_ref.at[index])
    for copy in leaving:
        copy.wait()


MIDDLE_STAGES = ((1, 2, 3), (1, 2), (1,), ())
MIDDLE_MOVES = ((), ((0, 0),), ((0, 1), (1, 0)), ((0, 2), (1, 1), (2, 0)))


def middle_call(attended, x_rows, out_grad, grad_got, vecs, out_low, mine, other):
    rows, width = x_rows.shape
    hidden = mine.shape[0]
    low = jnp.bfloat16
    anywhere = pl.BlockSpec(memory_space=pl.ANY)
    vmem = pl.BlockSpec(memory_space=pltpu.VMEM)
    dma = pltpu.SemaphoreType.DMA
    chunks = len(MIDDLE_STAGES)
    piece = hidden // (2 * chunks * 8)
    landing = landing_shapes((0, 0), piece, width)
    for stages in MIDDLE_STAGES:
        landing += landing_shapes(stages, piece, width)
    return pl.pallas_call(
        middle_kernel,
        in_specs=[vmem, anywhere, anywhere, anywhere, vmem, vmem, anywhere, anywhere],
        out_specs=[anywhere] * 4 + [vmem] * 2,
        out_shape=[
            jax.ShapeDtypeStruct((rows, width), low),
            jax.ShapeDtypeStruct((rows, width), jnp.float32),
            jax.ShapeDtypeStruct((rows, width), low),
            jax.ShapeDtypeStruct((chunks, 8, 2, piece, width), low),
            jax.ShapeDtypeStruct((2, 8, 2, piece, width // 2), low),
            jax.ShapeDtypeStruct((16, width), jnp.float32),
        ],
        scratch_shapes=[
            pltpu.VMEM((rows, width), low),
            pltpu.VMEM((rows, width), jnp.float32),
            pltpu.VMEM((rows, width), low),
            pltpu.VMEM((width, hidden), low),
            pltpu.VMEM((hidden, width), low),
            pltpu.VMEM((rows, width), low),
            pltpu.VMEM((rows, width), jnp.float32),
            pltpu.VMEM((rows, width), jnp.float32),
            pltpu.VMEM((rows, hidden // chunks), low),
            pltpu.VMEM((rows, hidden // chunks), low),
            pltpu.VMEM((2, 8, 2, piece, width), low),
            pltpu.VMEM((chunks, 8, 2, piece, width), low),
        ]
        + landing
        + sum_sems(chunks)
        + [dma((2, 2 * chunks)), dma((3,)), dma((7,))],
        compiler_params=pltpu.CompilerParams(
            vmem_limit_bytes=KERNEL_VMEM, collective_id=5, has_side_effects=True
        ),
        name="middle",
    )(attended, x_rows, out_grad, grad_got, vecs, out_low, mine, other)


def per_device_clips(
    x_tokens,
    out_grad,
    w_qkv,
    w_out,
    w_up,
    w_down,
    vectors,
    qkv_mean,
    qkv_square,
    out_mean,
    out_square,
    up_mean,
    up_square,
    down_mean,
    down_square,
    vectors_mean,
    vectors_square,
):
    me = lax.axis_index("ctx")
    width = x_tokens.shape[2]
    side = width // 2
    vector_own = jnp.pad(
        vectors.astype(jnp.bfloat16).astype(jnp.float32), ((0, 4), (0, 0))
    )
    (
        x_low,
        projected,
        qkv_low,
        out_low,
        vector_rows,
        norm_rows,
        late_weights,
    ) = start_call(x_tokens, vector_own, w_qkv, w_out, w_up, w_down)
    attended_low, inverse_total, exponent, late_other, grad_got = attend_call(
        projected, out_grad, late_weights, width
    )
    y_rows, grad_resid, grad_attended, partial, grad_out, part_sums = middle_call(
        attended_low,
        x_low,
        out_grad,
        grad_got,
        vector_rows,
        out_low,
        late_weights.reshape(-1, width),
        late_other.reshape(-1, width),
    )
    *grad_parts, late, first, y_got, small, last_parts = attend_back_call(
        projected,
        grad_attended,
        attended_low,
        inverse_total,
        exponent,
        partial,
        y_rows,
        norm_rows,
        grad_out,
    )
    x_grad, summed_vectors, late_shared, first_shared = finish_call(
        grad_parts,
        x_low,
        qkv_low,
        grad_resid,
        vector_rows,
        part_sums,
        late,
        first,
        small,
        last_parts,
    )

    vector_share = lax.dynamic_slice_in_dim(summed_vectors[:12], me * side, side, axis=1)

    weights, y_tokens, x_grad = update_call(
        (
            (w_qkv, qkv_mean, qkv_square),
            (w_out, out_mean, out_square),
            (w_up, up_mean, up_square),
            (w_down, down_mean, down_square),
        ),
        late_shared,
        first_shared,
        y_rows,
        y_got,
        x_grad,
    )
    qkv_new, out_new, up_new, down_new = (
        (weights[3 * i + 1], weights[3 * i + 2], weights[3 * i]) for i in range(4)
    )
    vectors_new = adam_update(
        vectors, vector_share, vectors_mean, vectors_square, vector_rate, 0.0
    )
    return (y_tokens, x_grad) + qkv_new + out_new + up_new + down_new + vectors_new


def per_device(x_tokens, *others):
    clips = x_tokens.shape[0]
    if lax.axis_size("ctx") == 2 and lax.axis_size("dp") == 16 and clips == 2:
        return per_device_clips(x_tokens, *others)
    return per_device_split(x_tokens, *others)


def solution(mesh):
    return jax.shard_map(
        per_device,
        mesh=mesh,
        in_specs=(
            P("dp", "ctx", None),
            P("dp", "ctx", None),
            P("ctx", None),
            P("ctx", None),
            P("ctx", None),
            P("ctx", None),
            P(None, "ctx"),
            P("ctx", None),
            P("ctx", None),
            P("ctx", None),
            P("ctx", None),
            P("ctx", None),
            P("ctx", None),
            P("ctx", None),
            P("ctx", None),
            P(None, "ctx"),
            P(None, "ctx"),
        ),
        out_specs=(
            P("dp", "ctx", None),
            P("dp", "ctx", None),
            P("ctx", None),
            P("ctx", None),
            P("ctx", None),
            P("ctx", None),
            P("ctx", None),
            P("ctx", None),
            P("ctx", None),
            P("ctx", None),
            P("ctx", None),
            P("ctx", None),
            P("ctx", None),
            P("ctx", None),
            P(None, "ctx"),
            P(None, "ctx"),
            P(None, "ctx"),
        ),
        check_vma=False,
    )
```
